32 devices in a mesh: dp: 4 (over y, core), fsdp: 8 (over z, x).
Axes of the slice: x: 2, y: 2, z: 4, core: 2. Of those that a mesh axis runs over, the one named last changes fastest.
Arguments:
- inputs: bfloat16 [32768, 512], P(('dp', 'fsdp')), may hold values from -6 to 6
- seq_lengths: int32 [32, 8], P(('dp', 'fsdp')), may hold values from 1 to 256, 1024 in all within a row
- query_weight: bfloat16 [512, 512], P(('dp', 'fsdp')), may hold values from -0.25 to 0.25
- key_weight: bfloat16 [512, 512], P(('dp', 'fsdp')), may hold values from -0.25 to 0.25
- value_weight: bfloat16 [512, 512], P(('dp', 'fsdp')), may hold values from -0.25 to 0.25
- output_weight: bfloat16 [512, 512], P(('dp', 'fsdp')), may hold values from -2 to 2
- query_bias: bfloat16 [512], P(('dp', 'fsdp')), may hold values from -3 to 3
- value_bias: bfloat16 [512], P(('dp', 'fsdp')), may hold values from -3 to 3
- output_bias: bfloat16 [512], P(('dp', 'fsdp')), may hold values from -3 to 3
- first_gain: bfloat16 [512], P(('dp', 'fsdp')), may hold values from 0.25 to 1.75
- first_shift: bfloat16 [512], P(('dp', 'fsdp')), may hold values from -3 to 3
- inner_weight: bfloat16 [512, 2048], P(('dp', 'fsdp')), may hold values from -0.25 to 0.25
- inner_bias: bfloat16 [2048], P(('dp', 'fsdp')), may hold values from -3 to 3
- outer_weight: bfloat16 [2048, 512], P(('dp', 'fsdp')), may hold values from -0.125 to 0.125
- outer_bias: bfloat16 [512], P(('dp', 'fsdp')), may hold values from -3 to 3
- final_gain: bfloat16 [512], P(('dp', 'fsdp')), may hold values from 0.25 to 1.75
- final_shift: bfloat16 [512], P(('dp', 'fsdp')), may hold values from -3 to 3
- cotangent: bfloat16 [32768, 512], P(('dp', 'fsdp')), may hold values from -6 to 6
Outputs:
- layer_out: bfloat16 [32768, 512], P(('dp', 'fsdp'))
- input_grad: float32 [32768, 512], P(('dp', 'fsdp'))
- query_weight_grad: float32 [512, 512], P(('dp', 'fsdp'))
- key_weight_grad: float32 [512, 512], P(('dp', 'fsdp'))
- value_weight_grad: float32 [512, 512], P(('dp', 'fsdp'))
- output_weight_grad: float32 [512, 512], P(('dp', 'fsdp'))
- query_bias_grad: float32 [512], P(('dp', 'fsdp'))
- value_bias_grad: float32 [512], P(('dp', 'fsdp'))
- output_bias_grad: float32 [512], P(('dp', 'fsdp'))
- first_gain_grad: float32 [512], P(('dp', 'fsdp'))
- first_shift_grad: float32 [512], P(('dp', 'fsdp'))
- inner_weight_grad: float32 [512, 2048], P(('dp', 'fsdp'))
- inner_bias_grad: float32 [2048], P(('dp', 'fsdp'))
- outer_weight_grad: float32 [2048, 512], P(('dp', 'fsdp'))
- outer_bias_grad: float32 [512], P(('dp', 'fsdp'))
- final_gain_grad: float32 [512], P(('dp', 'fsdp'))
- final_shift_grad: float32 [512], P(('dp', 'fsdp'))
The draws below stay inside these ranges and needn't reach their ends.
Inputs may be any that keep to these rules, and one draw needn't show every extreme that they name: `seq_lengths`: each device's row of 8 lengths sums to 1024, and its longest is exactly 256.
All inputs are finite; a program needn't handle non-finite values.
Results may differ from the reference program's by a relative error of at most 0.013.
The reference program's roundings to bfloat16 on the way count: a program that leaves them out, or rounds other values in their place, can miss the bound.
Values may be sent and summed in bfloat16 or wider, within the bound.
A program may use at most 192 MiB of HBM per device.

```python
import math
import jax
import jax.numpy as jnp
import numpy as np
from jax import lax

D = 512
FF = 2048
HEADS = 8
HEAD = 64
MAXLEN = 256
TOK_DEV = 1024
SEQ_DEV = 8
TOKENS = 32768
DEVICES = 32


def with_spikes(values, key, source, target, blocks, factor):
    owner, partner = [(jnp.arange(values.shape[position]) // (values.shape[position] // blocks)).reshape([-1 if axis == position else 1 for axis in range(values.ndim)]) for position in (source, target)]
    chosen = jax.random.permutation(key, blocks)[partner]
    strong = (owner == chosen) | (owner == (partner + blocks // 2) % blocks)
    return jnp.where(strong, factor * values, values)


def steps_of(key, dims, pieces, least, largest):
    gain = 1.0
    for axis_at, blocks in pieces:
        draws = jax.random.uniform(jax.random.fold_in(jax.random.fold_in(key, 6), axis_at), (blocks,), jnp.float32, least / len(pieces), largest / len(pieces))
        gain = gain * jnp.repeat(jnp.exp(draws), dims[axis_at] // blocks).reshape((-1,) + (1,) * (len(dims) - 1 - axis_at))
    return gain


def profile(count, total, bound, skew):
    loads = [(1 << 20) // math.isqrt(standing ** skew) + 1 for standing in range(2, count + 1)]
    spare, counts = total - bound - (count - 1), [1] * (count - 1)
    while spare > 0:
        movable = [i for i in range(count - 1) if counts[i] < bound]
        pool, remaining = sum([loads[i] for i in movable]), spare
        for i in movable:
            addition = min(bound - counts[i], max(1, remaining * loads[i] // pool), spare)
            counts[i] = counts[i] + addition
            spare = spare - addition
    return np.array([bound] + counts)


def ragged_sizes(key, number_of, total, most, lean):
    if number_of == 2:
        one = jax.random.randint(key, (), max(1, total - most), min(most, total - 1) + 1)
        return jnp.stack([one, total - one])
    sizes = jnp.asarray(profile(number_of, total, most, lean), jnp.int32)
    pairs = (number_of - 1) // 2
    donor, sink = sizes[1:1 + 2 * pairs:2], sizes[2:2 + 2 * pairs:2]
    slack = jnp.minimum(donor - 1, most - sink)
    shifted = jax.random.randint(jax.random.fold_in(key, 1), (pairs,), 0, 1 << 20) % (slack + 1)
    sizes = sizes.at[1:1 + 2 * pairs:2].set(donor - shifted).at[2:2 + 2 * pairs:2].set(sink + shifted)
    return sizes[jax.random.permutation(jax.random.fold_in(key, 2), number_of)]


def scatter_about(rng, dims, deviation, limit, cuts=(), kind=jnp.bfloat16):
    loudness = steps_of(rng, dims, cuts, -0.22, 0.18) if cuts else 1.0
    array = jax.random.normal(rng, dims, jnp.float32) * deviation * loudness
    return jnp.minimum(jnp.maximum(array, -limit), limit).astype(kind)


def heavy_noise(key, extent, deviation, limit, split, heavy, kind=jnp.bfloat16):
    entries = deviation * jax.random.normal(key, extent, jnp.float32)
    if split:
        entries = entries * steps_of(key, extent, split, -0.22, 0.18)
    return jnp.clip(with_spikes(entries, jax.random.fold_in(key, 3), *heavy), -limit, limit).astype(kind)


def setup_inputs(seed: int = 0) -> dict:
    arg_keys = jax.random.split(jax.random.key(seed), 19)
    return {
        "inputs": heavy_noise(arg_keys[0], (TOKENS, D), 1.0, 6.0, ((0, 32),), (0, 1, 32, 2.75)),
        "seq_lengths": jax.vmap(lambda own: ragged_sizes(own, SEQ_DEV, TOK_DEV, MAXLEN, 2))(jax.random.split(arg_keys[1], DEVICES)).reshape((DEVICES, SEQ_DEV)).astype(jnp.int32),
        "query_weight": scatter_about(arg_keys[2], (D, D), D ** -0.5, 0.25, ((0, 32),)),
        "key_weight": scatter_about(arg_keys[3], (D, D), D ** -0.5, 0.25, ((0, 32),)),
        "value_weight": scatter_about(arg_keys[4], (D, D), D ** -0.5, 0.25, ((0, 32),)),
        "output_weight": scatter_about(arg_keys[5], (D, D), (D // 64) ** -0.5, 2.0, ((0, 32),)),
        "query_bias": scatter_about(arg_keys[6], (D,), 0.5, 3.0, ((0, 32),)),
        "value_bias": scatter_about(arg_keys[7], (D,), 0.5, 3.0, ((0, 32),)),
        "output_bias": scatter_about(arg_keys[8], (D,), 0.5, 3.0, ((0, 32),)),
        "first_gain": jnp.clip(1.0 + 0.15 * jax.random.normal(arg_keys[9], (D,), jnp.float32), 0.25, 1.75).astype(jnp.bfloat16),
        "first_shift": scatter_about(arg_keys[10], (D,), 0.5, 3.0, ((0, 32),)),
        "inner_weight": scatter_about(arg_keys[11], (D, FF), D ** -0.5, 0.25, ((0, 32),)),
        "inner_bias": scatter_about(arg_keys[12], (FF,), 0.5, 3.0, ((0, 32),)),
        "outer_weight": scatter_about(arg_keys[13], (FF, D), FF ** -0.5, 0.125, ((0, 32),)),
        "outer_bias": scatter_about(arg_keys[14], (D,), 0.5, 3.0, ((0, 32),)),
        "final_gain": jnp.clip(1.0 + 0.15 * jax.random.normal(arg_keys[15], (D,), jnp.float32), 0.25, 1.75).astype(jnp.bfloat16),
        "final_shift": scatter_about(arg_keys[16], (D,), 0.5, 3.0, ((0, 32),)),
        "cotangent": scatter_about(arg_keys[17], (TOKENS, D), 1.0, 6.0, ((0, 32),)),
    }


masked_fill = -1e+30
norm_eps = 1e-05

@jax.custom_vjp
def low(v):
    return lax.optimization_barrier(v.astype(jnp.bfloat16)).astype(jnp.float32)

@jax.custom_vjp
def low_back(v):
    return v

def low_keep(v):
    return (low(v), None)

def low_pass(kept, grad):
    return (grad,)

def back_keep(v):
    return (v, None)

def back_low(kept, grad):
    return (low(grad),)
low.defvjp(low_keep, low_pass)
low_back.defvjp(back_keep, back_low)

def product(left_side, right_side):
    return jnp.dot(left_side, right_side, precision=lax.Precision.HIGHEST, preferred_element_type=jnp.float32)

def layer_norm(values, norm_gain, norm_shift):
    center = values - lax.optimization_barrier(jnp.mean(values, axis=-1, keepdims=True))
    spread = lax.optimization_barrier(jnp.mean(center * center, axis=-1, keepdims=True))
    return center * lax.rsqrt(spread + norm_eps) * norm_gain + norm_shift

def segment_ids(lengths_row, row_count):
    seq_ends = jnp.cumsum(lengths_row, dtype=jnp.int32)
    positions = jnp.arange(row_count, dtype=jnp.int32)
    return lax.optimization_barrier(jnp.sum((positions[:, None] >= seq_ends[None, :]).astype(jnp.int32), axis=1, dtype=jnp.int32))

def device_block(weight_list, token_rows, lengths_row):
    wide_query, wide_key, wide_value, wide_output, bias_query, bias_value, bias_output, gain_first, shift_first, wide_inner, bias_inner, wide_outer, bias_outer, gain_final, shift_final = weight_list
    row_count = token_rows.shape[0]
    score_scale = 1.0 / math.sqrt(HEAD)
    queries = low_back(low(product(token_rows, wide_query) + bias_query))
    keys_all = low_back(low(product(token_rows, wide_key)))
    values_all = low_back(low(product(token_rows, wide_value) + bias_value))
    segment = segment_ids(lengths_row, row_count)
    allowed = segment[:, None] == segment[None, :]
    query_heads = queries.reshape(row_count, HEADS, HEAD)
    key_heads = keys_all.reshape(row_count, HEADS, HEAD)
    value_heads = values_all.reshape(row_count, HEADS, HEAD)
    raw_scores = jnp.einsum('qhd,khd->hqk', query_heads, key_heads, precision=lax.Precision.HIGHEST)
    scores = low_back(raw_scores * score_scale)
    masked = jnp.where(allowed[None], scores, masked_fill)
    row_max = lax.optimization_barrier(jnp.max(masked, axis=-1, keepdims=True))
    exponent = jnp.exp(masked - row_max)
    attention = low(exponent / lax.optimization_barrier(jnp.sum(exponent, axis=-1, keepdims=True)))
    combined = jnp.einsum('hqk,khd->qhd', attention, value_heads, precision=lax.Precision.HIGHEST)
    combined = low_back(low(combined.reshape(row_count, D)))
    attended = low_back(product(combined, wide_output) + bias_output)
    hidden = layer_norm(token_rows + attended, gain_first, shift_first)
    inner_act = low_back(product(low(hidden), wide_inner) + bias_inner)
    active = low(jax.nn.gelu(inner_act, approximate=True))
    outer_act = low_back(product(active, wide_outer) + bias_outer)
    return layer_norm(outer_act + hidden + token_rows, gain_final, shift_final)

def reference(inputs, seq_lengths, query_weight, key_weight, value_weight, output_weight, query_bias, value_bias, output_bias, first_gain, first_shift, inner_weight, inner_bias, outer_weight, outer_bias, final_gain, final_shift, cotangent):
    weights = tuple((weight_item.astype(jnp.float32) for weight_item in (query_weight, key_weight, value_weight, output_weight, query_bias, value_bias, output_bias, first_gain, first_shift, inner_weight, inner_bias, outer_weight, outer_bias, final_gain, final_shift)))

    def forward(all_rows, weight_list):
        groups = all_rows.reshape(DEVICES, TOK_DEV, D)
        checked = jax.checkpoint(device_block)

        def group_step(carried, paired):
            return (carried, checked(weight_list, paired[0], paired[1]))
        unused, results = lax.scan(group_step, jnp.zeros((), jnp.float32), (groups, seq_lengths))
        return results.reshape(TOKENS, D)
    result, pullback = jax.vjp(forward, inputs.astype(jnp.float32), weights)
    input_grad, weight_grads = pullback(cotangent.astype(jnp.float32))
    grad_query, grad_key, grad_value, grad_output, grad_bias_query, grad_bias_value, grad_bias_output, grad_gain_first, grad_shift_first, grad_inner, grad_bias_inner, grad_outer, grad_bias_outer, grad_gain_final, grad_shift_final = weight_grads
    return (result.astype(jnp.bfloat16), input_grad, grad_query, grad_key, grad_value, grad_output, grad_bias_query, grad_bias_value, grad_bias_output, grad_gain_first, grad_shift_first, grad_inner, grad_bias_inner, grad_outer, grad_bias_outer, grad_gain_final, grad_shift_final)
```

```python
from functools import partial
import math

import jax
import jax.numpy as jnp
from jax import lax
from jax.experimental import pallas as pl
from jax.experimental.pallas import tpu as pltpu
from jax.sharding import PartitionSpec as P

HEADS = 8
MAXLEN = 256


masked_fill = -1e30
norm_eps = 1e-05


def product(left_side, right_side):
    return jnp.dot(left_side, right_side, preferred_element_type=jnp.float32)


def product_tn(left_side, right_side):
    return lax.dot_general(
        left_side, right_side, (((0,), (0,)), ((), ())), preferred_element_type=jnp.float32
    )


def product_nt(left_side, right_side):
    return lax.dot_general(
        left_side, right_side, (((1,), (1,)), ((), ())), preferred_element_type=jnp.float32
    )


def layer_norm(values, norm_gain, norm_shift):
    center = values - jnp.mean(values, axis=-1, keepdims=True)
    spread = jnp.mean(center * center, axis=-1, keepdims=True)
    return center * lax.rsqrt(spread + norm_eps) * norm_gain + norm_shift


def column_sums(values):
    return jnp.sum(values.astype(jnp.float32), axis=0)


def segment_ids(lengths_row, row_count):
    seq_ends = jnp.cumsum(lengths_row, dtype=jnp.int32)
    positions = jnp.arange(row_count, dtype=jnp.int32)
    return jnp.sum(
        (positions[:, None] >= seq_ends[None, :]).astype(jnp.int32), axis=1, dtype=jnp.int32
    )


MESH_ID = pl.DeviceIdType.MESH


def place():
    outer, inner = lax.axis_index("dp"), lax.axis_index("fsdp")
    return outer // 2, outer % 2, inner // 2, inner % 2


def device_at(y, core, z, x):
    return (y * 2 + core, z * 2 + x)


def greet_partners():
    y, core, z, x = place()
    partners = [
        device_at(y, 1 - core, z, x),
        device_at(1 - y, core, z, x),
        device_at(y, core, z, 1 - x),
    ] + [device_at(y, core, (z + step) % 4, x) for step in (1, 2, 3)]
    barrier = pltpu.get_barrier_semaphore()
    for partner in partners:
        pl.semaphore_signal(barrier, inc=1, device_id=partner, device_id_type=MESH_ID)
    pl.semaphore_wait(barrier, len(partners))


def remote(source, target, send_sem, recv_sem, to):
    return pltpu.make_async_remote_copy(
        src_ref=source,
        dst_ref=target,
        send_sem=send_sem,
        recv_sem=recv_sem,
        device_id=to,
        device_id_type=MESH_ID,
    )


class Corner:
    def __init__(self):
        y, core, z, x = place()
        self.y, self.core, self.z, self.x = y, core, z, x
        self.ya, self.xa = jnp.where(core == 0, y, 1 - y), jnp.where(core == 0, 1 - x, x)
        self.yb, self.xb = jnp.where(core == 0, 1 - y, y), jnp.where(core == 0, x, 1 - x)
        self.partner_a = device_at(self.ya, core, z, self.xa)
        self.partner_b = device_at(self.yb, core, z, self.xb)
        self.sibling = device_at(y, 1 - core, z, x)

    def along_z(self, step):
        return device_at(self.y, self.core, (self.z + step) % 4, self.x)


class Gather:
    def __init__(self, corner, own, whole, send_sem, recv_sem):
        self.at, self.own, self.whole = corner, own, whole
        self.send_sem, self.recv_sem = send_sem, recv_sem

    def to_z(self, step):
        at = self.at
        slot = self.whole.at[at.y, at.core, at.z, at.x]
        return remote(
            self.own, slot, self.send_sem.at[step - 1], self.recv_sem.at[step - 1], at.along_z(step)
        )

    def line(self, y, x, number, to):
        line = self.whole.at[y, self.at.core, :, x]
        return remote(line, line, self.send_sem.at[number], self.recv_sem.at[number], to)

    def to_a(self):
        return self.line(self.at.y, self.at.x, 3, self.at.partner_a)

    def to_b(self, part):
        at = self.at
        y, x = ((at.y, at.x), (at.ya, at.xa))[part]
        return self.line(y, x, 4 + part, at.partner_b)

    def to_sibling(self, part):
        at = self.at
        y, x = ((at.y, at.x), (at.ya, at.xa), (at.yb, at.xb), (1 - at.y, 1 - at.x))[part]
        return self.line(y, x, 6 + part, at.sibling)

    def phase(self, number):
        if number == 0:
            for step in (2, 1, 3):
                self.to_z(step).start()
            at = self.at
            self.whole[at.y, at.core, at.z, at.x] = self.own[...]
        elif number == 1:
            for step in (1, 2, 3):
                self.to_z(step).wait_recv()
            self.to_a().start()
            self.to_b(0).start()
            self.to_sibling(0).start()
        elif number == 2:
            self.to_a().wait_recv()
            self.to_b(1).start()
            self.to_sibling(1).start()
        elif number == 3:
            self.to_b(0).wait_recv()
            self.to_sibling(2).start()
            self.to_b(1).wait_recv()
            self.to_sibling(3).start()
        elif number == 4:
            for part in range(4):
                self.to_sibling(part).wait_recv()

    def finish(self):
        for step in (1, 2, 3):
            self.to_z(step).wait_send()
        self.to_a().wait_send()
        for part in range(2):
            self.to_b(part).wait_send()
        for part in range(4):
            self.to_sibling(part).wait_send()


class Scatter:
    def __init__(self, corner, whole, out, got_core, got_b, got_a, got_z, send_sem, recv_sem):
        self.at, self.whole, self.out = corner, whole, out
        self.got_core, self.got_b, self.got_a, self.got_z = got_core, got_b, got_a, got_z
        self.send_sem, self.recv_sem = send_sem, recv_sem

    def sems(self, number):
        return self.send_sem.at[number], self.recv_sem.at[number]

    def to_sibling(self):
        return remote(
            self.whole.at[:, 1 - self.at.core], self.got_core, *self.sems(0), self.at.sibling
        )

    def to_b(self, part):
        at = self.at
        y, x = ((at.yb, at.xb), (1 - at.y, 1 - at.x))[part]
        return remote(
            self.whole.at[y, at.core, :, x], self.got_b.at[part], *self.sems(1 + part), at.partner_b
        )

    def to_a(self):
        at = self.at
        return remote(
            self.whole.at[at.ya, at.core, :, at.xa], self.got_a, *self.sems(3), at.partner_a
        )

    def to_z(self, step):
        at = self.at
        return remote(
            self.whole.at[at.y, at.core, (at.z + step) % 4, at.x],
            self.got_z.at[step - 1],
            *self.sems(3 + step),
            at.along_z(step),
        )

    def add_line(self, y, x, other):
        core = self.at.core
        for z in range(4):
            total = self.whole[y, core, z, x].astype(jnp.float32) + other(z).astype(jnp.float32)
            self.whole[y, core, z, x] = total.astype(self.whole.dtype)

    def add_core(self, y, x):
        self.add_line(y, x, lambda z: self.got_core[y, z, x])

    def phase(self, number):
        at = self.at
        if number == 0:
            self.to_sibling().start()
        elif number == 1:
            self.to_sibling().wait_recv()
            self.add_core(at.yb, at.xb)
            self.to_b(0).start()
            self.add_core(1 - at.y, 1 - at.x)
            self.to_b(1).start()
            self.add_core(at.ya, at.xa)
            self.add_core(at.y, at.x)
        elif number == 2:
            self.to_b(1).wait_recv()
            self.add_line(at.ya, at.xa, lambda z: self.got_b[1, z])
            self.to_a().start()
            self.to_b(0).wait_recv()
            self.add_line(at.y, at.x, lambda z: self.got_b[0, z])
        elif number == 3:
            self.to_a().wait_recv()
            self.add_line(at.y, at.x, lambda z: self.got_a[z])
            for step in (2, 1, 3):
                self.to_z(step).start()
        elif number == 4:
            total = self.whole[at.y, at.core, at.z, at.x].astype(jnp.float32)
            for step in (1, 2, 3):
                self.to_z(step).wait_recv()
                total = total + self.got_z[step - 1].astype(jnp.float32)
            self.out[...] = total

    def finish(self):
        self.to_sibling().wait_send()
        for part in range(2):
            self.to_b(part).wait_send()
        self.to_a().wait_send()
        for step in (1, 2, 3):
            self.to_z(step).wait_send()


def in_steps(moves):
    for step in range(len(moves) + 4):
        for number, move in enumerate(moves):
            if 0 <= step - number <= 4:
                move.phase(step - number)
    for move in moves:
        move.finish()


def gather_kernel(count, *refs):
    owns, wholes = refs[:count], refs[count : 2 * count]
    send_sem, recv_sem = refs[2 * count :]
    greet_partners()
    corner = Corner()
    in_steps(
        [Gather(corner, owns[i], wholes[i], send_sem.at[i], recv_sem.at[i]) for i in range(count)]
    )


def scatter_kernel(count, *refs):
    wholes, outs, given = refs[:count], refs[count : 2 * count], refs[2 * count : 3 * count]
    got = refs[3 * count : 7 * count]
    send_sem, recv_sem = refs[7 * count :]
    greet_partners()
    corner = Corner()
    for i in range(count):
        given[i][...] = wholes[i][...]
    in_steps(
        [
            Scatter(corner, given[i], outs[i], *got[4 * i : 4 * i + 4], send_sem.at[i], recv_sem.at[i])
            for i in range(count)
        ]
    )


def in_vmem(count):
    return [pl.BlockSpec(memory_space=pltpu.VMEM)] * count


def gather_all(owns):
    count = len(owns)
    return pl.pallas_call(
        partial(gather_kernel, count),
        out_shape=[jax.ShapeDtypeStruct((2, 2, 4, 2) + own.shape, own.dtype) for own in owns],
        in_specs=in_vmem(count),
        out_specs=in_vmem(count),
        scratch_shapes=[pltpu.SemaphoreType.DMA((count, 10))] * 2,
        compiler_params=pltpu.CompilerParams(
            collective_id=0, has_side_effects=True, vmem_limit_bytes=60 << 20
        ),
    )(*owns)


def scatter_all(wholes):
    count = len(wholes)
    scratch = [pltpu.VMEM(whole.shape, whole.dtype) for whole in wholes]
    for whole in wholes:
        rest, kind = whole.shape[4:], whole.dtype
        scratch += [
            pltpu.VMEM((2, 4, 2) + rest, kind),
            pltpu.VMEM((2, 4) + rest, kind),
            pltpu.VMEM((4,) + rest, kind),
            pltpu.VMEM((3,) + rest, kind),
        ]
    return pl.pallas_call(
        partial(scatter_kernel, count),
        out_shape=[jax.ShapeDtypeStruct(whole.shape[4:], jnp.float32) for whole in wholes],
        in_specs=in_vmem(count),
        out_specs=in_vmem(count),
        scratch_shapes=scratch + [pltpu.SemaphoreType.DMA((count, 7))] * 2,
        compiler_params=pltpu.CompilerParams(
            collective_id=1, has_side_effects=True, vmem_limit_bytes=60 << 20
        ),
    )(*wholes)


def pack_vectors(vectors, inner):
    first = jnp.concatenate(vectors).astype(jnp.float32)[None]
    second = jnp.pad(inner.astype(jnp.float32), (0, 64))[None]
    return jnp.concatenate([first, second, jnp.zeros((6, 128), jnp.float32)])


def collect(weights, vectors, inner_bias):
    qkv = jnp.concatenate(weights[:3], axis=1)
    wide, output, inner, outer, small = gather_all(
        [qkv, weights[3], weights[4], weights[5], pack_vectors(vectors, inner_bias)]
    )
    wide = wide.reshape(512, 1536)
    small = small.reshape(32, 8, 128)
    whole_vectors = [small[:, 0, 16 * i : 16 * i + 16].reshape(512) for i in range(8)]
    return (
        [wide[:, :512], wide[:, 512:1024], wide[:, 1024:]]
        + [output.reshape(512, 512), inner.reshape(512, 2048), outer.reshape(2048, 512)],
        whole_vectors,
        small[:, 1, :64].reshape(2048),
    )


def hand_out(grads, vectors, inner_bias):
    low = [grad.astype(jnp.bfloat16) for grad in grads]
    first = jnp.stack([vector.reshape(32, 16) for vector in vectors], 1).reshape(32, 1, 128)
    second = jnp.pad(inner_bias.reshape(32, 1, 64), ((0, 0), (0, 0), (0, 64)))
    small = jnp.concatenate([first, second, jnp.zeros((32, 6, 128), jnp.float32)], axis=1)
    shaped = [jnp.concatenate(low[:3], axis=1).reshape(2, 2, 4, 2, 16, 1536)]
    shaped += [low[3].reshape(2, 2, 4, 2, 16, 512), low[4].reshape(2, 2, 4, 2, 16, 2048)]
    shaped += [low[5].reshape(2, 2, 4, 2, 64, 512), small.reshape(2, 2, 4, 2, 8, 128)]
    qkv, output, inner, outer, small = scatter_all(shaped)
    return (
        [qkv[:, :512], qkv[:, 512:1024], qkv[:, 1024:], output, inner, outer],
        [small[0, 16 * i : 16 * i + 16] for i in range(8)],
        small[1, :64],
    )


def shards(
    direct,
    inputs,
    seq_lengths,
    query_weight,
    key_weight,
    value_weight,
    output_weight,
    query_bias,
    value_bias,
    output_bias,
    first_gain,
    first_shift,
    inner_weight,
    inner_bias,
    outer_weight,
    outer_bias,
    final_gain,
    final_shift,
    cotangent,
):
    weights = [query_weight, key_weight, value_weight, output_weight, inner_weight, outer_weight]
    vectors = [query_bias, value_bias, output_bias, first_gain, first_shift]
    vectors += [outer_bias, final_gain, final_shift]
    if direct:
        weights, vectors, bias_inner = collect(weights, vectors, inner_bias)
    else:
        weights, vectors, bias_inner = jax.tree.map(
            lambda own: lax.all_gather(own, ("dp", "fsdp"), axis=0, tiled=True),
            (weights, vectors, inner_bias),
        )
    wide_query, wide_key, wide_value, wide_output, wide_inner, wide_outer = weights
    bias_query, bias_value, bias_output, gain_first, shift_first = vectors[:5]
    bias_outer, gain_final, shift_final = vectors[5:]
    row_count = inputs.shape[0]
    model_width = inputs.shape[1]
    head_count = HEADS
    head_width = model_width // head_count
    score_scale = 1.0 / math.sqrt(head_width)
    margin_rows = MAXLEN
    block_rows = min(512, row_count)
    block_count = row_count // block_rows
    window_rows = block_rows + 2 * margin_rows
    rows_float = inputs.astype(jnp.float32)
    queries = (product(inputs, wide_query) + bias_query.astype(jnp.float32)).astype(jnp.bfloat16)
    keys_all = product(inputs, wide_key).astype(jnp.bfloat16)
    values_all = (product(inputs, wide_value) + bias_value.astype(jnp.float32)).astype(jnp.bfloat16)
    segment = segment_ids(seq_lengths[0], row_count)
    segment_pad = jnp.pad(segment, (margin_rows, margin_rows), constant_values=-1)
    query_heads = queries.reshape(row_count, head_count, head_width)
    key_pad = jnp.pad(
        keys_all.reshape(row_count, head_count, head_width),
        ((margin_rows, margin_rows), (0, 0), (0, 0)),
    )
    value_pad = jnp.pad(
        values_all.reshape(row_count, head_count, head_width),
        ((margin_rows, margin_rows), (0, 0), (0, 0)),
    )

    def scores_of(block_index):
        start_row = block_index * block_rows
        query_block = lax.dynamic_slice_in_dim(query_heads, start_row, block_rows, 0)
        key_window = lax.dynamic_slice_in_dim(key_pad, start_row, window_rows, 0)
        value_window = lax.dynamic_slice_in_dim(value_pad, start_row, window_rows, 0)
        segment_query = lax.dynamic_slice_in_dim(segment, start_row, block_rows, 0)
        segment_key = lax.dynamic_slice_in_dim(segment_pad, start_row, window_rows, 0)
        allowed = segment_query[:, None] == segment_key[None, :]
        raw_scores = (
            jnp.einsum("qhd,khd->hqk", query_block, key_window, preferred_element_type=jnp.float32)
            * score_scale
        )
        masked = jnp.where(allowed[None], raw_scores, masked_fill)
        return (masked, query_block, key_window, value_window)

    def forward_block(block_index):
        masked, query_block, key_window, value_window = scores_of(block_index)
        row_max = jnp.max(masked, axis=-1, keepdims=True)
        exponent = jnp.exp(masked - row_max)
        row_total = jnp.sum(exponent, axis=-1, keepdims=True)
        attention_low = (exponent / row_total).astype(jnp.bfloat16)
        mixed_block = jnp.einsum(
            "hqk,khd->qhd", attention_low, value_window, preferred_element_type=jnp.float32
        )
        return (mixed_block.astype(jnp.bfloat16), row_max + jnp.log(row_total))

    mixed_blocks, log_totals = lax.map(forward_block, jnp.arange(block_count, dtype=jnp.int32))
    combined = mixed_blocks.reshape(row_count, model_width)
    attended = product(combined, wide_output) + bias_output.astype(jnp.float32)
    residual_one = rows_float + attended
    hidden = layer_norm(
        residual_one, gain_first.astype(jnp.float32), shift_first.astype(jnp.float32)
    )
    hidden_low = hidden.astype(jnp.bfloat16)
    inner_act = product(hidden_low, wide_inner) + bias_inner.astype(jnp.float32)
    active = jax.nn.gelu(inner_act, approximate=True).astype(jnp.bfloat16)
    outer_act = product(active, wide_outer) + bias_outer.astype(jnp.float32)
    residual_two = outer_act + hidden + rows_float
    final = layer_norm(
        residual_two, gain_final.astype(jnp.float32), shift_final.astype(jnp.float32)
    )
    layer_out = final.astype(jnp.bfloat16)
    unused_final, final_pull = jax.vjp(
        layer_norm,
        residual_two,
        gain_final.astype(jnp.float32),
        shift_final.astype(jnp.float32),
    )
    grad_two, grad_gain_final, grad_shift_final = final_pull(cotangent.astype(jnp.float32))
    grad_outer = grad_two.astype(jnp.bfloat16)
    grad_wide_outer = product_tn(active, grad_outer)
    grad_bias_outer = column_sums(grad_outer)
    grad_active = product_nt(grad_outer, wide_outer)
    unused_gelu, gelu_pull = jax.vjp(partial(jax.nn.gelu, approximate=True), inner_act)
    grad_inner = gelu_pull(grad_active)[0].astype(jnp.bfloat16)
    grad_wide_inner = product_tn(hidden_low, grad_inner)
    grad_bias_inner = column_sums(grad_inner)
    grad_hidden = product_nt(grad_inner, wide_inner) + grad_two
    unused_first, first_pull = jax.vjp(
        layer_norm,
        residual_one,
        gain_first.astype(jnp.float32),
        shift_first.astype(jnp.float32),
    )
    grad_one, grad_gain_first, grad_shift_first = first_pull(grad_hidden)
    grad_attended = grad_one.astype(jnp.bfloat16)
    grad_wide_output = product_tn(combined, grad_attended)
    grad_bias_output = column_sums(grad_attended)
    grad_combined = product_nt(grad_attended, wide_output).astype(jnp.bfloat16)
    grad_combined_heads = grad_combined.reshape(row_count, head_count, head_width)

    def backward_block(carried, block_index):
        key_grads, value_grads = carried
        masked, query_block, key_window, value_window = scores_of(block_index)
        start_row = block_index * block_rows
        attention = jnp.exp(masked - log_totals[block_index])
        grad_block = lax.dynamic_slice_in_dim(grad_combined_heads, start_row, block_rows, 0)
        grad_attention = jnp.einsum(
            "qhd,khd->hqk", grad_block, value_window, preferred_element_type=jnp.float32
        )
        inner_total = jnp.sum(attention * grad_attention, axis=-1, keepdims=True)
        grad_scores = (attention * (grad_attention - inner_total)).astype(jnp.bfloat16)
        query_part = (
            jnp.einsum("hqk,khd->qhd", grad_scores, key_window, preferred_element_type=jnp.float32)
            * score_scale
        )
        key_part = (
            jnp.einsum("hqk,qhd->khd", grad_scores, query_block, preferred_element_type=jnp.float32)
            * score_scale
        )
        value_part = jnp.einsum(
            "hqk,qhd->khd",
            attention.astype(jnp.bfloat16),
            grad_block,
            preferred_element_type=jnp.float32,
        )
        key_grads = lax.dynamic_update_slice_in_dim(
            key_grads,
            lax.dynamic_slice_in_dim(key_grads, start_row, window_rows, 0) + key_part,
            start_row,
            0,
        )
        value_grads = lax.dynamic_update_slice_in_dim(
            value_grads,
            lax.dynamic_slice_in_dim(value_grads, start_row, window_rows, 0) + value_part,
            start_row,
            0,
        )
        return ((key_grads, value_grads), query_part)

    empty_pad = jnp.zeros((row_count + 2 * margin_rows, head_count, head_width), jnp.float32)
    (key_grads, value_grads), query_grads = lax.scan(
        backward_block, (empty_pad, empty_pad), jnp.arange(block_count, dtype=jnp.int32)
    )
    grad_queries = query_grads.reshape(row_count, model_width).astype(jnp.bfloat16)
    grad_keys = (
        key_grads[margin_rows : margin_rows + row_count]
        .reshape(row_count, model_width)
        .astype(jnp.bfloat16)
    )
    grad_values = (
        value_grads[margin_rows : margin_rows + row_count]
        .reshape(row_count, model_width)
        .astype(jnp.bfloat16)
    )
    grad_wide_query = product_tn(inputs, grad_queries)
    grad_bias_query = column_sums(grad_queries)
    grad_wide_key = product_tn(inputs, grad_keys)
    grad_wide_value = product_tn(inputs, grad_values)
    grad_bias_value = column_sums(grad_values)
    input_grad = (
        grad_two
        + grad_one
        + product_nt(grad_queries, wide_query)
        + product_nt(grad_keys, wide_key)
        + product_nt(grad_values, wide_value)
    )
    grads = [grad_wide_query, grad_wide_key, grad_wide_value]
    grads += [grad_wide_output, grad_wide_inner, grad_wide_outer]
    vectors = [grad_bias_query, grad_bias_value, grad_bias_output, grad_gain_first]
    vectors += [grad_shift_first, grad_bias_outer, grad_gain_final, grad_shift_final]
    if direct:
        grads, vectors, inner_total = hand_out(grads, vectors, grad_bias_inner)
    else:
        grads, vectors, inner_total = jax.tree.map(
            lambda part: lax.psum_scatter(part, ("dp", "fsdp"), scatter_dimension=0, tiled=True),
            (grads, vectors, grad_bias_inner),
        )
    return (
        layer_out,
        input_grad,
        *grads[:4],
        *vectors[:5],
        grads[4],
        inner_total,
        grads[5],
        *vectors[5:],
    )


def solution(mesh):
    in_specs = (
        P(("dp", "fsdp"), None),
        P(("dp", "fsdp"), None),
        P(("dp", "fsdp"), None),
        P(("dp", "fsdp"), None),
        P(("dp", "fsdp"), None),
        P(("dp", "fsdp"), None),
        P(("dp", "fsdp")),
        P(("dp", "fsdp")),
        P(("dp", "fsdp")),
        P(("dp", "fsdp")),
        P(("dp", "fsdp")),
        P(("dp", "fsdp"), None),
        P(("dp", "fsdp")),
        P(("dp", "fsdp"), None),
        P(("dp", "fsdp")),
        P(("dp", "fsdp")),
        P(("dp", "fsdp")),
        P(("dp", "fsdp"), None),
    )
    out_specs = (
        P(("dp", "fsdp"), None),
        P(("dp", "fsdp"), None),
        P(("dp", "fsdp"), None),
        P(("dp", "fsdp"), None),
        P(("dp", "fsdp"), None),
        P(("dp", "fsdp"), None),
        P(("dp", "fsdp")),
        P(("dp", "fsdp")),
        P(("dp", "fsdp")),
        P(("dp", "fsdp")),
        P(("dp", "fsdp")),
        P(("dp", "fsdp"), None),
        P(("dp", "fsdp")),
        P(("dp", "fsdp"), None),
        P(("dp", "fsdp")),
        P(("dp", "fsdp")),
        P(("dp", "fsdp")),
    )
    direct = mesh.shape["dp"] == 4 and mesh.shape["fsdp"] == 8
    return jax.shard_map(partial(shards, direct), mesh=mesh, in_specs=in_specs, out_specs=out_specs, check_vma=False)
```

```python
from functools import partial
import math
import types

import jax
import jax.numpy as jnp
from jax import lax
from jax.experimental import pallas as pl
from jax.experimental.pallas import tpu as pltpu
from jax.sharding import PartitionSpec as P

norm_eps = 1e-05
Q_BIAS, V_BIAS, O_BIAS, GAIN_ONE, SHIFT_ONE, U_BIAS, GAIN_TWO, SHIFT_TWO = range(8)
BLOCK = 256
STARTS, PACKED = (0, 640, 1152), 512
LANES = 128
far = -1e30


def nn(left, right):
    return jnp.dot(left, right, preferred_element_type=jnp.float32)


def tn(left, right):
    return lax.dot_general(left, right, (((0,), (0,)), ((), ())), preferred_element_type=jnp.float32)


def nt(left, right):
    return lax.dot_general(left, right, (((1,), (1,)), ((), ())), preferred_element_type=jnp.float32)


def low(values):
    return values.astype(jnp.bfloat16)


def wide(values):
    return values.astype(jnp.float32)


def iota(shape, axis):
    return lax.broadcasted_iota(jnp.int32, shape, axis)


def matrix(ref):
    return ref[...].reshape(-1, ref.shape[-1])


def whole_loop(count, body):
    def step(i, carried):
        body(i)
        return carried

    lax.fori_loop(0, count, step, 0)


def block_of(i):
    return pl.ds(pl.multiple_of(i * BLOCK, BLOCK), BLOCK)


def lanes_of(first):
    return pl.ds(first if isinstance(first, int) else pl.multiple_of(first, LANES), LANES)


def boundaries(lengths):
    starts, ends, at = [], [], 0
    for s in range(lengths.shape[1]):
        starts.append(at)
        at = at + lengths[0, s]
        ends.append(at)
    before, after = [], []
    for edge in (BLOCK, 2 * BLOCK, 3 * BLOCK):
        tail, head = 0, 0
        for start, end in zip(starts, ends):
            across = (start < edge) & (end > edge)
            tail = tail + jnp.where(across, edge - start, 0)
            head = head + jnp.where(across, end - edge, 0)
        before.append(tail)
        after.append(head)
    return starts, ends, before, after


class Attention:
    def __init__(self, lengths):
        self.starts, self.ends, self.before, self.after = boundaries(lengths)
        self.rows = iota((BLOCK, LANES), 0)
        self.lanes = iota((BLOCK, LANES), 1)
        self.left = self.lanes < 64

    def members(self, block):
        rows, lanes = self.rows + block * BLOCK, lax.rem(self.lanes, 64)
        marks = jnp.zeros((BLOCK, LANES), jnp.float32)
        for s, (start, end) in enumerate(zip(self.starts, self.ends)):
            inside = (rows >= start) & (rows < end) & (lanes == s)
            marks = jnp.where(inside, 1.0, marks)
        return marks

    def half(self, side):
        return self.left if side == 0 else ~self.left

    def in_head(self, edge):
        return self.rows < self.after[edge]

    def in_tail(self, edge):
        return self.rows >= BLOCK - self.before[edge]

    def pick(self, parts):
        out = []
        for i in range(4):
            block = parts[i]
            if i < 3:
                block = jnp.where(self.in_tail(i), parts[4 + i], block)
            if i > 0:
                block = jnp.where(self.in_head(i - 1), parts[3 + i], block)
            out.append(block)
        return out

    def gather_sums(self, parts):
        out = []
        for i in range(4):
            block = parts[i]
            if i < 3:
                block = block + jnp.where(self.in_head(i), 0.0, parts[4 + i])
            if i > 0:
                block = block + jnp.where(self.in_head(i - 1), parts[3 + i], 0.0)
            out.append(block)
        return out

    def units(self, blocks):
        out = []
        for i in range(4):
            block = blocks[i]
            if i < 3:
                block = jnp.where(self.in_tail(i), 0.0, block)
            if i > 0:
                block = jnp.where(self.in_head(i - 1), 0.0, block)
            out.append(block)
        for i in range(3):
            tail = jnp.where(self.in_tail(i), blocks[i], 0.0)
            out.append(jnp.where(self.in_head(i), blocks[i + 1], tail))
        return out


def square_of(r, part):
    first = STARTS[part]
    return r.wqkv[:, :, :, :, :, first : first + 512].reshape(512, 512)


def project(r, at, part):
    dest = (r.q, r.k, r.v)[part]
    for i in range(4):
        product = nn(r.x[BLOCK * i : BLOCK * (i + 1)], square_of(r, part))
        beside = 1.0
        if part == 0:
            product = (product + r.vec[Q_BIAS : Q_BIAS + 1]) * 0.125
            beside = at.members(i)
        elif part == 1:
            beside = jnp.where(lax.rem(at.lanes, 64) < 8, far * (1.0 - at.members(i)), 0.0)
        else:
            product = product + r.vec[V_BIAS : V_BIAS + 1]
        for pair in range(4):
            both = product[:, LANES * pair : LANES * (pair + 1)]
            for side in range(2):
                dest[2 * pair + side, i] = low(jnp.where(at.half(side), both, beside))

    def across(head):
        for edge in range(3):
            merged = jnp.where(at.in_head(edge), wide(dest[head, edge + 1]), wide(dest[head, edge]))
            dest[head, 4 + edge] = low(merged)

    whole_loop(8, across)


def attend(r, at, pair):
    outs = []
    for side in range(2):
        head = 2 * pair + side
        parts = []
        for unit in range(7):
            scores = nt(r.k[head, unit], r.q[head, unit])
            top = jnp.max(scores, axis=0, keepdims=True)
            grown = low(jnp.exp(scores - top))
            r.e[head, unit] = grown
            parts.append(tn(grown, r.v[head, unit]))
        outs.append(at.pick(parts))
    columns = lanes_of(pair * LANES)
    for i in range(4):
        even, odd = outs[0][i], outs[1][i]
        share = 1.0 / pltpu.roll(jnp.where(at.left, odd, even), 64, 1)
        mixed = jnp.where(at.left, even, odd) * share
        r.combined[BLOCK * i : BLOCK * (i + 1), columns] = low(mixed)
        r.share[BLOCK * i : BLOCK * (i + 1), columns] = share


def normal(values):
    center = values - jnp.mean(values, axis=-1, keepdims=True)
    spread = jnp.mean(center * center, axis=-1, keepdims=True)
    scale = lax.rsqrt(spread + norm_eps)
    return center * scale, scale


def normal_back(grad, normed, scale):
    return scale * (
        grad
        - jnp.mean(grad, axis=-1, keepdims=True)
        - normed * jnp.mean(grad * normed, axis=-1, keepdims=True)
    )


def sums(values):
    return jnp.sum(values, axis=0, keepdims=True)


def attended_rows(r, i):
    rows = block_of(i)
    attended = nn(r.combined[rows], matrix(r.wo)) + r.vec[O_BIAS : O_BIAS + 1]
    normed, scale = normal(wide(r.x[rows]) + attended)
    r.normed[rows] = normed
    r.scale[rows] = jnp.broadcast_to(scale, (BLOCK, LANES))
    r.hidden[rows] = low(normed * r.vec[GAIN_ONE : GAIN_ONE + 1] + r.vec[SHIFT_ONE : SHIFT_ONE + 1])


def active_rows(r, i):
    rows = block_of(i)
    hidden_low = r.hidden[rows]
    slope = math.sqrt(2 / math.pi)
    for part in range(4):
        columns = slice(512 * part, 512 * (part + 1))
        inner = nn(hidden_low, r.wi[:, :, :, :, :, columns].reshape(512, 512)) + r.ib[:, columns]
        square = inner * inner
        half = 0.5 * jnp.tanh(inner * (slope + (slope * 0.044715) * square)) + 0.5
        active = inner * half
        r.active[rows, columns] = low(active)
        turn = half + active * (1.0 - half) * (2 * slope + (6 * slope * 0.044715) * square)
        r.turn[rows, columns] = low(turn)


def final_rows(r, i):
    rows = block_of(i)
    hidden = r.normed[rows] * r.vec[GAIN_ONE : GAIN_ONE + 1] + r.vec[SHIFT_ONE : SHIFT_ONE + 1]
    outer = nn(r.active[rows], matrix(r.wu)) + r.vec[U_BIAS : U_BIAS + 1]
    normed, scale = normal(outer + hidden + wide(r.x[rows]))
    gain = r.vec[GAIN_TWO : GAIN_TWO + 1]
    r.out[rows] = low(normed * gain + r.vec[SHIFT_TWO : SHIFT_TWO + 1])
    grad = wide(r.cot[rows])
    r.gvec[GAIN_TWO : GAIN_TWO + 1] += sums(grad * normed)
    r.gvec[SHIFT_TWO : SHIFT_TWO + 1] += sums(grad)
    grad_two = normal_back(grad * gain, normed, scale)
    r.grad[rows] = grad_two
    grad_outer = low(grad_two)
    r.grad_outer[rows] = grad_outer
    r.gvec[U_BIAS : U_BIAS + 1] += sums(wide(grad_outer))


def rows_of(ref, quarter):
    return ref[quarter // 2, quarter % 2].reshape(-1, ref.shape[-1])


def outer_weight_grad(r):
    for quarter in range(4):
        columns = slice(512 * quarter, 512 * (quarter + 1))
        product = low(tn(r.active[:, columns], r.grad_outer[...]))
        r.gu[quarter // 2, quarter % 2] = product.reshape(r.gu.shape[2:])


def inner_rows(r, i):
    rows = block_of(i)
    grad_outer = r.grad_outer[rows]
    for part in range(4):
        columns = slice(512 * part, 512 * (part + 1))
        grad_inner = low(nt(grad_outer, rows_of(r.wu, part)) * wide(r.turn[rows, columns]))
        r.active[rows, columns] = grad_inner
        r.gib[:, columns] += sums(wide(grad_inner))


def inner_weight_grad(r, side):
    for half in range(2):
        for part in (2 * side, 2 * side + 1):
            columns = slice(512 * part, 512 * (part + 1))
            product = low(tn(r.hidden[:, 256 * half : 256 * (half + 1)], r.active[:, columns]))
            r.gi[half, :, :, :, :, columns] = product.reshape(2, 4, 2, -1, 512)


def hidden_rows(r, i):
    rows = block_of(i)
    grad_two = r.grad[rows]
    grad_hidden = nt(r.active[rows], matrix(r.wi)) + grad_two
    normed = r.normed[rows]
    r.gvec[GAIN_ONE : GAIN_ONE + 1] += sums(grad_hidden * normed)
    r.gvec[SHIFT_ONE : SHIFT_ONE + 1] += sums(grad_hidden)
    gain = r.vec[GAIN_ONE : GAIN_ONE + 1]
    grad_one = normal_back(grad_hidden * gain, normed, r.scale[rows, 0:1])
    r.grad[rows] = grad_two + grad_one
    attended = low(grad_one)
    r.attended[rows] = attended
    r.gvec[O_BIAS : O_BIAS + 1] += sums(wide(attended))
    r.grad_outer[rows] = low(nt(attended, matrix(r.wo)))


def output_weight_grad(r):
    for half in range(2):
        product = low(tn(r.combined[:, 256 * half : 256 * (half + 1)], r.attended[...]))
        r.go[half] = product.reshape(r.go.shape[1:])


def attend_back(r, at, pair):
    columns = lanes_of(pair * LANES)
    ones = low(jnp.where((iota((LANES, LANES), 0) < 64) == (iota((LANES, LANES), 1) < 64), 1.0, 0.0))
    sides = [[], []]
    for i in range(4):
        rows = slice(BLOCK * i, BLOCK * (i + 1))
        grad = wide(r.grad_outer[rows, columns])
        share = r.share[rows, columns]
        product = grad * wide(r.combined[rows, columns])
        high = low(product)
        total = nn(high, ones) + nn(low(product - wide(high)), ones)
        total = pltpu.roll(-(total * share), 64, 1)
        rest = total - wide(low(total))
        lanes = lax.rem(at.lanes, 64)
        beside = jnp.where(lanes == 0, total, jnp.where(lanes == 1, rest, 0.0))
        grad = grad * share
        for side in range(2):
            sides[side].append(jnp.where(at.half(side), grad, beside))
    found = [[], [], []]
    for side in range(2):
        head = 2 * pair + side
        parts = [[], [], []]
        for unit, grad in enumerate(at.units(sides[side])):
            grad = low(grad)
            grown = r.e[head, unit]
            scores = low(wide(grown) * nt(r.v[head, unit], grad))
            parts[0].append(tn(scores, r.k[head, unit]))
            parts[1].append(nn(scores, r.q[head, unit]))
            parts[2].append(nn(grown, grad))
        for which in range(3):
            found[which].append(at.gather_sums(parts[which]))
    for which in range(3):
        for i in range(4):
            both = jnp.where(at.left, found[which][0][i], found[which][1][i])
            both = low(both * 0.125 if which == 0 else both)
            (r.dq, r.dk, r.dv)[which][BLOCK * i : BLOCK * (i + 1), columns] = both


def qkv_weight_grad(r, side):
    for part, grads in enumerate((r.dq, r.dk, r.dv)):
        first = 768 * side + 256 * part
        columns = slice(first, first + 256)
        for half in range(2):
            rows = slice(256 * half, 256 * (half + 1))
            product = low(tn(r.x[:, rows], grads[:, 256 * side : 256 * (side + 1)]))
            r.gqkv[half, :, :, :, :, columns] = product.reshape(2, 4, 2, -1, 256)


def qkv_bias_grads(r):
    r.gvec[Q_BIAS : Q_BIAS + 1] = sums(wide(r.dq[...]))
    r.gvec[V_BIAS : V_BIAS + 1] = sums(wide(r.dv[...]))


def input_rows(r, i):
    rows = block_of(i)
    total = r.grad[rows]
    for part, grads in enumerate((r.dq, r.dk, r.dv)):
        total = total + nt(grads[rows], square_of(r, part))
    r.grad[rows] = total


MESH_ID = pl.DeviceIdType.MESH


def place():
    outer, inner = lax.axis_index("dp"), lax.axis_index("fsdp")
    return outer // 2, outer % 2, inner // 2, inner % 2


def device_at(y, core, z, x):
    return (y * 2 + core, z * 2 + x)


def greet_partners():
    y, core, z, x = place()
    partners = [
        device_at(y, 1 - core, z, x),
        device_at(1 - y, core, z, x),
        device_at(y, core, z, 1 - x),
    ] + [device_at(y, core, (z + step) % 4, x) for step in (1, 2, 3)]
    barrier = pltpu.get_barrier_semaphore()
    for partner in partners:
        pl.semaphore_signal(barrier, inc=1, device_id=partner, device_id_type=MESH_ID)
    pl.semaphore_wait(barrier, len(partners))


def remote(source, target, send_sem, recv_sem, to):
    return pltpu.make_async_remote_copy(
        src_ref=source,
        dst_ref=target,
        send_sem=send_sem,
        recv_sem=recv_sem,
        device_id=to,
        device_id_type=MESH_ID,
    )


class Corner:
    def __init__(self):
        y, core, z, x = place()
        self.y, self.core, self.z, self.x = y, core, z, x
        self.ya, self.xa = jnp.where(core == 0, y, 1 - y), jnp.where(core == 0, 1 - x, x)
        self.yb, self.xb = jnp.where(core == 0, 1 - y, y), jnp.where(core == 0, x, 1 - x)
        self.partner_a = device_at(self.ya, core, z, self.xa)
        self.partner_b = device_at(self.yb, core, z, self.xb)
        self.sibling = device_at(y, 1 - core, z, x)

    def along_z(self, step):
        return device_at(self.y, self.core, (self.z + step) % 4, self.x)


class Gather:
    def __init__(self, corner, own, whole, send_sem, recv_sem):
        self.at, self.own, self.whole = corner, own, whole
        self.send_sem, self.recv_sem = send_sem, recv_sem

    def to_z(self, step):
        at = self.at
        slot = self.whole.at[at.y, at.core, at.z, at.x]
        return remote(
            self.own, slot, self.send_sem.at[step - 1], self.recv_sem.at[step - 1], at.along_z(step)
        )

    def line(self, y, x, number, to):
        line = self.whole.at[y, self.at.core, :, x]
        return remote(line, line, self.send_sem.at[number], self.recv_sem.at[number], to)

    def to_a(self):
        return self.line(self.at.y, self.at.x, 3, self.at.partner_a)

    def to_b(self, part):
        at = self.at
        y, x = ((at.y, at.x), (at.ya, at.xa))[part]
        return self.line(y, x, 4 + part, at.partner_b)

    def to_sibling(self, part):
        at = self.at
        y, x = ((at.y, at.x), (at.ya, at.xa), (at.yb, at.xb), (1 - at.y, 1 - at.x))[part]
        return self.line(y, x, 6 + part, at.sibling)

    def phase(self, number):
        if number == 0:
            for step in (2, 1, 3):
                self.to_z(step).start()
            at = self.at
            self.whole[at.y, at.core, at.z, at.x] = self.own[...]
        elif number == 1:
            for step in (1, 2, 3):
                self.to_z(step).wait_recv()
            self.to_a().start()
            self.to_b(0).start()
            self.to_sibling(0).start()
        elif number == 2:
            self.to_a().wait_recv()
            self.to_b(1).start()
            self.to_sibling(1).start()
        elif number == 3:
            self.to_b(0).wait_recv()
            self.to_sibling(2).start()
            self.to_b(1).wait_recv()
            self.to_sibling(3).start()
        elif number == 4:
            for part in range(4):
                self.to_sibling(part).wait_recv()

    def finish(self):
        for step in (1, 2, 3):
            self.to_z(step).wait_send()
        self.to_a().wait_send()
        for part in range(2):
            self.to_b(part).wait_send()
        for part in range(4):
            self.to_sibling(part).wait_send()


class Scatter:
    def __init__(self, corner, whole, out, got_core, got_b, got_a, got_z, send_sem, recv_sem):
        self.at, self.whole, self.out = corner, whole, out
        self.got_core, self.got_b, self.got_a, self.got_z = got_core, got_b, got_a, got_z
        self.send_sem, self.recv_sem = send_sem, recv_sem

    def sems(self, number):
        return self.send_sem.at[number], self.recv_sem.at[number]

    def to_sibling(self):
        return remote(
            self.whole.at[:, 1 - self.at.core], self.got_core, *self.sems(0), self.at.sibling
        )

    def to_b(self, part):
        at = self.at
        y, x = ((at.yb, at.xb), (1 - at.y, 1 - at.x))[part]
        return remote(
            self.whole.at[y, at.core, :, x], self.got_b.at[part], *self.sems(1 + part), at.partner_b
        )

    def to_a(self):
        at = self.at
        return remote(
            self.whole.at[at.ya, at.core, :, at.xa], self.got_a, *self.sems(3), at.partner_a
        )

    def to_z(self, step):
        at = self.at
        return remote(
            self.whole.at[at.y, at.core, (at.z + step) % 4, at.x],
            self.got_z.at[step - 1],
            *self.sems(3 + step),
            at.along_z(step),
        )

    def add_line(self, y, x, other):
        core = self.at.core
        for z in range(4):
            total = self.whole[y, core, z, x].astype(jnp.float32) + other(z).astype(jnp.float32)
            self.whole[y, core, z, x] = total.astype(self.whole.dtype)

    def add_core(self, y, x):
        self.add_line(y, x, lambda z: self.got_core[y, z, x])

    def phase(self, number):
        at = self.at
        if number == 0:
            self.to_sibling().start()
        elif number == 1:
            self.to_sibling().wait_recv()
            self.add_core(at.yb, at.xb)
            self.to_b(0).start()
            self.add_core(1 - at.y, 1 - at.x)
            self.to_b(1).start()
            self.add_core(at.ya, at.xa)
            self.add_core(at.y, at.x)
        elif number == 2:
            self.to_b(1).wait_recv()
            self.add_line(at.ya, at.xa, lambda z: self.got_b[1, z])
            self.to_a().start()
            self.to_b(0).wait_recv()
            self.add_line(at.y, at.x, lambda z: self.got_b[0, z])
        elif number == 3:
            self.to_a().wait_recv()
            self.add_line(at.y, at.x, lambda z: self.got_a[z])
            for step in (2, 1, 3):
                self.to_z(step).start()
        elif number == 4:
            total = self.whole[at.y, at.core, at.z, at.x].astype(jnp.float32)
            for step in (1, 2, 3):
                self.to_z(step).wait_recv()
                total = total + self.got_z[step - 1].astype(jnp.float32)
            self.out[...] = total

    def finish(self):
        self.to_sibling().wait_send()
        for part in range(2):
            self.to_b(part).wait_send()
        self.to_a().wait_send()
        for step in (1, 2, 3):
            self.to_z(step).wait_send()


LEAD = (2, 2, 4, 2)
TOKENS, WIDTH = 1024, 512
BF, F32 = jnp.bfloat16, jnp.float32
AXES = ("dp", "fsdp")
SHARDS = dict(wqkv=(16, 1664), wo=(16, 512), wi=(16, 2048), wu=(64, 512))


def local_scratch():
    units, tokens = (8, 7, BLOCK, LANES), (TOKENS, WIDTH)
    return dict(
        q=(units, BF),
        k=(units, BF),
        v=(units, BF),
        e=((8, 7, BLOCK, BLOCK), BF),
        share=(tokens, F32),
        combined=(tokens, BF),
        normed=(tokens, F32),
        scale=((TOKENS, LANES), F32),
        hidden=(tokens, BF),
        active=((TOKENS, 2048), BF),
        turn=((TOKENS, 2048), BF),
        grad_outer=(tokens, BF),
        attended=(tokens, BF),
    )


def call(kernel, inputs, spaces, outputs, scratch, sems, **params):
    names = [*inputs, *outputs, *scratch, *sems]

    def body(*refs):
        kernel(types.SimpleNamespace(**dict(zip(names, refs, strict=True))))

    made = pl.pallas_call(
        body,
        out_shape=[jax.ShapeDtypeStruct(*given) for given in outputs.values()],
        in_specs=[pl.BlockSpec(memory_space=spaces.get(name, pltpu.VMEM)) for name in inputs],
        out_specs=[pl.BlockSpec(memory_space=spaces.get(name, pltpu.VMEM)) for name in outputs],
        scratch_shapes=[pltpu.VMEM(*given) for given in scratch.values()]
        + [pltpu.SemaphoreType.DMA(shape) for shape in sems.values()],
        compiler_params=pltpu.CompilerParams(vmem_limit_bytes=63 << 20, **params),
    )(*inputs.values())
    return types.SimpleNamespace(**dict(zip(outputs, made, strict=True)))


def halves(body):
    def half(side):
        whole_loop(2, lambda i: body(2 * side + i))

    return half


def run(r, move):
    at = Attention(r.lengths)
    r.gvec[...] = jnp.zeros_like(r.gvec)
    r.gib[...] = jnp.zeros_like(r.gib)
    for part in range(3):
        move(part)
        project(r, at, part)
    for pair in range(4):
        move(3 + pair)
        attend(r, at, pair)
    move(7)
    whole_loop(4, partial(attended_rows, r))
    active, inner, hidden, back = [
        halves(partial(rows, r)) for rows in (active_rows, inner_rows, hidden_rows, input_rows)
    ]
    for side in range(2):
        move(8 + side)
        active(side)
    move(10)
    whole_loop(4, partial(final_rows, r))
    outer_weight_grad(r)
    for side in range(2):
        move(11 + side)
        inner(side)
    for side in range(2):
        move(13 + side)
        inner_weight_grad(r, side)
    for side in range(2):
        move(15 + side)
        hidden(side)
    move(17)
    output_weight_grad(r)
    for pair in range(4):
        if pair == 2:
            move(20)
            qkv_weight_grad(r, 0)
        move((18, 19, 21, 22)[pair])
        attend_back(r, at, pair)
    move(23)
    qkv_weight_grad(r, 1)
    qkv_bias_grads(r)
    for side in range(2):
        move(24 + side)
        back(side)
    move(26)


def chosen_lanes(count):
    shape = (LANES, 32 * count)
    return low(jnp.where(iota(shape, 0) == lax.rem(iota(shape, 1), count), 1.0, 0.0))


def of_owner(rows, count):
    shape = (rows, 32 * count)
    return lax.rem(iota(shape, 0), 32) == lax.div(iota(shape, 1), count)


def chosen_rows():
    row, column = iota((288, 512), 0), iota((288, 512), 1)
    return low(jnp.where(column == lax.rem(row, 32) * 16 + lax.div(row, 32), 1.0, 0.0))


def unpack_vectors(r):
    packed = r.wqkv[:, :, :, :, :, PACKED : PACKED + LANES].reshape(512, LANES)
    packed = low(nn(chosen_rows(), packed))
    vectors = jnp.where(of_owner(256, 16), nn(packed[:256], chosen_lanes(16)), 0.0)
    for kind in range(8):
        r.vec[kind : kind + 1] = sums(vectors[32 * kind : 32 * (kind + 1)])
    r.ib[...] = sums(jnp.where(of_owner(32, 64), nn(packed[256:], chosen_lanes(64)), 0.0))


def pack_sums(r):
    def placed(values, count):
        alone = jnp.where(of_owner(32, count), values, 0.0)
        high = low(alone)
        lanes = chosen_lanes(count)
        return nt(high, lanes) + nt(low(alone - wide(high)), lanes)

    rows = [placed(r.gvec[kind : kind + 1], 16) for kind in range(8)] + [placed(r.gib[...], 64)]
    packed = tn(chosen_rows(), low(jnp.concatenate(rows, axis=0)))
    r.gqkv[:, :, :, :, :, 1536:1664] = low(packed).reshape(*LEAD, 16, LANES)


def direct_kernel(r):
    r.gi = r.turn.at[0:512].reshape(*LEAD, 16, 2048)
    r.gqkv = r.turn.at[512:1024].reshape(*LEAD, 16, 2048).at[:, :, :, :, :, 0:1664]
    r.dq = r.wu.at[0].reshape(TOKENS, 512)
    r.dk = r.wu.at[1].reshape(TOKENS, 512)
    r.dv = r.attended
    r.cot = r.attended
    spare = [
        r.active.at[first : first + 16 * math.prod(lead)].reshape(*lead, 16, 2048)
        for lead, first in (((2, 4, 2), 0), ((2, 4), 256), ((4,), 384), ((3,), 448))
    ]
    local = [
        pltpu.make_async_copy(source, target, r.local.at[i])
        for i, (source, target) in enumerate(
            [(r.x_far, r.x), (r.cot_far, r.cot), (r.out, r.out_far)]
            + [(r.grad.at[BLOCK * i : BLOCK * (i + 1)], r.grad_far.at[BLOCK * i : BLOCK * (i + 1)]) for i in range(4)]
        )
    ]
    local[0].start()
    local[1].start()
    corner = Corner()
    r.own_qkv[:, 0:512] = r.own_query[...]
    r.own_qkv[:, 640:1152] = r.own_key[...]
    r.own_qkv[:, 1152:1664] = r.own_value[...]
    r.own_small[...] = jnp.zeros_like(r.own_small)
    vectors = [r.own0, r.own1, r.own2, r.own3, r.own4, r.own5, r.own6, r.own7, r.own8]
    for i, vector in enumerate(vectors):
        r.own_small[i : i + 1, 0 : vector.shape[0]] = wide(vector[...]).reshape(1, vector.shape[0])
    r.own_qkv[:, 512:640] = low(r.own_small[...])
    greet_partners()

    def column_part(ref, first, last):
        return ref.at[(slice(None),) * (len(ref.shape) - 1) + (slice(first, last),)]

    def row_part(ref, first, last):
        return ref.at[(slice(None),) * (len(ref.shape) - 2) + (slice(first, last),)]

    pieces = [(column_part, r.own_qkv, r.wqkv, *ends) for ends in ((0, 640), (640, 1152), (1152, 1664))]
    pieces += [(column_part, r.own_output, r.wo, 0, 512)]
    pieces += [(column_part, r.own_inner, r.wi, *ends) for ends in ((0, 1024), (1024, 2048))]
    pieces += [(row_part, r.own_outer, r.wu, *ends) for ends in ((0, 32), (32, 64))]
    gathers = [
        Gather(corner, cut(own, *ends), cut(whole, *ends), r.gather_send.at[i], r.gather_recv.at[i])
        for i, (cut, own, whole, *ends) in enumerate(pieces)
    ]
    q, k, v, o, i0, i1, u0, u1 = gathers

    got0 = (r.got0_core, r.got0_b, r.got0_a, r.got0_z)
    got1 = (r.got1_core, r.got1_b, r.got1_a, r.got1_z)
    got2 = (r.got2_core, r.got2_b, r.got2_a, r.got2_z)
    pieces = [(row_part, r.gu, r.out_outer, got0, *ends) for ends in ((0, 32), (32, 64))]
    pieces += [(column_part, r.gi, r.out_inner, got1, *ends) for ends in ((0, 1024), (1024, 2048))]
    pieces += [(column_part, r.go, r.out_output, got2, 0, 512)]
    pieces += [(column_part, r.gqkv, r.out_qkv, spare, *ends) for ends in ((0, 768), (768, 1664))]
    scatters = [
        Scatter(
            corner, cut(whole, *ends), cut(out, *ends), *[cut(ref, *ends) for ref in got],
            r.scatter_send.at[i], r.scatter_recv.at[i],
        )
        for i, (cut, whole, out, got, *ends) in enumerate(pieces)
    ]
    su0, su1, si0, si1, so, sa, sb = scatters

    plan = {
        0: [(g, 0) for g in gathers]
        + [(q, 1), (k, 1), (q, 2), (v, 1), (k, 2), (o, 1), (q, 3), (v, 2), (i0, 1), (k, 3), (o, 2), (i1, 1), (q, 4)],
        1: [(v, 3), (i0, 2), (u0, 1), (k, 4)],
        2: [(o, 3), (i1, 2), (u1, 1), (v, 4)],
        3: [(i0, 3), (u0, 2)],
        4: [(o, 4), (i1, 3), (u1, 2)],
        5: [(i0, 4), (u0, 3)],
        6: [(i1, 4), (u1, 3)],
        9: [(u0, 4)],
        10: [(u1, 4)],
        11: [(su0, 0), (su1, 0)],
        12: [(su0, 1), (su1, 1)],
        14: [(si0, 0)],
        15: [(si1, 0), (su0, 2)],
        16: [(su1, 2), (si0, 1)],
        17: [(si1, 1), (su0, 3)],
        18: [(so, 0), (su1, 3)],
        19: [(si0, 2), (so, 1), (su0, 4)],
        20: [(si1, 2), (su1, 4), (so, 2)],
        21: [(sa, 0), (si0, 3)],
        22: [(sa, 1), (si1, 3), (so, 3)],
        23: [(sa, 2), (si0, 4)],
        24: [(sb, 0), (si1, 4), (so, 4), (sa, 3), (sb, 1)],
        25: [(sa, 4)],
        26: [(sb, 2), (sb, 3), (sb, 4)],
    }

    def move(point):
        if point == 24:
            pack_sums(r)
        for piece, number in plan.get(point, ()):
            piece.phase(number)
        if point == 0:
            local[0].wait()
            unpack_vectors(r)
        elif point == 10:
            for piece in gathers:
                piece.finish()
            local[1].wait()
        elif point == 11:
            local[2].start()
        elif point == 25:
            local[3].start()
            local[4].start()
        elif point == 26:
            local[5].start()
            local[6].start()

    run(r, move)
    for piece in scatters:
        piece.finish()
    for copy in local[2:]:
        copy.wait()


def received(shard):
    return [(lead + shard[0], shard[1]) for lead in ((2, 4, 2), (2, 4), (4,), (3,))]


def direct(inputs, lengths, cotangent, weights, vectors, inner_bias):
    tokens = (TOKENS, WIDTH)
    given = dict(x_far=inputs, cot_far=cotangent, lengths=lengths)
    given |= dict(own_query=weights[0], own_key=weights[1], own_value=weights[2])
    given |= dict(own_output=weights[3], own_inner=weights[4], own_outer=weights[5])
    given |= {"own%d" % i: vector for i, vector in enumerate([*vectors, inner_bias])}
    outputs = dict(
        out_far=(tokens, BF),
        grad_far=(tokens, F32),
        out_qkv=(SHARDS["wqkv"], F32),
        out_output=(SHARDS["wo"], F32),
        out_inner=(SHARDS["wi"], F32),
        out_outer=(SHARDS["wu"], F32),
    )
    whole = {name: (LEAD + shard, BF) for name, shard in SHARDS.items()}
    got0, got1, got2 = [received((SHARDS[name], BF)) for name in ("wu", "wi", "wo")]
    scratch = local_scratch() | whole
    scratch |= dict(
        x=(tokens, BF),
        out=(tokens, BF),
        grad=(tokens, F32),
        gu=whole["wu"],
        go=whole["wo"],
        own_qkv=(SHARDS["wqkv"], BF),
        own_small=((16, LANES), F32),
        vec=((8, WIDTH), F32),
        ib=((1, 2048), F32),
        gvec=((8, WIDTH), F32),
        gib=((1, 2048), F32),
        got0_core=got0[0], got0_b=got0[1], got0_a=got0[2], got0_z=got0[3],
        got1_core=got1[0], got1_b=got1[1], got1_a=got1[2], got1_z=got1[3],
        got2_core=got2[0], got2_b=got2[1], got2_a=got2[2], got2_z=got2[3],
    )
    sems = dict(gather_send=(8, 10), gather_recv=(8, 10), scatter_send=(7, 7), scatter_recv=(7, 7), local=(7,))
    spaces = dict(lengths=pltpu.SMEM, x_far=pl.ANY, cot_far=pl.ANY, out_far=pl.ANY, grad_far=pl.ANY)
    made = call(
        direct_kernel, given, spaces, outputs, scratch, sems, collective_id=0, has_side_effects=True
    )
    return hand_over(made)


def hand_over(made):
    count = 4
    rows = TOKENS // count

    def body(out, grad, qkv, output, inner, outer, *refs):
        to_out, to_grad, to_q, to_k, to_v, to_output, to_inner, to_outer = refs[:8]
        vectors, (held_out, held_grad, held_qkv, sem) = refs[8:17], refs[17:]
        copies = []

        def copy(source, target):
            copies.append(pltpu.make_async_copy(source, target, sem.at[len(copies)]))
            copies[-1].start()
            return copies[-1]

        small = copy(qkv, held_qkv)
        parts = []
        for i in range(count):
            part = pl.ds(rows * i, rows)
            for source, held, target in ((grad, held_grad, to_grad), (out, held_out, to_out)):
                parts.append((copy(source.at[part], held.at[part]), held.at[part], target.at[part]))
        to_output[...] = output[...]
        to_inner[...] = inner[...]
        to_outer[...] = outer[...]
        small.wait()
        for i, target in enumerate((to_q, to_k, to_v)):
            target[:, 0:256] = held_qkv[:, 256 * i : 256 * (i + 1)]
            target[:, 256:512] = held_qkv[:, 768 + 256 * i : 768 + 256 * (i + 1)]
        for i, target in enumerate(vectors):
            target[...] = held_qkv[i, 1536 : 1536 + target.shape[0]]
        back = []
        for into, held, target in parts:
            into.wait()
            back.append(copy(held, target))
        for each in back:
            each.wait()

    given = [made.out_far, made.grad_far, made.out_qkv, made.out_output, made.out_inner, made.out_outer]
    square = jax.ShapeDtypeStruct((16, 512), F32)
    shapes = [jax.ShapeDtypeStruct(part.shape, part.dtype) for part in given]
    vectors = [jax.ShapeDtypeStruct((16,), F32)] * 8 + [jax.ShapeDtypeStruct((64,), F32)]
    far, near = pl.BlockSpec(memory_space=pl.ANY), pl.BlockSpec(memory_space=pltpu.VMEM)
    out, grad, q, k, v, output, inner, outer, *vectors = pl.pallas_call(
        body,
        out_shape=[*shapes[:2], square, square, square, *shapes[3:], *vectors],
        in_specs=[far, far, far, near, near, near],
        out_specs=[far, far, *[near] * 15],
        scratch_shapes=[
            pltpu.VMEM((TOKENS, WIDTH), BF),
            pltpu.VMEM((TOKENS, WIDTH), F32),
            pltpu.VMEM(SHARDS["wqkv"], F32),
            pltpu.SemaphoreType.DMA((1 + 4 * count,)),
        ],
    )(*given)
    return out, grad, [q, k, v, output, inner, outer], vectors[:8], vectors[8]


def through_collectives(inputs, lengths, cotangent, weights, vectors, inner_bias):
    weights, vectors, inner_bias = jax.tree.map(
        lambda own: lax.all_gather(own, AXES, axis=0, tiled=True), (weights, vectors, inner_bias)
    )
    empty = jnp.zeros((WIDTH, LANES), BF)
    weights = [jnp.concatenate([weights[0], empty, *weights[1:3]], axis=1), *weights[3:]]
    whole = {name: weight.reshape(LEAD + SHARDS[name]) for name, weight in zip(SHARDS, weights)}
    given = dict(x=inputs, cot=cotangent, lengths=lengths, **whole)
    given |= dict(vec=jnp.stack(vectors).astype(F32), ib=inner_bias.astype(F32)[None])
    tokens = (TOKENS, WIDTH)
    outputs = dict(out=(tokens, BF), grad=(tokens, F32), gvec=((8, WIDTH), F32), gib=((1, 2048), F32))
    outputs |= {"g" + name[1:]: (LEAD + shard, BF) for name, shard in SHARDS.items()}
    scratch = local_scratch() | dict(dq=(tokens, BF), dk=(tokens, BF), dv=(tokens, BF))
    made = call(
        lambda r: run(r, lambda point: None),
        given, dict(lengths=pltpu.SMEM), outputs, scratch, {},
    )
    qkv, output, inner, outer = [
        part.reshape(-1, part.shape[-1]).astype(F32) for part in (made.gqkv, made.go, made.gi, made.gu)
    ]
    sides = qkv[:, :768], qkv[:, 768:1536]
    grads = [jnp.concatenate([side[:, i : i + 256] for side in sides], axis=1) for i in (0, 256, 512)]
    grads += [output, inner, outer]
    grads, vectors, inner_bias = jax.tree.map(
        lambda part: lax.psum_scatter(part, AXES, scatter_dimension=0, tiled=True),
        (grads, [made.gvec[i] for i in range(8)], made.gib[0]),
    )
    return made.out, made.grad, grads, vectors, inner_bias


def solution(mesh):
    on_chips = (mesh.shape["dp"], mesh.shape["fsdp"]) == (4, 8)
    way = direct if on_chips else through_collectives

    def shards(
        inputs, seq_lengths, query_weight, key_weight, value_weight, output_weight, query_bias, value_bias,
        output_bias, first_gain, first_shift, inner_weight, inner_bias, outer_weight, outer_bias, final_gain,
        final_shift, cotangent,
    ):
        weights = [query_weight, key_weight, value_weight, output_weight, inner_weight, outer_weight]
        vectors = [query_bias, value_bias, output_bias, first_gain, first_shift]
        vectors += [outer_bias, final_gain, final_shift]
        out, grad, grads, vectors, inner_total = way(
            inputs, seq_lengths, cotangent, weights, vectors, inner_bias
        )
        return (out, grad, *grads[:4], *vectors[:5], grads[4], inner_total, grads[5], *vectors[5:])

    flat, rows = P(AXES), P(AXES, None)
    weights = (*[rows] * 4, *[flat] * 5, rows, flat, rows, *[flat] * 3)
    return jax.shard_map(
        shards,
        mesh=mesh,
        in_specs=(rows, rows, *weights, rows),
        out_specs=(rows, rows, *weights),
        check_vma=False,
    )
```

```python
from functools import partial
import math
import types

import jax
import jax.numpy as jnp
from jax import lax
from jax.experimental import pallas as pl
from jax.experimental.pallas import tpu as pltpu
from jax.sharding import PartitionSpec as P

norm_eps = 1e-05
Q_BIAS, V_BIAS, O_BIAS, GAIN_ONE, SHIFT_ONE, U_BIAS, GAIN_TWO, SHIFT_TWO = range(8)
BLOCK = 256
STARTS, PACKED = (0, 640, 1152), 512
PAIRS = ((0, 256), (256, 384), (384, 512))
LANES = 128
far = -1e30


def nn(left, right):
    return jnp.dot(left, right, preferred_element_type=jnp.float32)


def tn(left, right):
    return lax.dot_general(left, right, (((0,), (0,)), ((), ())), preferred_element_type=jnp.float32)


def nt(left, right):
    return lax.dot_general(left, right, (((1,), (1,)), ((), ())), preferred_element_type=jnp.float32)


def low(values):
    return values.astype(jnp.bfloat16)


def wide(values):
    return values.astype(jnp.float32)


def iota(shape, axis):
    return lax.broadcasted_iota(jnp.int32, shape, axis)


def matrix(ref):
    return ref[...].reshape(-1, ref.shape[-1])


def block_of(i):
    return pl.ds(BLOCK * i if isinstance(i, int) else pl.multiple_of(i * BLOCK, BLOCK), BLOCK)


def lanes_of(first):
    return pl.ds(first if isinstance(first, int) else pl.multiple_of(first, LANES), LANES)


def boundaries(lengths):
    starts, ends, at = [], [], 0
    for s in range(lengths.shape[1]):
        starts.append(at)
        at = at + lengths[0, s]
        ends.append(at)
    before, after = [], []
    for edge in (BLOCK, 2 * BLOCK, 3 * BLOCK):
        tail, head = 0, 0
        for start, end in zip(starts, ends):
            across = (start < edge) & (end > edge)
            tail = tail + jnp.where(across, edge - start, 0)
            head = head + jnp.where(across, end - edge, 0)
        before.append(tail)
        after.append(head)
    return starts, ends, before, after


class Attention:
    def __init__(self, lengths):
        self.starts, self.ends, self.before, self.after = boundaries(lengths)
        self.rows = iota((BLOCK, LANES), 0)
        self.lanes = iota((BLOCK, LANES), 1)
        self.left = self.lanes < 64

    def members(self, block):
        rows, lanes = self.rows + block * BLOCK, lax.rem(self.lanes, 64)
        marks = jnp.zeros((BLOCK, LANES), jnp.float32)
        for s, (start, end) in enumerate(zip(self.starts, self.ends)):
            inside = (rows >= start) & (rows < end) & (lanes == s)
            marks = jnp.where(inside, 1.0, marks)
        return marks

    def merged(self, blocks):
        return [*blocks, *[jnp.where(self.in_head(i), blocks[i + 1], blocks[i]) for i in range(3)]]

    def half(self, side):
        return self.left if side == 0 else ~self.left

    def in_head(self, edge):
        return self.rows < self.after[edge]

    def in_tail(self, edge):
        return self.rows >= BLOCK - self.before[edge]

    def pick(self, parts):
        out = []
        for i in range(4):
            block = parts[i]
            if i < 3:
                block = jnp.where(self.in_tail(i), parts[4 + i], block)
            if i > 0:
                block = jnp.where(self.in_head(i - 1), parts[3 + i], block)
            out.append(block)
        return out

    def gather_sums(self, parts):
        out = []
        for i in range(4):
            block = parts[i]
            if i < 3:
                block = block + jnp.where(self.in_head(i), 0.0, parts[4 + i])
            if i > 0:
                block = block + jnp.where(self.in_head(i - 1), parts[3 + i], 0.0)
            out.append(block)
        return out

    def units(self, blocks):
        out = []
        for i in range(4):
            block = blocks[i]
            if i < 3:
                block = jnp.where(self.in_tail(i), 0.0, block)
            if i > 0:
                block = jnp.where(self.in_head(i - 1), 0.0, block)
            out.append(block)
        for i in range(3):
            tail = jnp.where(self.in_tail(i), blocks[i], 0.0)
            out.append(jnp.where(self.in_head(i), blocks[i + 1], tail))
        return out


def square_of(r, part):
    first = STARTS[part]
    return r.wqkv[:, :, :, :, :, first : first + 512].reshape(512, 512)


def mark(r, at):
    for unit, marks in enumerate(at.merged([at.members(i) for i in range(4)])):
        r.marks[unit] = low(marks)


def project(r, at, part):
    dest = (r.q, r.k, r.v)[part]

    def put(unit, product):
        marks = wide(r.marks[unit])
        beside = (marks, jnp.where(lax.rem(at.lanes, 64) < 8, far - far * marks, 0.0), 1.0)[part]
        for pair in range(4):
            both = product[:, LANES * pair : LANES * (pair + 1)]
            for side in range(2):
                dest[2 * pair + side, unit] = low(jnp.where(at.half(side), both, beside))

    head = [iota((BLOCK, 512), 0) < count for count in at.after]
    for i in range(4):
        product = nn(r.x[block_of(i)], square_of(r, part))
        if part == 0:
            product = (product + r.vec[Q_BIAS : Q_BIAS + 1]) * 0.125
        elif part == 2:
            product = product + r.vec[V_BIAS : V_BIAS + 1]
        put(i, product)
        if i > 0:
            put(3 + i, jnp.where(head[i - 1], product, before))
        before = product


def attend(r, at, pair):
    outs = []
    for side in range(2):
        head = 2 * pair + side
        parts = []
        for unit in range(7):
            scores = nt(r.k[head, unit], r.q[head, unit])
            top = jnp.max(scores, axis=0, keepdims=True)
            grown = low(jnp.exp(scores - top))
            r.e[head, unit] = grown
            parts.append(tn(grown, r.v[head, unit]))
        outs.append(at.pick(parts))
    columns = lanes_of(pair * LANES)
    for i in range(4):
        even, odd = outs[0][i], outs[1][i]
        share = 1.0 / pltpu.roll(jnp.where(at.left, odd, even), 64, 1)
        mixed = jnp.where(at.left, even, odd) * share
        r.combined[BLOCK * i : BLOCK * (i + 1), columns] = low(mixed)
        r.share[BLOCK * i : BLOCK * (i + 1), columns] = share


def normal(values):
    center = values - jnp.mean(values, axis=-1, keepdims=True)
    spread = jnp.mean(center * center, axis=-1, keepdims=True)
    scale = lax.rsqrt(spread + norm_eps)
    return center * scale, scale


def normal_back(grad, normed, scale):
    return scale * (
        grad
        - jnp.mean(grad, axis=-1, keepdims=True)
        - normed * jnp.mean(grad * normed, axis=-1, keepdims=True)
    )


def sums(values):
    return jnp.sum(values, axis=0, keepdims=True)


def attended_rows(r, i):
    rows = block_of(i)
    attended = nn(r.combined[rows], matrix(r.wo)) + r.vec[O_BIAS : O_BIAS + 1]
    normed, scale = normal(wide(r.x[rows]) + attended)
    r.normed[rows] = normed
    r.scale[rows] = jnp.broadcast_to(scale, (BLOCK, LANES))
    r.hidden[rows] = low(normed * r.vec[GAIN_ONE : GAIN_ONE + 1] + r.vec[SHIFT_ONE : SHIFT_ONE + 1])


def active_rows(r, side, i):
    rows = block_of(i)
    hidden_low = r.hidden[rows]
    slope = math.sqrt(2 / math.pi)
    for part in (2 * side, 2 * side + 1):
        columns = slice(512 * part, 512 * (part + 1))
        inner = nn(hidden_low, r.wi[:, :, :, :, :, columns].reshape(512, 512)) + r.ib[:, columns]
        square = inner * inner
        half = 0.5 * jnp.tanh(inner * (slope + (slope * 0.044715) * square)) + 0.5
        active = inner * half
        r.active[rows, columns] = low(active)
        turn = half + active * (1.0 - half) * (2 * slope + (6 * slope * 0.044715) * square)
        r.turn[rows, columns] = low(turn)


def final_rows(r, i):
    rows = block_of(i)
    hidden = r.normed[rows] * r.vec[GAIN_ONE : GAIN_ONE + 1] + r.vec[SHIFT_ONE : SHIFT_ONE + 1]
    outer = nn(r.active[rows], matrix(r.wu)) + r.vec[U_BIAS : U_BIAS + 1]
    normed, scale = normal(outer + hidden + wide(r.x[rows]))
    gain = r.vec[GAIN_TWO : GAIN_TWO + 1]
    r.out[rows] = low(normed * gain + r.vec[SHIFT_TWO : SHIFT_TWO + 1])
    grad = wide(r.cot[rows])
    r.gvec[GAIN_TWO : GAIN_TWO + 1] += sums(grad * normed)
    r.gvec[SHIFT_TWO : SHIFT_TWO + 1] += sums(grad)
    grad_two = normal_back(grad * gain, normed, scale)
    r.grad[rows] = grad_two
    grad_outer = low(grad_two)
    r.grad_outer[rows] = grad_outer
    r.gvec[U_BIAS : U_BIAS + 1] += sums(wide(grad_outer))


def rows_of(ref, quarter):
    return ref[quarter // 2, quarter % 2].reshape(-1, ref.shape[-1])


def outer_weight_grad(r):
    for quarter in range(4):
        columns = slice(512 * quarter, 512 * (quarter + 1))
        product = low(tn(r.active[:, columns], r.grad_outer[...]))
        r.gu[quarter // 2, quarter % 2] = product.reshape(r.gu.shape[2:])


def inner_rows(r, i):
    rows = block_of(i)
    grad_outer = r.grad_outer[rows]
    for part in range(4):
        columns = slice(512 * part, 512 * (part + 1))
        grad_inner = low(nt(grad_outer, rows_of(r.wu, part)) * wide(r.turn[rows, columns]))
        r.active[rows, columns] = grad_inner
        r.gib[:, columns] += sums(wide(grad_inner))


def inner_weight_grad(r, side):
    for half in range(2):
        for part in (2 * side, 2 * side + 1):
            columns = slice(512 * part, 512 * (part + 1))
            product = low(tn(r.hidden[:, 256 * half : 256 * (half + 1)], r.active[:, columns]))
            r.gi[half, :, :, :, :, columns] = product.reshape(2, 4, 2, -1, 512)


def hidden_rows(r, i):
    rows = block_of(i)
    grad_two = r.grad[rows]
    grad_hidden = nt(r.active[rows], matrix(r.wi)) + grad_two
    normed = r.normed[rows]
    r.gvec[GAIN_ONE : GAIN_ONE + 1] += sums(grad_hidden * normed)
    r.gvec[SHIFT_ONE : SHIFT_ONE + 1] += sums(grad_hidden)
    gain = r.vec[GAIN_ONE : GAIN_ONE + 1]
    grad_one = normal_back(grad_hidden * gain, normed, r.scale[rows, 0:1])
    r.grad[rows] = grad_two + grad_one
    attended = low(grad_one)
    r.attended[rows] = attended
    r.gvec[O_BIAS : O_BIAS + 1] += sums(wide(attended))
    r.grad_outer[rows] = low(nt(attended, matrix(r.wo)))


def output_weight_grad(r):
    for half in range(2):
        product = low(tn(r.combined[:, 256 * half : 256 * (half + 1)], r.attended[...]))
        r.go[half] = product.reshape(r.go.shape[1:])


def attend_back(r, at, pair):
    columns = lanes_of(pair * LANES)
    ones = low(jnp.where((iota((LANES, LANES), 0) < 64) == (iota((LANES, LANES), 1) < 64), 1.0, 0.0))
    sides = [[], []]
    for i in range(4):
        rows = slice(BLOCK * i, BLOCK * (i + 1))
        grad = wide(r.grad_outer[rows, columns])
        share = r.share[rows, columns]
        product = grad * wide(r.combined[rows, columns])
        high = low(product)
        total = nn(high, ones) + nn(low(product - wide(high)), ones)
        total = pltpu.roll(-(total * share), 64, 1)
        rest = total - wide(low(total))
        lanes = lax.rem(at.lanes, 64)
        beside = jnp.where(lanes == 0, total, jnp.where(lanes == 1, rest, 0.0))
        grad = grad * share
        for side in range(2):
            sides[side].append(jnp.where(at.half(side), grad, beside))
    found = [[], [], []]
    for side in range(2):
        head = 2 * pair + side
        parts = [[], [], []]
        for unit, grad in enumerate(at.units(sides[side])):
            grad = low(grad)
            grown = r.e[head, unit]
            scores = low(wide(grown) * nt(r.v[head, unit], grad))
            parts[0].append(tn(scores, r.k[head, unit]))
            parts[1].append(nn(scores, r.q[head, unit]))
            parts[2].append(nn(grown, grad))
        for which in range(3):
            found[which].append(at.gather_sums(parts[which]))
    for which in range(3):
        total = 0.0
        for i in range(4):
            both = jnp.where(at.left, found[which][0][i], found[which][1][i])
            both = low(both * 0.125 if which == 0 else both)
            (r.dq, r.dk, r.dv)[which][BLOCK * i : BLOCK * (i + 1), columns] = both
            total = total + wide(both)
        if which != 1:
            r.gvec[which // 2 : which // 2 + 1, columns] = sums(total)


def qkv_weight_grad(r, piece):
    first, last = PAIRS[piece]
    for part, grads in enumerate((r.dq, r.dk, r.dv)):
        start = 3 * first + (last - first) * part
        for half in range(2):
            product = low(tn(r.x[:, 256 * half : 256 * (half + 1)], grads[:, first:last]))
            columns = slice(start, start + last - first)
            r.gqkv[half, :, :, :, :, columns] = product.reshape(2, 4, 2, -1, last - first)


def input_rows(r, i):
    rows = block_of(i)
    total = r.grad[rows]
    for part, grads in enumerate((r.dq, r.dk, r.dv)):
        total = total + nt(grads[rows], square_of(r, part))
    r.grad[rows] = total


(
    ZERO, MARK, UNPACK, PROJECT_Q, PROJECT_K, PROJECT_V, ATTEND, ATTENDED, ACTIVE0, ACTIVE1, FINAL, OUTER_GRAD, INNER,
    INNER_GRAD0, INNER_GRAD1, HIDDEN, OUTPUT_GRAD, PACK_EARLY, BACK, QKV_GRAD0, QKV_GRAD1, QKV_GRAD2, PACK_LATE, INPUT,
) = range(24)
LOCAL = [step for step in range(24) if step not in (UNPACK, PACK_EARLY, PACK_LATE)]


def all_rows(rows, r, *given):
    for i in range(4):
        rows(r, *given, i)


def zero(r):
    r.gvec[...] = jnp.zeros_like(r.gvec)
    r.gib[...] = jnp.zeros_like(r.gib)


def steps_of(r):
    at = Attention(r.lengths)
    steps = {
        ZERO: partial(zero, r),
        MARK: partial(mark, r, at),
        UNPACK: partial(unpack_vectors, r),
        ATTEND: partial(attend, r, at),
        ATTENDED: partial(all_rows, attended_rows, r),
        FINAL: partial(all_rows, final_rows, r),
        OUTER_GRAD: partial(outer_weight_grad, r),
        INNER: partial(all_rows, inner_rows, r),
        HIDDEN: partial(all_rows, hidden_rows, r),
        OUTPUT_GRAD: partial(output_weight_grad, r),
        PACK_EARLY: partial(pack_sums, r, True),
        BACK: partial(attend_back, r, at),
        PACK_LATE: partial(pack_sums, r, False),
        INPUT: partial(all_rows, input_rows, r),
    }
    for i in range(3):
        steps[PROJECT_Q + i] = partial(project, r, at, i)
        steps[QKV_GRAD0 + i] = partial(qkv_weight_grad, r, i)
    for i in range(2):
        steps[ACTIVE0 + i] = partial(all_rows, active_rows, r, i)
        steps[INNER_GRAD0 + i] = partial(inner_weight_grad, r, i)
    return steps


def always():
    return lax.axis_index("dp") >= 0


def take(step):
    pl.when(always())(step)


def over_pairs(step, between):
    def body(pair, carried):
        for n in range(4):
            pl.when(pair == n)(partial(between, n))
        step(pair)
        return carried

    lax.fori_loop(0, 4, body, 0)


def run_local(r):
    steps = steps_of(r)
    for step in LOCAL:
        if step in (ATTEND, BACK):
            over_pairs(steps[step], lambda n: None)
        else:
            take(steps[step])
MESH_ID = pl.DeviceIdType.MESH


def place():
    outer, inner = lax.axis_index("dp"), lax.axis_index("fsdp")
    return outer // 2, outer % 2, inner // 2, inner % 2


def device_at(y, core, z, x):
    return (y * 2 + core, z * 2 + x)


def greet_partners():
    y, core, z, x = place()
    partners = [
        device_at(y, 1 - core, z, x),
        device_at(1 - y, core, z, x),
        device_at(y, core, z, 1 - x),
    ] + [device_at(y, core, (z + step) % 4, x) for step in (1, 2, 3)]
    barrier = pltpu.get_barrier_semaphore()
    for partner in partners:
        pl.semaphore_signal(barrier, inc=1, device_id=partner, device_id_type=MESH_ID)
    return lambda: pl.semaphore_wait(barrier, len(partners))


def remote(source, target, send_sem, recv_sem, to):
    return pltpu.make_async_remote_copy(
        src_ref=source,
        dst_ref=target,
        send_sem=send_sem,
        recv_sem=recv_sem,
        device_id=to,
        device_id_type=MESH_ID,
    )


class Corner:
    def __init__(self):
        y, core, z, x = place()
        self.y, self.core, self.z, self.x = y, core, z, x
        self.ya, self.xa = jnp.where(core == 0, y, 1 - y), jnp.where(core == 0, 1 - x, x)
        self.yb, self.xb = jnp.where(core == 0, 1 - y, y), jnp.where(core == 0, x, 1 - x)
        self.partner_a = device_at(self.ya, core, z, self.xa)
        self.partner_b = device_at(self.yb, core, z, self.xb)
        self.sibling = device_at(y, 1 - core, z, x)

    def along_z(self, step):
        return device_at(self.y, self.core, (self.z + step) % 4, self.x)


class Gather:
    def __init__(self, corner, own, whole, send_sem, recv_sem):
        self.at, self.own, self.whole = corner, own, whole
        self.send_sem, self.recv_sem = send_sem, recv_sem

    def to_z(self, step):
        at = self.at
        slot = self.whole.at[at.y, at.core, at.z, at.x]
        return remote(
            self.own, slot, self.send_sem.at[step - 1], self.recv_sem.at[step - 1], at.along_z(step)
        )

    def line(self, y, x, number, to):
        line = self.whole.at[y, self.at.core, :, x]
        return remote(line, line, self.send_sem.at[number], self.recv_sem.at[number], to)

    def to_a(self):
        return self.line(self.at.y, self.at.x, 3, self.at.partner_a)

    def to_b(self, part):
        at = self.at
        y, x = ((at.y, at.x), (at.ya, at.xa))[part]
        return self.line(y, x, 4 + part, at.partner_b)

    def to_sibling(self, part):
        at = self.at
        y, x = ((at.y, at.x), (at.ya, at.xa), (at.yb, at.xb), (1 - at.y, 1 - at.x))[part]
        return self.line(y, x, 6 + part, at.sibling)

    def phase(self, number):
        if number == 0:
            for step in (2, 1, 3):
                self.to_z(step).start()
            at = self.at
            self.whole[at.y, at.core, at.z, at.x] = self.own[...]
        elif number == 1:
            for step in (1, 2, 3):
                self.to_z(step).wait_recv()
            self.to_a().start()
            self.to_b(0).start()
            self.to_sibling(0).start()
        elif number == 2:
            self.to_a().wait_recv()
            self.to_b(1).start()
            self.to_sibling(1).start()
        elif number == 3:
            self.to_b(0).wait_recv()
            self.to_sibling(2).start()
            self.to_b(1).wait_recv()
            self.to_sibling(3).start()
        elif number == 4:
            for part in range(4):
                self.to_sibling(part).wait_recv()

    def finish(self):
        for step in (1, 2, 3):
            self.to_z(step).wait_send()
        self.to_a().wait_send()
        for part in range(2):
            self.to_b(part).wait_send()
        for part in range(4):
            self.to_sibling(part).wait_send()


class Scatter:
    def __init__(self, corner, whole, out, got_core, got_b, got_a, got_z, send_sem, recv_sem):
        self.at, self.whole, self.out = corner, whole, out
        self.got_core, self.got_b, self.got_a, self.got_z = got_core, got_b, got_a, got_z
        self.send_sem, self.recv_sem = send_sem, recv_sem

    def sems(self, number):
        return self.send_sem.at[number], self.recv_sem.at[number]

    def to_sibling(self):
        return remote(
            self.whole.at[:, 1 - self.at.core], self.got_core, *self.sems(0), self.at.sibling
        )

    def to_b(self, part):
        at = self.at
        y, x = ((at.yb, at.xb), (1 - at.y, 1 - at.x))[part]
        return remote(
            self.whole.at[y, at.core, :, x], self.got_b.at[part], *self.sems(1 + part), at.partner_b
        )

    def to_a(self):
        at = self.at
        return remote(
            self.whole.at[at.ya, at.core, :, at.xa], self.got_a, *self.sems(3), at.partner_a
        )

    def to_z(self, step):
        at = self.at
        return remote(
            self.whole.at[at.y, at.core, (at.z + step) % 4, at.x],
            self.got_z.at[step - 1],
            *self.sems(3 + step),
            at.along_z(step),
        )

    def add_line(self, y, x, other):
        core = self.at.core
        for z in range(4):
            total = self.whole[y, core, z, x].astype(jnp.float32) + other(z).astype(jnp.float32)
            self.whole[y, core, z, x] = total.astype(self.whole.dtype)

    def add_core(self, y, x):
        self.add_line(y, x, lambda z: self.got_core[y, z, x])

    def phase(self, number):
        at = self.at
        if number == 0:
            self.to_sibling().start()
        elif number == 1:
            self.to_sibling().wait_recv()
            self.add_core(at.yb, at.xb)
            self.to_b(0).start()
            self.add_core(1 - at.y, 1 - at.x)
            self.to_b(1).start()
            self.add_core(at.ya, at.xa)
            self.add_core(at.y, at.x)
        elif number == 2:
            self.to_b(1).wait_recv()
            self.add_line(at.ya, at.xa, lambda z: self.got_b[1, z])
            self.to_a().start()
            self.to_b(0).wait_recv()
            self.add_line(at.y, at.x, lambda z: self.got_b[0, z])
        elif number == 3:
            self.to_a().wait_recv()
            self.add_line(at.y, at.x, lambda z: self.got_a[z])
            for step in (2, 1, 3):
                self.to_z(step).start()
        elif number == 4:
            total = self.whole[at.y, at.core, at.z, at.x].astype(jnp.float32)
            for step in (1, 2, 3):
                self.to_z(step).wait_recv()
                total = total + self.got_z[step - 1].astype(jnp.float32)
            self.out[...] = total

    def finish(self):
        self.to_sibling().wait_send()
        for part in range(2):
            self.to_b(part).wait_send()
        self.to_a().wait_send()
        for step in (1, 2, 3):
            self.to_z(step).wait_send()


LEAD = (2, 2, 4, 2)
TOKENS, WIDTH = 1024, 512
BF, F32 = jnp.bfloat16, jnp.float32
AXES = ("dp", "fsdp")
SHARDS = dict(wqkv=(16, 1664), wo=(16, 512), wi=(16, 2048), wu=(64, 512))


def local_scratch():
    units, tokens = (8, 7, BLOCK, LANES), (TOKENS, WIDTH)
    return dict(
        q=(units, BF),
        k=(units, BF),
        v=(units, BF),
        e=((8, 7, BLOCK, BLOCK), BF),
        marks=((7, BLOCK, LANES), BF),
        share=(tokens, F32),
        combined=(tokens, BF),
        normed=(tokens, F32),
        scale=((TOKENS, LANES), F32),
        hidden=(tokens, BF),
        active=((TOKENS, 2048), BF),
        turn=((TOKENS, 2048), BF),
        grad_outer=(tokens, BF),
        attended=(tokens, BF),
    )


def call(kernel, inputs, spaces, outputs, scratch, sems, **params):
    names = [*inputs, *outputs, *scratch, *sems]

    def body(*refs):
        kernel(types.SimpleNamespace(**dict(zip(names, refs, strict=True))))

    made = pl.pallas_call(
        body,
        out_shape=[jax.ShapeDtypeStruct(*given) for given in outputs.values()],
        in_specs=[pl.BlockSpec(memory_space=spaces.get(name, pltpu.VMEM)) for name in inputs],
        out_specs=[pl.BlockSpec(memory_space=spaces.get(name, pltpu.VMEM)) for name in outputs],
        scratch_shapes=[pltpu.VMEM(*given) for given in scratch.values()]
        + [pltpu.SemaphoreType.DMA(shape) for shape in sems.values()],
        compiler_params=pltpu.CompilerParams(vmem_limit_bytes=63 << 20, **params),
    )(*inputs.values())
    return types.SimpleNamespace(**dict(zip(outputs, made, strict=True)))


def chosen_lanes(count):
    shape = (LANES, 32 * count)
    return low(jnp.where(iota(shape, 0) == lax.rem(iota(shape, 1), count), 1.0, 0.0))


def of_owner(rows, count):
    shape = (rows, 32 * count)
    return lax.rem(iota(shape, 0), 32) == lax.div(iota(shape, 1), count)


def chosen_rows():
    row, column = iota((288, 512), 0), iota((288, 512), 1)
    return low(jnp.where(column == lax.rem(row, 32) * 16 + lax.div(row, 32), 1.0, 0.0))


def unpack_vectors(r):
    packed = r.wqkv[:, :, :, :, :, PACKED : PACKED + LANES].reshape(512, LANES)
    packed = low(nn(chosen_rows(), packed))
    vectors = jnp.where(of_owner(256, 16), nn(packed[:256], chosen_lanes(16)), 0.0)
    for kind in range(8):
        r.vec[kind : kind + 1] = sums(vectors[32 * kind : 32 * (kind + 1)])
    r.ib[...] = sums(jnp.where(of_owner(32, 64), nn(packed[256:], chosen_lanes(64)), 0.0))


def pack_sums(r, early):
    def placed(values, count):
        alone = jnp.where(of_owner(32, count), values, 0.0)
        high = low(alone)
        lanes = chosen_lanes(count)
        return nt(high, lanes) + nt(low(alone - wide(high)), lanes)

    rows = [placed(r.gvec[kind : kind + 1], 16) for kind in (range(2, 8) if early else range(2))]
    rows += [placed(r.gib[...], 64)] if early else []
    chosen = chosen_rows()[64:] if early else chosen_rows()[:64]
    packed = low(tn(chosen, low(jnp.concatenate(rows, axis=0)))).reshape(*LEAD, 16, LANES)
    if not early:
        packed = packed + r.gqkv[:, :, :, :, :, 1536:1664]
    r.gqkv[:, :, :, :, :, 1536:1664] = packed


Q, K, V, O, I0, I1, U0, U1 = range(8)
SU0, SU1, SI0, SI1, SO, SA, SB, SC = range(8, 16)
X_HERE, COT_HERE, OUT_AWAY, GRAD_AWAY0, GRAD_AWAY1 = range(100, 105)
PLAN = [
    (K, 0), (Q, 0), (V, 0), (O, 0), ZERO, MARK, X_HERE, (K, 1), (I0, 0), (U0, 0), (Q, 1), (K, 2), (V, 1), (Q, 2),
    (O, 1), (I0, 1), (I1, 0), (V, 2), (Q, 3), (Q, 4), (U0, 1), (O, 2), (U1, 0), UNPACK, PROJECT_Q, (K, 3), (V, 3),
    (I1, 1), (V, 4), (K, 4), PROJECT_K, (I0, 2), (U0, 2), PROJECT_V,
    [ATTEND, [], [(O, 3), (U1, 1)], [], [(I1, 2), (O, 4), (I0, 3)]], (U1, 2), (I0, 4), (U0, 3), ATTENDED, ACTIVE0,
    (I1, 3), (U1, 3), (I1, 4), ACTIVE1, (U1, 4), (U0, 4), COT_HERE, FINAL, OUT_AWAY, OUTER_GRAD, (SU0, 0), (SU1, 0),
    INNER, INNER_GRAD0, (SI0, 0), (SU1, 1), (SU0, 1), INNER_GRAD1, HIDDEN, (SU1, 2), OUTPUT_GRAD, (SI1, 0), (SI0, 1),
    PACK_EARLY, (SO, 0), (SU0, 2),
    [BACK, [], [(SU1, 3), (SO, 1), (SI1, 1)], [QKV_GRAD0, (SA, 0), (SU0, 3), (SI0, 2), (SO, 2)], [QKV_GRAD1, (SB, 0), (SA, 1), (SI1, 2), (SI0, 3)]],
    (SB, 1), QKV_GRAD2, PACK_LATE, (SC, 0), (SO, 3), (SA, 2), (SC, 1), (SB, 2), (SI1, 3), (SO, 4), (SU1, 4), (SA, 3),
    (SU0, 4), (SC, 2), (SB, 3), (SC, 3), INPUT, GRAD_AWAY0, GRAD_AWAY1, (SI1, 4), (SI0, 4), (SA, 4), (SB, 4), (SC, 4),
]


def halves_of(buffer):
    first, second = [buffer.at[i : i + 512].reshape(*LEAD, 16, 2048) for i in (0, 512)]
    return first, second.at[:, :, :, :, :, 0:1664]


def direct_kernel(r):
    r.gi, r.gqkv = halves_of(r.turn)
    r.dq = r.wu.at[0].reshape(TOKENS, 512)
    r.dk = r.wu.at[1].reshape(TOKENS, 512)
    r.dv = r.attended
    r.cot = r.attended
    spare = [
        r.active.at[first : first + 16 * math.prod(lead)].reshape(*lead, 16, 2048)
        for lead, first in (((2, 4, 2), 0), ((2, 4), 256), ((4,), 384), ((3,), 448))
    ]
    local = [
        pltpu.make_async_copy(source, target, r.local.at[i])
        for i, (source, target) in enumerate(
            [(r.x_far, r.x), (r.cot_far, r.cot), (r.out, r.out_far)]
            + [(r.grad.at[BLOCK * i : BLOCK * (i + 1)], r.grad_far.at[BLOCK * i : BLOCK * (i + 1)]) for i in range(4)]
        )
    ]
    local[0].start()
    local[1].start()
    corner = Corner()
    met = greet_partners()
    r.own_qkv[:, 0:512] = r.own_query[...]
    r.own_qkv[:, 640:1152] = r.own_key[...]
    r.own_qkv[:, 1152:1664] = r.own_value[...]
    r.own_small[...] = jnp.zeros_like(r.own_small)
    vectors = [r.own0, r.own1, r.own2, r.own3, r.own4, r.own5, r.own6, r.own7, r.own8]
    for i, vector in enumerate(vectors):
        r.own_small[i : i + 1, 0 : vector.shape[0]] = wide(vector[...]).reshape(1, vector.shape[0])
    r.own_qkv[:, 512:640] = low(r.own_small[...])
    met()

    def column_part(ref, first, last):
        return ref.at[(slice(None),) * (len(ref.shape) - 1) + (slice(first, last),)]

    def row_part(ref, first, last):
        return ref.at[(slice(None),) * (len(ref.shape) - 2) + (slice(first, last),)]

    pieces = [(column_part, r.own_qkv, r.wqkv, *ends) for ends in ((0, 640), (640, 1152), (1152, 1664))]
    pieces += [(column_part, r.own_output, r.wo, 0, 512)]
    pieces += [(column_part, r.own_inner, r.wi, *ends) for ends in ((0, 1024), (1024, 2048))]
    pieces += [(row_part, r.own_outer, r.wu, *ends) for ends in ((0, 32), (32, 64))]
    gathers = [
        Gather(corner, cut(own, *ends), cut(whole, *ends), r.gather_send.at[i], r.gather_recv.at[i])
        for i, (cut, own, whole, *ends) in enumerate(pieces)
    ]

    got0 = (r.got0_core, r.got0_b, r.got0_a, r.got0_z)
    got1 = (r.got1_core, r.got1_b, r.got1_a, r.got1_z)
    got2 = (r.got2_core, r.got2_b, r.got2_a, r.got2_z)
    pieces = [(row_part, r.gu, r.out_outer, got0, *ends) for ends in ((0, 32), (32, 64))]
    pieces += [(column_part, r.gi, r.out_inner, got1, *ends) for ends in ((0, 1024), (1024, 2048))]
    pieces += [(column_part, r.go, r.out_output, got2, 0, 512)]
    pieces += [(column_part, r.gqkv, r.out_qkv, spare, *ends) for ends in ((0, 768), (768, 1152), (1152, 1664))]
    scatters = [
        Scatter(
            corner, cut(whole, *ends), cut(out, *ends), *[cut(ref, *ends) for ref in got],
            r.scatter_send.at[i], r.scatter_recv.at[i],
        )
        for i, (cut, whole, out, got, *ends) in enumerate(pieces)
    ]
    pieces = gathers + scatters

    def out_away():
        local[2].start()

    def grad_away(side):
        for copy in local[3 + 2 * side : 5 + 2 * side]:
            copy.start()

    def cot_here():
        for piece in gathers:
            piece.finish()
        local[1].wait()

    steps = steps_of(r) | {
        X_HERE: local[0].wait,
        COT_HERE: cot_here,
        OUT_AWAY: out_away,
        GRAD_AWAY0: partial(grad_away, 0),
        GRAD_AWAY1: partial(grad_away, 1),
    }
    def go_all(items):
        for item in items:
            go(item)

    def go(item):
        if isinstance(item, tuple):
            pieces[item[0]].phase(item[1])
        elif isinstance(item, list):
            over_pairs(steps[item[0]], lambda n: go_all(item[1 + n]))
        elif item < X_HERE:
            take(steps[item])
        else:
            steps[item]()

    go_all(PLAN)
    for piece in scatters:
        piece.finish()
    for copy in local[2:]:
        copy.wait()


def received(shard):
    return [(lead + shard[0], shard[1]) for lead in ((2, 4, 2), (2, 4), (4,), (3,))]


def direct(inputs, lengths, cotangent, weights, vectors, inner_bias):
    tokens = (TOKENS, WIDTH)
    given = dict(x_far=inputs, cot_far=cotangent, lengths=lengths)
    given |= dict(own_query=weights[0], own_key=weights[1], own_value=weights[2])
    given |= dict(own_output=weights[3], own_inner=weights[4], own_outer=weights[5])
    given |= {"own%d" % i: vector for i, vector in enumerate([*vectors, inner_bias])}
    outputs = dict(
        out_far=(tokens, BF),
        grad_far=(tokens, F32),
        out_qkv=(SHARDS["wqkv"], F32),
        out_output=(SHARDS["wo"], F32),
        out_inner=(SHARDS["wi"], F32),
        out_outer=(SHARDS["wu"], F32),
    )
    whole = {name: (LEAD + shard, BF) for name, shard in SHARDS.items()}
    got0, got1, got2 = [received((SHARDS[name], BF)) for name in ("wu", "wi", "wo")]
    scratch = local_scratch() | whole
    scratch |= dict(
        x=(tokens, BF),
        out=(tokens, BF),
        grad=(tokens, F32),
        gu=whole["wu"],
        go=whole["wo"],
        own_qkv=(SHARDS["wqkv"], BF),
        own_small=((16, LANES), F32),
        vec=((8, WIDTH), F32),
        ib=((1, 2048), F32),
        gvec=((8, WIDTH), F32),
        gib=((1, 2048), F32),
        got0_core=got0[0], got0_b=got0[1], got0_a=got0[2], got0_z=got0[3],
        got1_core=got1[0], got1_b=got1[1], got1_a=got1[2], got1_z=got1[3],
        got2_core=got2[0], got2_b=got2[1], got2_a=got2[2], got2_z=got2[3],
    )
    sems = dict(gather_send=(8, 10), gather_recv=(8, 10), scatter_send=(8, 7), scatter_recv=(8, 7), local=(7,))
    spaces = dict(lengths=pltpu.SMEM, x_far=pl.ANY, cot_far=pl.ANY, out_far=pl.ANY, grad_far=pl.ANY)
    made = call(
        direct_kernel, given, spaces, outputs, scratch, sems, collective_id=0, has_side_effects=True
    )
    return hand_over(made)


def hand_over(made):
    count = 4
    rows = TOKENS // count

    def body(out, grad, qkv, output, inner, outer, *refs):
        to_out, to_grad, to_q, to_k, to_v, to_output, to_inner, to_outer = refs[:8]
        vectors, (held_out, held_grad, held_qkv, sem) = refs[8:17], refs[17:]
        copies = []

        def copy(source, target):
            copies.append(pltpu.make_async_copy(source, target, sem.at[len(copies)]))
            copies[-1].start()
            return copies[-1]

        small = copy(qkv, held_qkv)
        parts = []
        for i in range(count):
            part = pl.ds(rows * i, rows)
            for source, held, target in ((grad, held_grad, to_grad), (out, held_out, to_out)):
                parts.append((copy(source.at[part], held.at[part]), held.at[part], target.at[part]))
        to_output[...] = output[...]
        to_inner[...] = inner[...]
        to_outer[...] = outer[...]
        small.wait()
        for i, target in enumerate((to_q, to_k, to_v)):
            for first, last in PAIRS:
                start = 3 * first + (last - first) * i
                target[:, first:last] = held_qkv[:, start : start + last - first]
        for i, target in enumerate(vectors):
            target[...] = held_qkv[i, 1536 : 1536 + target.shape[0]]
        back = []
        for into, held, target in parts:
            into.wait()
            back.append(copy(held, target))
        for each in back:
            each.wait()

    given = [made.out_far, made.grad_far, made.out_qkv, made.out_output, made.out_inner, made.out_outer]
    square = jax.ShapeDtypeStruct((16, 512), F32)
    shapes = [jax.ShapeDtypeStruct(part.shape, part.dtype) for part in given]
    vectors = [jax.ShapeDtypeStruct((16,), F32)] * 8 + [jax.ShapeDtypeStruct((64,), F32)]
    far, near = pl.BlockSpec(memory_space=pl.ANY), pl.BlockSpec(memory_space=pltpu.VMEM)
    out, grad, q, k, v, output, inner, outer, *vectors = pl.pallas_call(
        body,
        out_shape=[*shapes[:2], square, square, square, *shapes[3:], *vectors],
        in_specs=[far, far, far, near, near, near],
        out_specs=[far, far, *[near] * 15],
        scratch_shapes=[
            pltpu.VMEM((TOKENS, WIDTH), BF),
            pltpu.VMEM((TOKENS, WIDTH), F32),
            pltpu.VMEM(SHARDS["wqkv"], F32),
            pltpu.SemaphoreType.DMA((1 + 4 * count,)),
        ],
    )(*given)
    return out, grad, [q, k, v, output, inner, outer], vectors[:8], vectors[8]


def alone_kernel(r):
    r.gi, r.gqkv = halves_of(r.turn)
    r.cot, r.dv, r.dk = r.attended, r.attended, r.hidden
    here = pltpu.make_async_copy(r.cot_far, r.cot, r.local.at[0])
    here.start()
    here.wait()
    run_local(r)
    away = [
        pltpu.make_async_copy(source, target, r.local.at[1 + i])
        for i, (source, target) in enumerate(((r.gi, r.gi_far), (r.gqkv, r.gqkv_far)))
    ]
    for copy in away:
        copy.start()
    for copy in away:
        copy.wait()


def through_collectives(inputs, lengths, cotangent, weights, vectors, inner_bias):
    weights, vectors, inner_bias = jax.tree.map(
        lambda own: lax.all_gather(own, AXES, axis=0, tiled=True), (weights, vectors, inner_bias)
    )
    empty = jnp.zeros((WIDTH, LANES), BF)
    weights = [jnp.concatenate([weights[0], empty, *weights[1:3]], axis=1), *weights[3:]]
    whole = {name: weight.reshape(LEAD + SHARDS[name]) for name, weight in zip(SHARDS, weights)}
    given = dict(x=inputs, cot_far=cotangent, lengths=lengths, **whole)
    given |= dict(vec=jnp.stack(vectors).astype(F32), ib=inner_bias.astype(F32)[None])
    tokens = (TOKENS, WIDTH)
    outputs = dict(out=(tokens, BF), grad=(tokens, F32), gvec=((8, WIDTH), F32), gib=((1, 2048), F32))
    outputs |= dict(gqkv_far=(LEAD + SHARDS["wqkv"], BF), gi_far=(LEAD + SHARDS["wi"], BF))
    outputs |= dict(go=(LEAD + SHARDS["wo"], BF), gu=(LEAD + SHARDS["wu"], BF))
    spaces = dict(lengths=pltpu.SMEM, cot_far=pl.ANY, gqkv_far=pl.ANY, gi_far=pl.ANY)
    scratch = local_scratch() | dict(dq=(tokens, BF))
    made = call(alone_kernel, given, spaces, outputs, scratch, dict(local=(3,)))
    qkv, output, inner, outer = [
        part.reshape(-1, part.shape[-1]).astype(F32) for part in (made.gqkv_far, made.go, made.gi_far, made.gu)
    ]
    grads = []
    for i in range(3):
        starts = [(3 * first + (last - first) * i, last - first) for first, last in PAIRS]
        grads.append(jnp.concatenate([qkv[:, start : start + count] for start, count in starts], axis=1))
    grads += [output, inner, outer]
    grads, vectors, inner_bias = jax.tree.map(
        lambda part: lax.psum_scatter(part, AXES, scatter_dimension=0, tiled=True),
        (grads, [made.gvec[i] for i in range(8)], made.gib[0]),
    )
    return made.out, made.grad, grads, vectors, inner_bias


def solution(mesh):
    on_chips = (mesh.shape["dp"], mesh.shape["fsdp"]) == (4, 8)
    way = direct if on_chips else through_collectives

    def shards(
        inputs, seq_lengths, query_weight, key_weight, value_weight, output_weight, query_bias, value_bias,
        output_bias, first_gain, first_shift, inner_weight, inner_bias, outer_weight, outer_bias, final_gain,
        final_shift, cotangent,
    ):
        weights = [query_weight, key_weight, value_weight, output_weight, inner_weight, outer_weight]
        vectors = [query_bias, value_bias, output_bias, first_gain, first_shift]
        vectors += [outer_bias, final_gain, final_shift]
        out, grad, grads, vectors, inner_total = way(
            inputs, seq_lengths, cotangent, weights, vectors, inner_bias
        )
        return (out, grad, *grads[:4], *vectors[:5], grads[4], inner_total, grads[5], *vectors[5:])

    flat, rows = P(AXES), P(AXES, None)
    weights = (*[rows] * 4, *[flat] * 5, rows, flat, rows, *[flat] * 3)
    return jax.shard_map(
        shards,
        mesh=mesh,
        in_specs=(rows, rows, *weights, rows),
        out_specs=(rows, rows, *weights),
        check_vma=False,
    )
```

```python
from functools import partial
import math
import types

import jax
import jax.numpy as jnp
from jax import lax
from jax.experimental import pallas as pl
from jax.experimental.pallas import tpu as pltpu
from jax.sharding import PartitionSpec as P

norm_eps = 1e-05
Q_BIAS, V_BIAS, O_BIAS, GAIN_ONE, SHIFT_ONE, U_BIAS, GAIN_TWO, SHIFT_TWO = range(8)
BLOCK = 256
STARTS, PACKED = (0, 640, 1152), 512
PAIRS = ((0, 256), (256, 384), (384, 512))
LANES = 128
far = -1e30


def nn(left, right):
    return jnp.dot(left, right, preferred_element_type=jnp.float32)


def tn(left, right):
    return lax.dot_general(left, right, (((0,), (0,)), ((), ())), preferred_element_type=jnp.float32)


def nt(left, right):
    return lax.dot_general(left, right, (((1,), (1,)), ((), ())), preferred_element_type=jnp.float32)


def low(values):
    return values.astype(jnp.bfloat16)


def wide(values):
    return values.astype(jnp.float32)


def iota(shape, axis):
    return lax.broadcasted_iota(jnp.int32, shape, axis)


def matrix(ref):
    return ref[...].reshape(-1, ref.shape[-1])


def block_of(i):
    return pl.ds(BLOCK * i if isinstance(i, int) else pl.multiple_of(i * BLOCK, BLOCK), BLOCK)


def lanes_of(first):
    return pl.ds(first if isinstance(first, int) else pl.multiple_of(first, LANES), LANES)


def boundaries(lengths):
    starts, ends, at = [], [], 0
    for s in range(lengths.shape[1]):
        starts.append(at)
        at = at + lengths[0, s]
        ends.append(at)
    before, after = [], []
    for edge in (BLOCK, 2 * BLOCK, 3 * BLOCK):
        tail, head = 0, 0
        for start, end in zip(starts, ends):
            across = (start < edge) & (end > edge)
            tail = tail + jnp.where(across, edge - start, 0)
            head = head + jnp.where(across, end - edge, 0)
        before.append(tail)
        after.append(head)
    return starts, ends, before, after


class Attention:
    def __init__(self, lengths):
        self.starts, self.ends, self.before, self.after = boundaries(lengths)
        self.rows = iota((BLOCK, LANES), 0)
        self.lanes = iota((BLOCK, LANES), 1)
        self.left = self.lanes < 64

    def members(self, block):
        rows, lanes = self.rows + block * BLOCK, lax.rem(self.lanes, 64)
        marks = jnp.zeros((BLOCK, LANES), jnp.float32)
        for s, (start, end) in enumerate(zip(self.starts, self.ends)):
            inside = (rows >= start) & (rows < end) & (lanes == s)
            marks = jnp.where(inside, 1.0, marks)
        return marks

    def merged(self, blocks):
        return [*blocks, *[jnp.where(self.in_head(i), blocks[i + 1], blocks[i]) for i in range(3)]]

    def half(self, side):
        return self.left if side == 0 else ~self.left

    def in_head(self, edge):
        return self.rows < self.after[edge]

    def in_tail(self, edge):
        return self.rows >= BLOCK - self.before[edge]

    def pick(self, parts):
        out = []
        for i in range(4):
            block = parts[i]
            if i < 3:
                block = jnp.where(self.in_tail(i), parts[4 + i], block)
            if i > 0:
                block = jnp.where(self.in_head(i - 1), parts[3 + i], block)
            out.append(block)
        return out

    def gather_sums(self, parts):
        out = []
        for i in range(4):
            block = parts[i]
            if i < 3:
                block = block + jnp.where(self.in_head(i), 0.0, parts[4 + i])
            if i > 0:
                block = block + jnp.where(self.in_head(i - 1), parts[3 + i], 0.0)
            out.append(block)
        return out

    def units(self, blocks):
        out = []
        for i in range(4):
            block = blocks[i]
            if i < 3:
                block = jnp.where(self.in_tail(i), 0.0, block)
            if i > 0:
                block = jnp.where(self.in_head(i - 1), 0.0, block)
            out.append(block)
        for i in range(3):
            tail = jnp.where(self.in_tail(i), blocks[i], 0.0)
            out.append(jnp.where(self.in_head(i), blocks[i + 1], tail))
        return out


def square_of(r, part):
    first = STARTS[part]
    return r.wqkv[:, :, :, :, :, first : first + 512].reshape(512, 512)


def mark(r, at):
    for unit, marks in enumerate(at.merged([at.members(i) for i in range(4)])):
        r.marks[unit] = low(marks)


def project(r, at, part):
    dest = (r.q, r.k, r.v)[part]

    def put(unit, product):
        marks = wide(r.marks[unit])
        beside = (marks, jnp.where(lax.rem(at.lanes, 64) < 8, far - far * marks, 0.0), 1.0)[part]
        for pair in range(4):
            both = product[:, LANES * pair : LANES * (pair + 1)]
            for side in range(2):
                dest[2 * pair + side, unit] = low(jnp.where(at.half(side), both, beside))

    head = [iota((BLOCK, 512), 0) < count for count in at.after]
    for i in range(4):
        product = nn(r.x[block_of(i)], square_of(r, part))
        if part == 0:
            product = (product + r.vec[Q_BIAS : Q_BIAS + 1]) * 0.125
        elif part == 2:
            product = product + r.vec[V_BIAS : V_BIAS + 1]
        put(i, product)
        if i > 0:
            put(3 + i, jnp.where(head[i - 1], product, before))
        before = product


def attend(r, at, pair):
    outs = []
    for side in range(2):
        head = 2 * pair + side
        parts = []
        for unit in range(7):
            scores = nt(r.k[head, unit], r.q[head, unit])
            top = jnp.max(scores, axis=0, keepdims=True)
            grown = low(jnp.exp(scores - top))
            r.e[head, unit] = grown
            parts.append(tn(grown, r.v[head, unit]))
        outs.append(at.pick(parts))
    columns = lanes_of(pair * LANES)
    for i in range(4):
        even, odd = outs[0][i], outs[1][i]
        share = 1.0 / pltpu.roll(jnp.where(at.left, odd, even), 64, 1)
        mixed = jnp.where(at.left, even, odd) * share
        r.combined[BLOCK * i : BLOCK * (i + 1), columns] = low(mixed)
        r.share[BLOCK * i : BLOCK * (i + 1), columns] = share


def normal(values):
    center = values - jnp.mean(values, axis=-1, keepdims=True)
    spread = jnp.mean(center * center, axis=-1, keepdims=True)
    scale = lax.rsqrt(spread + norm_eps)
    return center * scale, scale


def normal_back(grad, normed, scale):
    return scale * (
        grad
        - jnp.mean(grad, axis=-1, keepdims=True)
        - normed * jnp.mean(grad * normed, axis=-1, keepdims=True)
    )


def sums(values):
    return jnp.sum(values, axis=0, keepdims=True)


def attended_rows(r, i):
    rows = block_of(i)
    attended = nn(r.combined[rows], matrix(r.wo)) + r.vec[O_BIAS : O_BIAS + 1]
    normed, scale = normal(wide(r.x[rows]) + attended)
    r.normed[rows] = normed
    r.scale[rows] = jnp.broadcast_to(scale, (BLOCK, LANES))
    r.hidden[rows] = low(normed * r.vec[GAIN_ONE : GAIN_ONE + 1] + r.vec[SHIFT_ONE : SHIFT_ONE + 1])


def active_rows(r, side, i):
    rows = block_of(i)
    hidden_low = r.hidden[rows]
    slope = math.sqrt(2 / math.pi)
    for part in (2 * side, 2 * side + 1):
        columns = slice(512 * part, 512 * (part + 1))
        inner = nn(hidden_low, r.wi[:, :, :, :, :, columns].reshape(512, 512)) + r.ib[:, columns]
        square = inner * inner
        half = 0.5 * jnp.tanh(inner * (slope + (slope * 0.044715) * square)) + 0.5
        active = inner * half
        r.active[rows, columns] = low(active)
        turn = half + active * (1.0 - half) * (2 * slope + (6 * slope * 0.044715) * square)
        r.turn[rows, columns] = low(turn)


def final_rows(r, i):
    rows = block_of(i)
    hidden = r.normed[rows] * r.vec[GAIN_ONE : GAIN_ONE + 1] + r.vec[SHIFT_ONE : SHIFT_ONE + 1]
    outer = nn(r.active[rows], matrix(r.wu)) + r.vec[U_BIAS : U_BIAS + 1]
    normed, scale = normal(outer + hidden + wide(r.x[rows]))
    gain = r.vec[GAIN_TWO : GAIN_TWO + 1]
    r.out[rows] = low(normed * gain + r.vec[SHIFT_TWO : SHIFT_TWO + 1])
    grad = wide(r.cot[rows])
    r.gvec[GAIN_TWO : GAIN_TWO + 1] += sums(grad * normed)
    r.gvec[SHIFT_TWO : SHIFT_TWO + 1] += sums(grad)
    grad_two = normal_back(grad * gain, normed, scale)
    r.grad[rows] = grad_two
    grad_outer = low(grad_two)
    r.grad_outer[rows] = grad_outer
    r.gvec[U_BIAS : U_BIAS + 1] += sums(wide(grad_outer))


def rows_of(ref, quarter):
    return ref[quarter // 2, quarter % 2].reshape(-1, ref.shape[-1])


def outer_weight_grad(r, side):
    for quarter in range(4):
        rows, columns = slice(512 * quarter, 512 * (quarter + 1)), slice(256 * side, 256 * (side + 1))
        product = low(tn(r.active[:, rows], r.grad_outer[:, columns]))
        r.gu[quarter // 2, quarter % 2, :, :, :, columns] = product.reshape(4, 2, -1, 256)


def inner_rows(r, i):
    rows = block_of(i)
    grad_outer = r.grad_outer[rows]
    for part in range(4):
        columns = slice(512 * part, 512 * (part + 1))
        grad_inner = low(nt(grad_outer, rows_of(r.wu, part)) * wide(r.turn[rows, columns]))
        r.active[rows, columns] = grad_inner
        r.gib[:, columns] += sums(wide(grad_inner))


def inner_weight_grad(r, side):
    for half in range(2):
        for part in (2 * side, 2 * side + 1):
            columns = slice(512 * part, 512 * (part + 1))
            product = low(tn(r.hidden[:, 256 * half : 256 * (half + 1)], r.active[:, columns]))
            r.gi[half, :, :, :, :, columns] = product.reshape(2, 4, 2, -1, 512)


def hidden_rows(r, i):
    rows = block_of(i)
    grad_two = r.grad[rows]
    grad_hidden = nt(r.active[rows], matrix(r.wi)) + grad_two
    normed = r.normed[rows]
    r.gvec[GAIN_ONE : GAIN_ONE + 1] += sums(grad_hidden * normed)
    r.gvec[SHIFT_ONE : SHIFT_ONE + 1] += sums(grad_hidden)
    gain = r.vec[GAIN_ONE : GAIN_ONE + 1]
    grad_one = normal_back(grad_hidden * gain, normed, r.scale[rows, 0:1])
    r.grad[rows] = grad_two + grad_one
    attended = low(grad_one)
    r.attended[rows] = attended
    r.gvec[O_BIAS : O_BIAS + 1] += sums(wide(attended))
    r.grad_outer[rows] = low(nt(attended, matrix(r.wo)))


def output_weight_grad(r):
    for half in range(2):
        product = low(tn(r.combined[:, 256 * half : 256 * (half + 1)], r.attended[...]))
        r.go[half] = product.reshape(r.go.shape[1:])


def attend_back(r, at, pair):
    columns = lanes_of(pair * LANES)
    ones = low(jnp.where((iota((LANES, LANES), 0) < 64) == (iota((LANES, LANES), 1) < 64), 1.0, 0.0))
    sides = [[], []]
    for i in range(4):
        rows = slice(BLOCK * i, BLOCK * (i + 1))
        grad = wide(r.grad_outer[rows, columns])
        share = r.share[rows, columns]
        product = grad * wide(r.combined[rows, columns])
        high = low(product)
        total = nn(high, ones) + nn(low(product - wide(high)), ones)
        total = pltpu.roll(-(total * share), 64, 1)
        rest = total - wide(low(total))
        lanes = lax.rem(at.lanes, 64)
        beside = jnp.where(lanes == 0, total, jnp.where(lanes == 1, rest, 0.0))
        grad = grad * share
        for side in range(2):
            sides[side].append(jnp.where(at.half(side), grad, beside))
    found = [[], [], []]
    for side in range(2):
        head = 2 * pair + side
        parts = [[], [], []]
        for unit, grad in enumerate(at.units(sides[side])):
            grad = low(grad)
            grown = r.e[head, unit]
            scores = low(wide(grown) * nt(r.v[head, unit], grad))
            parts[0].append(tn(scores, r.k[head, unit]))
            parts[1].append(nn(scores, r.q[head, unit]))
            parts[2].append(nn(grown, grad))
        for which in range(3):
            found[which].append(at.gather_sums(parts[which]))
    for which in range(3):
        total = 0.0
        for i in range(4):
            both = jnp.where(at.left, found[which][0][i], found[which][1][i])
            both = low(both * 0.125 if which == 0 else both)
            (r.dq, r.dk, r.dv)[which][BLOCK * i : BLOCK * (i + 1), columns] = both
            total = total + wide(both)
        if which != 1:
            r.gvec[which // 2 : which // 2 + 1, columns] = sums(total)


def qkv_weight_grad(r, piece):
    first, last = PAIRS[piece]
    for part, grads in enumerate((r.dq, r.dk, r.dv)):
        start = 3 * first + (last - first) * part
        for half in range(2):
            product = low(tn(r.x[:, 256 * half : 256 * (half + 1)], grads[:, first:last]))
            columns = slice(start, start + last - first)
            r.gqkv[half, :, :, :, :, columns] = product.reshape(2, 4, 2, -1, last - first)


def input_rows(r, i):
    rows = block_of(i)
    total = r.grad[rows]
    for part, grads in enumerate((r.dq, r.dk, r.dv)):
        total = total + nt(grads[rows], square_of(r, part))
    r.grad[rows] = total


(
    ZERO, MARK, UNPACK, PROJECT_Q, PROJECT_K, PROJECT_V, ATTEND, ATTENDED, ACTIVE0, ACTIVE1, FINAL, OUTER_GRAD0, OUTER_GRAD1, INNER,
    INNER_GRAD0, INNER_GRAD1, HIDDEN, OUTPUT_GRAD, PACK_EARLY, BACK, QKV_GRAD0, QKV_GRAD1, QKV_GRAD2, PACK_LATE, INPUT,
) = range(25)
LOCAL = [step for step in range(25) if step not in (UNPACK, PACK_EARLY, PACK_LATE)]


def all_rows(rows, r, *given):
    for i in range(4):
        rows(r, *given, i)


def rows_by_two(rows, r):
    def two(i, carried):
        rows(r, 2 * i)
        rows(r, 2 * i + 1)
        return carried

    lax.fori_loop(0, 2, two, 0)


def zero(r):
    r.gvec[...] = jnp.zeros_like(r.gvec)
    r.gib[...] = jnp.zeros_like(r.gib)


def steps_of(r):
    at = Attention(r.lengths)
    steps = {
        ZERO: partial(zero, r),
        MARK: partial(mark, r, at),
        UNPACK: partial(unpack_vectors, r),
        ATTEND: partial(attend, r, at),
        ATTENDED: partial(all_rows, attended_rows, r),
        FINAL: partial(all_rows, final_rows, r),
        INNER: partial(all_rows, inner_rows, r),
        HIDDEN: partial(rows_by_two, hidden_rows, r),
        OUTPUT_GRAD: partial(output_weight_grad, r),
        PACK_EARLY: partial(pack_sums, r, True),
        BACK: partial(attend_back, r, at),
        PACK_LATE: partial(pack_sums, r, False),
        INPUT: partial(rows_by_two, input_rows, r),
    }
    for i in range(3):
        steps[PROJECT_Q + i] = partial(project, r, at, i)
        steps[QKV_GRAD0 + i] = partial(qkv_weight_grad, r, i)
    for i in range(2):
        steps[ACTIVE0 + i] = partial(all_rows, active_rows, r, i)
        steps[OUTER_GRAD0 + i] = partial(outer_weight_grad, r, i)
        steps[INNER_GRAD0 + i] = partial(inner_weight_grad, r, i)
    return steps


def always():
    return lax.axis_index("dp") >= 0


def take(step):
    pl.when(always())(step)


def over_pairs(step, between):
    def body(pair, carried):
        for n in range(4):
            pl.when(pair == n)(partial(between, n))
        step(pair)
        return carried

    lax.fori_loop(0, 4, body, 0)


def run_local(r):
    steps = steps_of(r)
    for step in LOCAL:
        if step in (ATTEND, BACK):
            over_pairs(steps[step], lambda n: None)
        else:
            take(steps[step])
MESH_ID = pl.DeviceIdType.MESH


def place():
    outer, inner = lax.axis_index("dp"), lax.axis_index("fsdp")
    return outer // 2, outer % 2, inner // 2, inner % 2


def device_at(y, core, z, x):
    return (y * 2 + core, z * 2 + x)


def greet_partners():
    y, core, z, x = place()
    partners = [
        device_at(y, 1 - core, z, x),
        device_at(1 - y, core, z, x),
        device_at(y, core, z, 1 - x),
        device_at(1 - y, core, z, 1 - x),
    ] + [device_at(y, core, (z + step) % 4, x) for step in (1, 2, 3)]
    barrier = pltpu.get_barrier_semaphore()
    for partner in partners:
        pl.semaphore_signal(barrier, inc=1, device_id=partner, device_id_type=MESH_ID)
    return lambda: pl.semaphore_wait(barrier, len(partners))


def remote(source, target, send_sem, recv_sem, to):
    return pltpu.make_async_remote_copy(
        src_ref=source,
        dst_ref=target,
        send_sem=send_sem,
        recv_sem=recv_sem,
        device_id=to,
        device_id_type=MESH_ID,
    )


class Corner:
    def __init__(self):
        y, core, z, x = place()
        self.y, self.core, self.z, self.x = y, core, z, x
        self.ya, self.xa = jnp.where(core == 0, y, 1 - y), jnp.where(core == 0, 1 - x, x)
        self.yb, self.xb = jnp.where(core == 0, 1 - y, y), jnp.where(core == 0, x, 1 - x)
        self.partner_a = device_at(self.ya, core, z, self.xa)
        self.partner_b = device_at(self.yb, core, z, self.xb)
        self.sibling = device_at(y, 1 - core, z, x)
        self.across = device_at(1 - y, core, z, 1 - x)

    def along_z(self, step):
        return device_at(self.y, self.core, (self.z + step) % 4, self.x)


class Gather:
    def __init__(self, corner, own, whole, send_sem, recv_sem):
        self.at, self.own, self.whole = corner, own, whole
        self.send_sem, self.recv_sem = send_sem, recv_sem

    def to_z(self, step):
        at = self.at
        slot = self.whole.at[at.y, at.core, at.z, at.x]
        return remote(
            self.own, slot, self.send_sem.at[step - 1], self.recv_sem.at[step - 1], at.along_z(step)
        )

    def line(self, y, x, number, to):
        line = self.whole.at[y, self.at.core, :, x]
        return remote(line, line, self.send_sem.at[number], self.recv_sem.at[number], to)

    def to_a(self):
        return self.line(self.at.y, self.at.x, 3, self.at.partner_a)

    def to_b(self, part):
        at = self.at
        y, x = ((at.y, at.x), (at.ya, at.xa))[part]
        return self.line(y, x, 4 + part, at.partner_b)

    def to_sibling(self, part):
        at = self.at
        y, x = ((at.y, at.x), (at.ya, at.xa), (at.yb, at.xb), (1 - at.y, 1 - at.x))[part]
        return self.line(y, x, 6 + part, at.sibling)

    def phase(self, number):
        if number == 0:
            for step in (2, 1, 3):
                self.to_z(step).start()
            at = self.at
            self.whole[at.y, at.core, at.z, at.x] = self.own[...]
        elif number == 1:
            for step in (1, 2, 3):
                self.to_z(step).wait_recv()
            self.to_a().start()
            self.to_b(0).start()
            self.to_sibling(0).start()
        elif number == 2:
            self.to_a().wait_recv()
            self.to_b(1).start()
            self.to_sibling(1).start()
        elif number == 3:
            self.to_b(0).wait_recv()
            self.to_sibling(2).start()
            self.to_b(1).wait_recv()
            self.to_sibling(3).start()
        elif number == 4:
            for part in range(4):
                self.to_sibling(part).wait_recv()

    def finish(self):
        for step in (1, 2, 3):
            self.to_z(step).wait_send()
        self.to_a().wait_send()
        for part in range(2):
            self.to_b(part).wait_send()
        for part in range(4):
            self.to_sibling(part).wait_send()


class GatherPlaneFirst(Gather):
    def slot(self, y, x, number, to):
        slot = self.whole.at[y, self.at.core, self.at.z, x]
        return remote(slot, slot, self.send_sem.at[number], self.recv_sem.at[number], to)

    def to_a(self):
        return self.slot(self.at.y, self.at.x, 3, self.at.partner_a)

    def to_b(self, part):
        at = self.at
        y, x = ((at.y, at.x), (at.ya, at.xa))[part]
        return self.slot(y, x, 4 + part, at.partner_b)

    def plane(self, z, number, to):
        plane = self.whole.at[:, self.at.core, z]
        return remote(plane, plane, self.send_sem.at[number], self.recv_sem.at[number], to)

    def to_z(self, step):
        return self.plane(self.at.z, step - 1, self.at.along_z(step))

    def to_sibling(self, part):
        return self.plane((self.at.z + part) % 4, 6 + part, self.at.sibling)

    def phase(self, number):
        at = self.at
        if number == 0:
            self.whole[at.y, at.core, at.z, at.x] = self.own[...]
            self.to_a().start()
            self.to_b(0).start()
        elif number == 1:
            self.to_a().wait_recv()
            self.to_b(1).start()
        elif number == 2:
            self.to_b(0).wait_recv()
            self.to_b(1).wait_recv()
            for step in (2, 1, 3):
                self.to_z(step).start()
            self.to_sibling(0).start()
        elif number == 3:
            for step in (1, 3, 2):
                self.to_z(step).wait_recv()
                self.to_sibling(4 - step).start()
        elif number == 4:
            for part in range(4):
                self.to_sibling(part).wait_recv()


class Scatter:
    def __init__(self, corner, whole, out, got_core, got_b, got_a, got_z, send_sem, recv_sem):
        self.at, self.whole, self.out = corner, whole, out
        self.got_core, self.got_b, self.got_a, self.got_z = got_core, got_b, got_a, got_z
        self.send_sem, self.recv_sem = send_sem, recv_sem

    def sems(self, number):
        return self.send_sem.at[number], self.recv_sem.at[number]

    def to_sibling(self):
        return remote(
            self.whole.at[:, 1 - self.at.core], self.got_core, *self.sems(0), self.at.sibling
        )

    def to_b(self, part):
        at = self.at
        y, x = ((at.yb, at.xb), (1 - at.y, 1 - at.x))[part]
        return remote(
            self.whole.at[y, at.core, :, x], self.got_b.at[part], *self.sems(1 + part), at.partner_b
        )

    def to_a(self):
        at = self.at
        return remote(
            self.whole.at[at.ya, at.core, :, at.xa], self.got_a, *self.sems(3), at.partner_a
        )

    def to_z(self, step):
        at = self.at
        return remote(
            self.whole.at[at.y, at.core, (at.z + step) % 4, at.x],
            self.got_z.at[step - 1],
            *self.sems(3 + step),
            at.along_z(step),
        )

    def add_line(self, y, x, other):
        core = self.at.core
        for z in range(4):
            total = self.whole[y, core, z, x].astype(jnp.float32) + other(z).astype(jnp.float32)
            self.whole[y, core, z, x] = total.astype(self.whole.dtype)

    def add_core(self, y, x):
        self.add_line(y, x, lambda z: self.got_core[y, z, x])

    def phase(self, number):
        at = self.at
        if number == 0:
            self.to_sibling().start()
        elif number == 1:
            self.to_sibling().wait_recv()
            self.add_core(at.yb, at.xb)
            self.to_b(0).start()
            self.add_core(1 - at.y, 1 - at.x)
            self.to_b(1).start()
            self.add_core(at.ya, at.xa)
            self.add_core(at.y, at.x)
        elif number == 2:
            self.to_b(1).wait_recv()
            self.add_line(at.ya, at.xa, lambda z: self.got_b[1, z])
            self.to_a().start()
            self.to_b(0).wait_recv()
            self.add_line(at.y, at.x, lambda z: self.got_b[0, z])
        elif number == 3:
            self.to_a().wait_recv()
            self.add_line(at.y, at.x, lambda z: self.got_a[z])
            for step in (2, 1, 3):
                self.to_z(step).start()
        elif number == 4:
            total = self.whole[at.y, at.core, at.z, at.x].astype(jnp.float32)
            for step in (1, 2, 3):
                self.to_z(step).wait_recv()
                total = total + self.got_z[step - 1].astype(jnp.float32)
            self.out[...] = total

    def finish(self):
        self.to_sibling().wait_send()
        for part in range(2):
            self.to_b(part).wait_send()
        self.to_a().wait_send()
        for step in (1, 2, 3):
            self.to_z(step).wait_send()


class ScatterDirect(Scatter):
    def phase(self, number):
        at = self.at
        if number == 1:
            self.to_sibling().wait_recv()
            self.add_core(1 - at.y, 1 - at.x)
            self.to_b(1).start()
            self.add_core(at.yb, at.xb)
            self.to_b(0).start()
            self.add_core(at.ya, at.xa)
            self.to_a().start()
            self.add_core(at.y, at.x)
        elif number == 2:
            self.to_a().wait_recv()
            for part in range(2):
                self.to_b(part).wait_recv()
            for z in range(4):
                line = self.whole[at.y, at.core, z, at.x].astype(jnp.float32)
                for got in (self.got_a[z], self.got_b[0, z], self.got_b[1, z]):
                    line = line + got.astype(jnp.float32)
                self.whole[at.y, at.core, z, at.x] = line.astype(self.whole.dtype)
            for step in (2, 1, 3):
                self.to_z(step).start()
        elif number != 3:
            super().phase(number)

    def to_b(self, part):
        at = self.at
        y, x, to = ((at.yb, at.xb, at.partner_b), (1 - at.y, 1 - at.x, at.across))[part]
        return remote(self.whole.at[y, at.core, :, x], self.got_b.at[part], *self.sems(1 + part), to)


class ScatterPlaneLast(Scatter):
    def to_z(self, step):
        at = self.at
        return remote(
            self.whole.at[:, at.core, (at.z + step) % 4],
            self.got_z.at[step - 1],
            *self.sems(3 + step),
            at.along_z(step),
        )

    def to_b(self, part):
        at = self.at
        y, x = ((at.yb, at.xb), (1 - at.y, 1 - at.x))[part]
        source = self.whole.at[y, at.core, at.z, x]
        return remote(source, self.got_b.at[part], *self.sems(1 + part), at.partner_b)

    def to_a(self):
        at = self.at
        source = self.whole.at[at.ya, at.core, at.z, at.xa]
        return remote(source, self.got_a, *self.sems(3), at.partner_a)

    def add(self, y, z, x, *others):
        core = self.at.core
        total = self.whole[y, core, z, x].astype(jnp.float32)
        for other in others:
            total = total + other.astype(jnp.float32)
        self.whole[y, core, z, x] = total.astype(self.whole.dtype)

    def phase(self, number):
        at = self.at
        places = [(y, x) for y in range(2) for x in range(2)]
        if number == 0:
            self.to_sibling().start()
        elif number == 1:
            self.to_sibling().wait_recv()
            for step in (2, 1, 3, 0):
                z = (at.z + step) % 4
                for y, x in places:
                    self.add(y, z, x, self.got_core[y, z, x])
                if step:
                    self.to_z(step).start()
        elif number == 2:
            for step in (1, 2, 3):
                self.to_z(step).wait_recv()
            for y, x in places:
                self.add(y, at.z, x, *[self.got_z[step, y, x] for step in range(3)])
            for part in range(2):
                self.to_b(part).start()
        elif number == 3:
            self.to_b(1).wait_recv()
            self.add(at.ya, at.z, at.xa, self.got_b[1])
            self.to_a().start()
            self.to_b(0).wait_recv()
        elif number == 4:
            self.to_a().wait_recv()
            total = self.whole[at.y, at.core, at.z, at.x].astype(jnp.float32)
            self.out[...] = total + self.got_b[0].astype(jnp.float32) + self.got_a[...].astype(jnp.float32)
LEAD = (2, 2, 4, 2)
TOKENS, WIDTH = 1024, 512
BF, F32 = jnp.bfloat16, jnp.float32
AXES = ("dp", "fsdp")
SHARDS = dict(wqkv=(16, 1664), wo=(16, 512), wi=(16, 2048), wu=(64, 512))


def local_scratch():
    units, tokens = (8, 7, BLOCK, LANES), (TOKENS, WIDTH)
    return dict(
        q=(units, BF),
        k=(units, BF),
        v=(units, BF),
        e=((8, 7, BLOCK, BLOCK), BF),
        marks=((7, BLOCK, LANES), BF),
        share=(tokens, F32),
        combined=(tokens, BF),
        normed=(tokens, F32),
        scale=((TOKENS, LANES), F32),
        hidden=(tokens, BF),
        active=((TOKENS, 2048), BF),
        turn=((TOKENS, 2048), BF),
        grad_outer=(tokens, BF),
        attended=(tokens, BF),
    )


def call(kernel, inputs, spaces, outputs, scratch, sems, **params):
    names = [*inputs, *outputs, *scratch, *sems]

    def body(*refs):
        kernel(types.SimpleNamespace(**dict(zip(names, refs, strict=True))))

    made = pl.pallas_call(
        body,
        out_shape=[jax.ShapeDtypeStruct(*given) for given in outputs.values()],
        in_specs=[pl.BlockSpec(memory_space=spaces.get(name, pltpu.VMEM)) for name in inputs],
        out_specs=[pl.BlockSpec(memory_space=spaces.get(name, pltpu.VMEM)) for name in outputs],
        scratch_shapes=[pltpu.VMEM(*given) for given in scratch.values()]
        + [pltpu.SemaphoreType.DMA(shape) for shape in sems.values()],
        compiler_params=pltpu.CompilerParams(vmem_limit_bytes=63 << 20, **params),
    )(*inputs.values())
    return types.SimpleNamespace(**dict(zip(outputs, made, strict=True)))


def chosen_lanes(count):
    shape = (LANES, 32 * count)
    return low(jnp.where(iota(shape, 0) == lax.rem(iota(shape, 1), count), 1.0, 0.0))


def of_owner(rows, count):
    shape = (rows, 32 * count)
    return lax.rem(iota(shape, 0), 32) == lax.div(iota(shape, 1), count)


def chosen_rows():
    row, column = iota((288, 512), 0), iota((288, 512), 1)
    return low(jnp.where(column == lax.rem(row, 32) * 16 + lax.div(row, 32), 1.0, 0.0))


def unpack_vectors(r):
    packed = r.wqkv[:, :, :, :, :, PACKED : PACKED + LANES].reshape(512, LANES)
    packed = low(nn(chosen_rows(), packed))
    vectors = jnp.where(of_owner(256, 16), nn(packed[:256], chosen_lanes(16)), 0.0)
    for kind in range(8):
        r.vec[kind : kind + 1] = sums(vectors[32 * kind : 32 * (kind + 1)])
    r.ib[...] = sums(jnp.where(of_owner(32, 64), nn(packed[256:], chosen_lanes(64)), 0.0))


def pack_sums(r, early):
    def placed(values, count):
        alone = jnp.where(of_owner(32, count), values, 0.0)
        high = low(alone)
        lanes = chosen_lanes(count)
        return nt(high, lanes) + nt(low(alone - wide(high)), lanes)

    rows = [placed(r.gvec[kind : kind + 1], 16) for kind in (range(2, 8) if early else range(2))]
    rows += [placed(r.gib[...], 64)] if early else []
    chosen = chosen_rows()[64:] if early else chosen_rows()[:64]
    packed = low(tn(chosen, low(jnp.concatenate(rows, axis=0)))).reshape(*LEAD, 16, LANES)
    if not early:
        packed = packed + r.gqkv[:, :, :, :, :, 1536:1664]
    r.gqkv[:, :, :, :, :, 1536:1664] = packed


Q, K, V, O, I0, I1, U0, U1 = range(8)
SU0, SU1, SI0, SI1, SO, SA, SB, SC = range(8, 16)
X_HERE, COT_HERE, OUT_AWAY, GRAD_AWAY0, GRAD_AWAY1 = range(100, 105)
PLAN = [
    (K, 0), (U1, 0), (Q, 0), (V, 0), ZERO, MARK, X_HERE, (U1, 1), (O, 0), (I0, 0), (K, 1), (I1, 0), (Q, 1), (U0, 0),
    (K, 2), (V, 1), (Q, 2), (O, 1), (V, 2), (I0, 1), (Q, 3), (K, 3), (O, 2), (Q, 4), (U1, 2), UNPACK, PROJECT_Q,
    (K, 4), (V, 3), (I1, 1), PROJECT_K, (I0, 2), (V, 4), PROJECT_V,
    [ATTEND, [], [(U0, 1)], [(I1, 2), (O, 3)], [(I0, 3)]], (O, 4), (U0, 2), (I0, 4), ATTENDED, ACTIVE0, (I1, 3),
    (U1, 3), (U0, 3), (I1, 4), ACTIVE1, (U0, 4), (U1, 4), COT_HERE, FINAL, OUT_AWAY, OUTER_GRAD0, OUTER_GRAD1,
    (SU0, 0), INNER, (SU1, 0), INNER_GRAD0, (SI0, 0), INNER_GRAD1, (SI1, 0), (SU0, 1), HIDDEN, (SI0, 1), OUTPUT_GRAD,
    (SO, 0), PACK_EARLY, (SU1, 1), (SI1, 1),
    [BACK, [], [(SO, 1), (SI0, 2)], [QKV_GRAD0, (SA, 0), (SO, 2), (SU0, 2), (SI1, 2)], [QKV_GRAD1, (SB, 0), (SO, 3), (SA, 1), (SI0, 3), (SU0, 3), (SB, 1)]],
    (SU1, 2), QKV_GRAD2, (SA, 2), PACK_LATE, (SC, 0), (SI1, 3), (SB, 2), (SC, 1), INPUT, GRAD_AWAY0, GRAD_AWAY1,
    (SO, 4), (SB, 3), (SA, 3), (SU1, 3), (SC, 2), (SB, 4), (SU0, 4), (SC, 3), (SI0, 4), (SC, 4), (SI1, 4), (SA, 4),
    (SU1, 4),
]


def halves_of(buffer):
    first, second = [buffer.at[i : i + 512].reshape(*LEAD, 16, 2048) for i in (0, 512)]
    return first, second.at[:, :, :, :, :, 0:1664]


def direct_kernel(r):
    r.gi, r.gqkv = halves_of(r.turn)
    r.dq = r.wu.at[0].reshape(TOKENS, 512)
    r.dk = r.wu.at[1].reshape(TOKENS, 512)
    r.dv = r.attended
    r.cot = r.attended
    spare = [
        r.active.at[first : first + 16 * math.prod(lead)].reshape(*lead, 16, 2048)
        for lead, first in (((2, 4, 2), 0), ((2, 4), 256), ((4,), 384), ((3,), 448))
    ]
    local = [
        pltpu.make_async_copy(source, target, r.local.at[i])
        for i, (source, target) in enumerate(
            [(r.x_far, r.x), (r.cot_far, r.cot), (r.out, r.out_far)]
            + [(r.grad.at[BLOCK * i : BLOCK * (i + 1)], r.grad_far.at[BLOCK * i : BLOCK * (i + 1)]) for i in range(4)]
        )
    ]
    local[0].start()
    local[1].start()
    corner = Corner()
    met = greet_partners()
    r.own_qkv[:, 0:512] = r.own_query[...]
    r.own_qkv[:, 640:1152] = r.own_key[...]
    r.own_qkv[:, 1152:1664] = r.own_value[...]
    r.own_small[...] = jnp.zeros_like(r.own_small)
    vectors = [r.own0, r.own1, r.own2, r.own3, r.own4, r.own5, r.own6, r.own7, r.own8]
    for i, vector in enumerate(vectors):
        r.own_small[i : i + 1, 0 : vector.shape[0]] = wide(vector[...]).reshape(1, vector.shape[0])
    r.own_qkv[:, 512:640] = low(r.own_small[...])
    met()

    def column_part(ref, first, last):
        return ref.at[(slice(None),) * (len(ref.shape) - 1) + (slice(first, last),)]

    def row_part(ref, first, last):
        return ref.at[(slice(None),) * (len(ref.shape) - 2) + (slice(first, last),)]

    pieces = [(column_part, r.own_qkv, r.wqkv, *ends) for ends in ((0, 640), (640, 1152), (1152, 1664))]
    pieces += [(column_part, r.own_output, r.wo, 0, 512)]
    pieces += [(column_part, r.own_inner, r.wi, *ends) for ends in ((0, 1024), (1024, 2048))]
    pieces += [(row_part, r.own_outer, r.wu, *ends) for ends in ((0, 32), (32, 64))]
    gathers = [
        (GatherPlaneFirst if i == U1 else Gather)(corner, cut(own, *ends), cut(whole, *ends), r.gather_send.at[i], r.gather_recv.at[i])
        for i, (cut, own, whole, *ends) in enumerate(pieces)
    ]

    got0 = (r.got0_core, r.got0_b, r.got0_a, r.got0_z)
    got1 = (r.got1_core, r.got1_b, r.got1_a, r.got1_z)
    got2 = (r.got2_core, r.got2_b, r.got2_a, r.got2_z)
    far = (r.far_core, r.far_b, r.far_a, r.far_z)
    pieces = [(column_part, r.gu, r.out_outer, got0, 0, 256), (column_part, r.gu, r.out_outer, far, 256, 512)]
    pieces += [(column_part, r.gi, r.out_inner, got1, *ends) for ends in ((0, 1024), (1024, 2048))]
    pieces += [(column_part, r.go, r.out_output, got2, 0, 512)]
    pieces += [(column_part, r.gqkv, r.out_qkv, spare, *ends) for ends in ((0, 768), (768, 1152), (1152, 1664))]
    kinds = [Scatter, ScatterPlaneLast, *[Scatter] * 5, ScatterDirect]
    scatters = [
        kinds[i](
            corner, cut(whole, *ends), cut(out, *ends), *(got if i < 2 else [cut(ref, *ends) for ref in got]),
            r.scatter_send.at[i], r.scatter_recv.at[i],
        )
        for i, (cut, whole, out, got, *ends) in enumerate(pieces)
    ]
    pieces = gathers + scatters

    def out_away():
        local[2].start()

    def grad_away(side):
        for copy in local[3 + 2 * side : 5 + 2 * side]:
            copy.start()

    def cot_here():
        for piece in gathers:
            piece.finish()
        local[1].wait()

    steps = steps_of(r) | {
        X_HERE: local[0].wait,
        COT_HERE: cot_here,
        OUT_AWAY: out_away,
        GRAD_AWAY0: partial(grad_away, 0),
        GRAD_AWAY1: partial(grad_away, 1),
    }
    def go_all(items):
        for item in items:
            go(item)

    def go(item):
        if isinstance(item, tuple):
            pieces[item[0]].phase(item[1])
        elif isinstance(item, list):
            over_pairs(steps[item[0]], lambda n: go_all(item[1 + n]))
        elif item < X_HERE:
            take(steps[item])
        else:
            steps[item]()

    go_all(PLAN)
    for piece in scatters:
        piece.finish()
    for copy in local[2:]:
        copy.wait()


def received(shard):
    return [(lead + tuple(shard[0]), shard[1]) for lead in ((2, 4, 2), (2, 4), (4,), (3,))]


def direct(inputs, lengths, cotangent, weights, vectors, inner_bias):
    tokens = (TOKENS, WIDTH)
    given = dict(x_far=inputs, cot_far=cotangent, lengths=lengths)
    given |= dict(own_query=weights[0], own_key=weights[1], own_value=weights[2])
    given |= dict(own_output=weights[3], own_inner=weights[4], own_outer=weights[5])
    given |= {"own%d" % i: vector for i, vector in enumerate([*vectors, inner_bias])}
    outputs = dict(
        out_far=(tokens, BF),
        grad_far=(tokens, F32),
        out_qkv=(SHARDS["wqkv"], F32),
        out_output=(SHARDS["wo"], F32),
        out_inner=(SHARDS["wi"], F32),
        out_outer=(SHARDS["wu"], F32),
    )
    whole = {name: (LEAD + shard, BF) for name, shard in SHARDS.items()}
    got0, got1, got2 = [received((shard, BF)) for shard in ((64, 256), (16, 2048), (16, 512))]
    scratch = local_scratch() | whole
    scratch |= dict(
        x=(tokens, BF),
        out=(tokens, BF),
        grad=(tokens, F32),
        gu=whole["wu"],
        go=whole["wo"],
        own_qkv=(SHARDS["wqkv"], BF),
        own_small=((16, LANES), F32),
        vec=((8, WIDTH), F32),
        ib=((1, 2048), F32),
        gvec=((8, WIDTH), F32),
        gib=((1, 2048), F32),
        far_core=got0[0],
        far_b=((2, 64, 256), BF),
        far_a=((64, 256), BF),
        far_z=((3, 2, 2, 64, 256), BF),
        got0_core=got0[0], got0_b=got0[1], got0_a=got0[2], got0_z=got0[3],
        got1_core=got1[0], got1_b=got1[1], got1_a=got1[2], got1_z=got1[3],
        got2_core=got2[0], got2_b=got2[1], got2_a=got2[2], got2_z=got2[3],
    )
    sems = dict(gather_send=(8, 10), gather_recv=(8, 10), scatter_send=(8, 7), scatter_recv=(8, 7), local=(7,))
    spaces = dict(lengths=pltpu.SMEM, x_far=pl.ANY, cot_far=pl.ANY, out_far=pl.ANY, grad_far=pl.ANY)
    made = call(
        direct_kernel, given, spaces, outputs, scratch, sems, collective_id=0, has_side_effects=True
    )
    return hand_over(made)


def hand_over(made):
    count = 4
    rows = TOKENS // count

    def body(out, grad, qkv, output, inner, outer, *refs):
        to_out, to_grad, to_q, to_k, to_v, to_output, to_inner, to_outer = refs[:8]
        vectors, (held_out, held_grad, held_qkv, sem) = refs[8:17], refs[17:]
        copies = []

        def copy(source, target):
            copies.append(pltpu.make_async_copy(source, target, sem.at[len(copies)]))
            copies[-1].start()
            return copies[-1]

        small = copy(qkv, held_qkv)
        parts = []
        for i in range(count):
            part = pl.ds(rows * i, rows)
            for source, held, target in ((grad, held_grad, to_grad), (out, held_out, to_out)):
                parts.append((copy(source.at[part], held.at[part]), held.at[part], target.at[part]))
        to_output[...] = output[...]
        to_inner[...] = inner[...]
        to_outer[...] = outer[...]
        small.wait()
        for i, target in enumerate((to_q, to_k, to_v)):
            for first, last in PAIRS:
                start = 3 * first + (last - first) * i
                target[:, first:last] = held_qkv[:, start : start + last - first]
        for i, target in enumerate(vectors):
            target[...] = held_qkv[i, 1536 : 1536 + target.shape[0]]
        back = []
        for into, held, target in parts:
            into.wait()
            back.append(copy(held, target))
        for each in back:
            each.wait()

    given = [made.out_far, made.grad_far, made.out_qkv, made.out_output, made.out_inner, made.out_outer]
    square = jax.ShapeDtypeStruct((16, 512), F32)
    shapes = [jax.ShapeDtypeStruct(part.shape, part.dtype) for part in given]
    vectors = [jax.ShapeDtypeStruct((16,), F32)] * 8 + [jax.ShapeDtypeStruct((64,), F32)]
    far, near = pl.BlockSpec(memory_space=pl.ANY), pl.BlockSpec(memory_space=pltpu.VMEM)
    out, grad, q, k, v, output, inner, outer, *vectors = pl.pallas_call(
        body,
        out_shape=[*shapes[:2], square, square, square, *shapes[3:], *vectors],
        in_specs=[far, far, far, near, near, near],
        out_specs=[far, far, *[near] * 15],
        scratch_shapes=[
            pltpu.VMEM((TOKENS, WIDTH), BF),
            pltpu.VMEM((TOKENS, WIDTH), F32),
            pltpu.VMEM(SHARDS["wqkv"], F32),
            pltpu.SemaphoreType.DMA((1 + 4 * count,)),
        ],
    )(*given)
    return out, grad, [q, k, v, output, inner, outer], vectors[:8], vectors[8]


def alone_kernel(r):
    r.gi, r.gqkv = halves_of(r.turn)
    r.cot, r.dv, r.dk = r.attended, r.attended, r.hidden
    here = pltpu.make_async_copy(r.cot_far, r.cot, r.local.at[0])
    here.start()
    here.wait()
    run_local(r)
    away = [
        pltpu.make_async_copy(source, target, r.local.at[1 + i])
        for i, (source, target) in enumerate(((r.gi, r.gi_far), (r.gqkv, r.gqkv_far)))
    ]
    for copy in away:
        copy.start()
    for copy in away:
        copy.wait()


def through_collectives(inputs, lengths, cotangent, weights, vectors, inner_bias):
    weights, vectors, inner_bias = jax.tree.map(
        lambda own: lax.all_gather(own, AXES, axis=0, tiled=True), (weights, vectors, inner_bias)
    )
    empty = jnp.zeros((WIDTH, LANES), BF)
    weights = [jnp.concatenate([weights[0], empty, *weights[1:3]], axis=1), *weights[3:]]
    whole = {name: weight.reshape(LEAD + SHARDS[name]) for name, weight in zip(SHARDS, weights)}
    given = dict(x=inputs, cot_far=cotangent, lengths=lengths, **whole)
    given |= dict(vec=jnp.stack(vectors).astype(F32), ib=inner_bias.astype(F32)[None])
    tokens = (TOKENS, WIDTH)
    outputs = dict(out=(tokens, BF), grad=(tokens, F32), gvec=((8, WIDTH), F32), gib=((1, 2048), F32))
    outputs |= dict(gqkv_far=(LEAD + SHARDS["wqkv"], BF), gi_far=(LEAD + SHARDS["wi"], BF))
    outputs |= dict(go=(LEAD + SHARDS["wo"], BF), gu=(LEAD + SHARDS["wu"], BF))
    spaces = dict(lengths=pltpu.SMEM, cot_far=pl.ANY, gqkv_far=pl.ANY, gi_far=pl.ANY)
    scratch = local_scratch() | dict(dq=(tokens, BF))
    made = call(alone_kernel, given, spaces, outputs, scratch, dict(local=(3,)))
    qkv, output, inner, outer = [
        part.reshape(-1, part.shape[-1]).astype(F32) for part in (made.gqkv_far, made.go, made.gi_far, made.gu)
    ]
    grads = []
    for i in range(3):
        starts = [(3 * first + (last - first) * i, last - first) for first, last in PAIRS]
        grads.append(jnp.concatenate([qkv[:, start : start + count] for start, count in starts], axis=1))
    grads += [output, inner, outer]
    grads, vectors, inner_bias = jax.tree.map(
        lambda part: lax.psum_scatter(part, AXES, scatter_dimension=0, tiled=True),
        (grads, [made.gvec[i] for i in range(8)], made.gib[0]),
    )
    return made.out, made.grad, grads, vectors, inner_bias


def solution(mesh):
    on_chips = (mesh.shape["dp"], mesh.shape["fsdp"]) == (4, 8)
    way = direct if on_chips else through_collectives

    def shards(
        inputs, seq_lengths, query_weight, key_weight, value_weight, output_weight, query_bias, value_bias,
        output_bias, first_gain, first_shift, inner_weight, inner_bias, outer_weight, outer_bias, final_gain,
        final_shift, cotangent,
    ):
        weights = [query_weight, key_weight, value_weight, output_weight, inner_weight, outer_weight]
        vectors = [query_bias, value_bias, output_bias, first_gain, first_shift]
        vectors += [outer_bias, final_gain, final_shift]
        out, grad, grads, vectors, inner_total = way(
            inputs, seq_lengths, cotangent, weights, vectors, inner_bias
        )
        return (out, grad, *grads[:4], *vectors[:5], grads[4], inner_total, grads[5], *vectors[5:])

    flat, rows = P(AXES), P(AXES, None)
    weights = (*[rows] * 4, *[flat] * 5, rows, flat, rows, *[flat] * 3)
    return jax.shard_map(
        shards,
        mesh=mesh,
        in_specs=(rows, rows, *weights, rows),
        out_specs=(rows, rows, *weights),
        check_vma=False,
    )
```

```python
from functools import partial
import math
import types

import jax
import jax.numpy as jnp
from jax import lax
from jax.experimental import pallas as pl
from jax.experimental.pallas import tpu as pltpu
from jax.sharding import PartitionSpec as P

norm_eps = 1e-05
Q_BIAS, V_BIAS, O_BIAS, GAIN_ONE, SHIFT_ONE, U_BIAS, GAIN_TWO, SHIFT_TWO = range(8)
BLOCK = 256
STARTS, PACKED = (0, 640, 1152), 512
PAIRS = ((0, 256), (256, 384), (384, 512))
LANES = 128
far = -1e30


def nn(left, right):
    return jnp.dot(left, right, preferred_element_type=jnp.float32)


def tn(left, right):
    return lax.dot_general(left, right, (((0,), (0,)), ((), ())), preferred_element_type=jnp.float32)


def nt(left, right):
    return lax.dot_general(left, right, (((1,), (1,)), ((), ())), preferred_element_type=jnp.float32)


def low(values):
    return values.astype(jnp.bfloat16)


def wide(values):
    return values.astype(jnp.float32)


def iota(shape, axis):
    return lax.broadcasted_iota(jnp.int32, shape, axis)


def matrix(ref):
    return ref[...].reshape(-1, ref.shape[-1])


def block_of(i):
    return pl.ds(BLOCK * i if isinstance(i, int) else pl.multiple_of(i * BLOCK, BLOCK), BLOCK)


def lanes_of(first):
    return pl.ds(first if isinstance(first, int) else pl.multiple_of(first, LANES), LANES)


def boundaries(lengths):
    starts, ends, at = [], [], 0
    for s in range(lengths.shape[1]):
        starts.append(at)
        at = at + lengths[0, s]
        ends.append(at)
    before, after = [], []
    for edge in (BLOCK, 2 * BLOCK, 3 * BLOCK):
        tail, head = 0, 0
        for start, end in zip(starts, ends):
            across = (start < edge) & (end > edge)
            tail = tail + jnp.where(across, edge - start, 0)
            head = head + jnp.where(across, end - edge, 0)
        before.append(tail)
        after.append(head)
    return starts, ends, before, after


class Attention:
    def __init__(self, lengths):
        self.starts, self.ends, self.before, self.after = boundaries(lengths)
        self.rows = iota((BLOCK, LANES), 0)
        self.lanes = iota((BLOCK, LANES), 1)
        self.left = self.lanes < 64

    def members(self, block):
        rows, lanes = self.rows + block * BLOCK, lax.rem(self.lanes, 64)
        marks = jnp.zeros((BLOCK, LANES), jnp.float32)
        for s, (start, end) in enumerate(zip(self.starts, self.ends)):
            inside = (rows >= start) & (rows < end) & (lanes == s)
            marks = jnp.where(inside, 1.0, marks)
        return marks

    def merged(self, blocks):
        return [*blocks, *[jnp.where(self.in_head(i), blocks[i + 1], blocks[i]) for i in range(3)]]

    def half(self, side):
        return self.left if side == 0 else ~self.left

    def in_head(self, edge):
        return self.rows < self.after[edge]

    def in_tail(self, edge):
        return self.rows >= BLOCK - self.before[edge]

    def pick(self, parts):
        out = []
        for i in range(4):
            block = parts[i]
            if i < 3:
                block = jnp.where(self.in_tail(i), parts[4 + i], block)
            if i > 0:
                block = jnp.where(self.in_head(i - 1), parts[3 + i], block)
            out.append(block)
        return out

    def gather_sums(self, parts):
        out = []
        for i in range(4):
            block = parts[i]
            if i < 3:
                block = block + jnp.where(self.in_head(i), 0.0, parts[4 + i])
            if i > 0:
                block = block + jnp.where(self.in_head(i - 1), parts[3 + i], 0.0)
            out.append(block)
        return out

    def units(self, blocks):
        out = []
        for i in range(4):
            block = blocks[i]
            if i < 3:
                block = jnp.where(self.in_tail(i), 0.0, block)
            if i > 0:
                block = jnp.where(self.in_head(i - 1), 0.0, block)
            out.append(block)
        for i in range(3):
            tail = jnp.where(self.in_tail(i), blocks[i], 0.0)
            out.append(jnp.where(self.in_head(i), blocks[i + 1], tail))
        return out


def square_of(r, part):
    first = STARTS[part]
    return r.wqkv[:, :, :, :, :, first : first + 512].reshape(512, 512)


def mark(r, at):
    for unit, marks in enumerate(at.merged([at.members(i) for i in range(4)])):
        r.marks[unit] = low(marks)


def project(r, at, part):
    dest = (r.q, r.k, r.v)[part]

    def put(unit, product):
        marks = wide(r.marks[unit])
        beside = (marks, jnp.where(lax.rem(at.lanes, 64) < 8, far - far * marks, 0.0), 1.0)[part]
        for pair in range(4):
            both = product[:, LANES * pair : LANES * (pair + 1)]
            for side in range(2):
                dest[2 * pair + side, unit] = low(jnp.where(at.half(side), both, beside))

    head = [iota((BLOCK, 512), 0) < count for count in at.after]
    for i in range(4):
        product = nn(r.x[block_of(i)], square_of(r, part))
        if part == 0:
            product = (product + r.vec[Q_BIAS : Q_BIAS + 1]) * 0.125
        elif part == 2:
            product = product + r.vec[V_BIAS : V_BIAS + 1]
        put(i, product)
        if i > 0:
            put(3 + i, jnp.where(head[i - 1], product, before))
        before = product


def attend(r, at, pair):
    outs = []
    for side in range(2):
        head = 2 * pair + side
        parts = []
        for unit in range(7):
            scores = nt(r.k[head, unit], r.q[head, unit])
            top = jnp.max(scores, axis=0, keepdims=True)
            grown = low(jnp.exp(scores - top))
            r.e[head, unit] = grown
            parts.append(tn(grown, r.v[head, unit]))
        outs.append(at.pick(parts))
    columns = lanes_of(pair * LANES)
    for i in range(4):
        even, odd = outs[0][i], outs[1][i]
        share = 1.0 / pltpu.roll(jnp.where(at.left, odd, even), 64, 1)
        mixed = jnp.where(at.left, even, odd) * share
        r.combined[BLOCK * i : BLOCK * (i + 1), columns] = low(mixed)
        r.share[BLOCK * i : BLOCK * (i + 1), columns] = share


def normal(values):
    center = values - jnp.mean(values, axis=-1, keepdims=True)
    spread = jnp.mean(center * center, axis=-1, keepdims=True)
    scale = lax.rsqrt(spread + norm_eps)
    return center * scale, scale


def normal_back(grad, normed, scale):
    return scale * (
        grad
        - jnp.mean(grad, axis=-1, keepdims=True)
        - normed * jnp.mean(grad * normed, axis=-1, keepdims=True)
    )


def sums(values):
    return jnp.sum(values, axis=0, keepdims=True)


def attended_rows(r, i):
    rows = block_of(i)
    attended = nn(r.combined[rows], matrix(r.wo)) + r.vec[O_BIAS : O_BIAS + 1]
    normed, scale = normal(wide(r.x[rows]) + attended)
    r.normed[rows] = normed
    r.scale[rows] = jnp.broadcast_to(scale, (BLOCK, LANES))
    r.hidden[rows] = low(normed * r.vec[GAIN_ONE : GAIN_ONE + 1] + r.vec[SHIFT_ONE : SHIFT_ONE + 1])


def active_rows(r, side, i):
    rows = block_of(i)
    hidden_low = r.hidden[rows]
    slope = math.sqrt(2 / math.pi)
    for part in (2 * side, 2 * side + 1):
        columns = slice(512 * part, 512 * (part + 1))
        inner = nn(hidden_low, r.wi[:, :, :, :, :, columns].reshape(512, 512)) + r.ib[:, columns]
        square = inner * inner
        half = 0.5 * jnp.tanh(inner * (slope + (slope * 0.044715) * square)) + 0.5
        active = inner * half
        r.active[rows, columns] = low(active)
        turn = half + active * (1.0 - half) * (2 * slope + (6 * slope * 0.044715) * square)
        r.turn[rows, columns] = low(turn)


def outer_half(r, rows, side):
    columns = slice(256 * side, 256 * (side + 1))
    return nn(r.active[rows], r.wu[:, :, :, :, :, columns].reshape(2048, 256))


def first_half_rows(r, i):
    rows = block_of(i)
    r.grad[rows, 0:256] = outer_half(r, rows, 0)


def final_rows(r, i):
    rows = block_of(i)
    hidden = r.normed[rows] * r.vec[GAIN_ONE : GAIN_ONE + 1] + r.vec[SHIFT_ONE : SHIFT_ONE + 1]
    outer = jnp.concatenate([r.grad[rows, 0:256], outer_half(r, rows, 1)], axis=1) + r.vec[U_BIAS : U_BIAS + 1]
    normed, scale = normal(outer + hidden + wide(r.x[rows]))
    gain = r.vec[GAIN_TWO : GAIN_TWO + 1]
    r.out[rows] = low(normed * gain + r.vec[SHIFT_TWO : SHIFT_TWO + 1])
    grad = wide(r.cot[rows])
    r.gvec[GAIN_TWO : GAIN_TWO + 1] += sums(grad * normed)
    r.gvec[SHIFT_TWO : SHIFT_TWO + 1] += sums(grad)
    grad_two = normal_back(grad * gain, normed, scale)
    r.grad[rows] = grad_two
    grad_outer = low(grad_two)
    r.grad_outer[rows] = grad_outer
    r.gvec[U_BIAS : U_BIAS + 1] += sums(wide(grad_outer))


def rows_of(ref, quarter):
    return ref[quarter // 2, quarter % 2].reshape(-1, ref.shape[-1])


def outer_weight_grad(r, side):
    for quarter in range(4):
        rows, columns = slice(512 * quarter, 512 * (quarter + 1)), slice(256 * side, 256 * (side + 1))
        product = low(tn(r.active[:, rows], r.grad_outer[:, columns]))
        r.gu[quarter // 2, quarter % 2, :, :, :, columns] = product.reshape(4, 2, -1, 256)


def inner_rows(r, i):
    rows = block_of(i)
    grad_outer = r.grad_outer[rows]
    for part in range(4):
        columns = slice(512 * part, 512 * (part + 1))
        grad_inner = low(nt(grad_outer, rows_of(r.wu, part)) * wide(r.turn[rows, columns]))
        r.active[rows, columns] = grad_inner
        r.gib[:, columns] += sums(wide(grad_inner))


def inner_weight_grad(r, side):
    for half in range(2):
        for part in (2 * side, 2 * side + 1):
            columns = slice(512 * part, 512 * (part + 1))
            product = low(tn(r.hidden[:, 256 * half : 256 * (half + 1)], r.active[:, columns]))
            r.gi[half, :, :, :, :, columns] = product.reshape(2, 4, 2, -1, 512)


def hidden_rows(r, i):
    rows = block_of(i)
    grad_two = r.grad[rows]
    grad_hidden = nt(r.active[rows], matrix(r.wi)) + grad_two
    normed = r.normed[rows]
    r.gvec[GAIN_ONE : GAIN_ONE + 1] += sums(grad_hidden * normed)
    r.gvec[SHIFT_ONE : SHIFT_ONE + 1] += sums(grad_hidden)
    gain = r.vec[GAIN_ONE : GAIN_ONE + 1]
    grad_one = normal_back(grad_hidden * gain, normed, r.scale[rows, 0:1])
    r.grad[rows] = grad_two + grad_one
    attended = low(grad_one)
    r.attended[rows] = attended
    r.gvec[O_BIAS : O_BIAS + 1] += sums(wide(attended))
    r.grad_outer[rows] = low(nt(attended, matrix(r.wo)))


def output_weight_grad(r):
    for half in range(2):
        product = low(tn(r.combined[:, 256 * half : 256 * (half + 1)], r.attended[...]))
        r.go[half] = product.reshape(r.go.shape[1:])


def attend_back(r, at, pair):
    columns = lanes_of(pair * LANES)
    ones = low(jnp.where((iota((LANES, LANES), 0) < 64) == (iota((LANES, LANES), 1) < 64), 1.0, 0.0))
    sides = [[], []]
    for i in range(4):
        rows = slice(BLOCK * i, BLOCK * (i + 1))
        grad = wide(r.grad_outer[rows, columns])
        share = r.share[rows, columns]
        product = grad * wide(r.combined[rows, columns])
        high = low(product)
        total = nn(high, ones) + nn(low(product - wide(high)), ones)
        total = pltpu.roll(-(total * share), 64, 1)
        rest = total - wide(low(total))
        lanes = lax.rem(at.lanes, 64)
        beside = jnp.where(lanes == 0, total, jnp.where(lanes == 1, rest, 0.0))
        grad = grad * share
        for side in range(2):
            sides[side].append(jnp.where(at.half(side), grad, beside))
    found = [[], [], []]
    for side in range(2):
        head = 2 * pair + side
        parts = [[], [], []]
        for unit, grad in enumerate(at.units(sides[side])):
            grad = low(grad)
            grown = r.e[head, unit]
            scores = low(wide(grown) * nt(r.v[head, unit], grad))
            parts[0].append(tn(scores, r.k[head, unit]))
            parts[1].append(nn(scores, r.q[head, unit]))
            parts[2].append(nn(grown, grad))
        for which in range(3):
            found[which].append(at.gather_sums(parts[which]))
    for which in range(3):
        total = 0.0
        for i in range(4):
            both = jnp.where(at.left, found[which][0][i], found[which][1][i])
            both = low(both * 0.125 if which == 0 else both)
            (r.dq, r.dk, r.dv)[which][BLOCK * i : BLOCK * (i + 1), columns] = both
            total = total + wide(both)
        if which != 1:
            r.gvec[which // 2 : which // 2 + 1, columns] = sums(total)


def qkv_weight_grad(r, piece):
    first, last = PAIRS[piece]
    for part, grads in enumerate((r.dq, r.dk, r.dv)):
        start = 3 * first + (last - first) * part
        for half in range(2):
            product = low(tn(r.x[:, 256 * half : 256 * (half + 1)], grads[:, first:last]))
            columns = slice(start, start + last - first)
            r.gqkv[half, :, :, :, :, columns] = product.reshape(2, 4, 2, -1, last - first)


def input_rows(r, i):
    rows = block_of(i)
    total = r.grad[rows]
    for part, grads in enumerate((r.dq, r.dk, r.dv)):
        total = total + nt(grads[rows], square_of(r, part))
    r.grad[rows] = total


(
    ZERO, MARK, UNPACK, PROJECT_Q, PROJECT_K, PROJECT_V, ATTEND, ATTENDED, ACTIVE0, ACTIVE1, FINAL0, FINAL, OUTER_GRAD0, OUTER_GRAD1, INNER,
    INNER_GRAD0, INNER_GRAD1, HIDDEN, OUTPUT_GRAD, PACK_EARLY, BACK, QKV_GRAD0, QKV_GRAD1, QKV_GRAD2, PACK_LATE, INPUT,
) = range(26)
LOCAL = [step for step in range(26) if step not in (UNPACK, PACK_EARLY, PACK_LATE)]


def all_rows(rows, r, *given):
    for i in range(4):
        rows(r, *given, i)


def rows_by_two(rows, r):
    def two(i, carried):
        rows(r, 2 * i)
        rows(r, 2 * i + 1)
        return carried

    lax.fori_loop(0, 2, two, 0)


def zero(r):
    r.gvec[...] = jnp.zeros_like(r.gvec)
    r.gib[...] = jnp.zeros_like(r.gib)


def steps_of(r):
    at = Attention(r.lengths)
    steps = {
        ZERO: partial(zero, r),
        MARK: partial(mark, r, at),
        UNPACK: partial(unpack_vectors, r),
        ATTEND: partial(attend, r, at),
        ATTENDED: partial(all_rows, attended_rows, r),
        FINAL0: partial(all_rows, first_half_rows, r),
        FINAL: partial(all_rows, final_rows, r),
        INNER: partial(all_rows, inner_rows, r),
        HIDDEN: partial(rows_by_two, hidden_rows, r),
        OUTPUT_GRAD: partial(output_weight_grad, r),
        PACK_EARLY: partial(pack_sums, r, True),
        BACK: partial(attend_back, r, at),
        PACK_LATE: partial(pack_sums, r, False),
        INPUT: partial(rows_by_two, input_rows, r),
    }
    for i in range(3):
        steps[PROJECT_Q + i] = partial(project, r, at, i)
        steps[QKV_GRAD0 + i] = partial(qkv_weight_grad, r, i)
    for i in range(2):
        steps[ACTIVE0 + i] = partial(all_rows, active_rows, r, i)
        steps[OUTER_GRAD0 + i] = partial(outer_weight_grad, r, i)
        steps[INNER_GRAD0 + i] = partial(inner_weight_grad, r, i)
    return steps


def always():
    return lax.axis_index("dp") >= 0


def take(step):
    pl.when(always())(step)


def over_pairs(step, between):
    def body(pair, carried):
        for n in range(4):
            pl.when(pair == n)(partial(between, n))
        step(pair)
        return carried

    lax.fori_loop(0, 4, body, 0)


def run_local(r):
    steps = steps_of(r)
    for step in LOCAL:
        if step in (ATTEND, BACK):
            over_pairs(steps[step], lambda n: None)
        else:
            take(steps[step])
MESH_ID = pl.DeviceIdType.MESH


def place():
    outer, inner = lax.axis_index("dp"), lax.axis_index("fsdp")
    return outer // 2, outer % 2, inner // 2, inner % 2


def device_at(y, core, z, x):
    return (y * 2 + core, z * 2 + x)


def greet_partners():
    y, core, z, x = place()
    partners = [
        device_at(y, 1 - core, z, x),
        device_at(1 - y, core, z, x),
        device_at(y, core, z, 1 - x),
        device_at(1 - y, core, z, 1 - x),
    ] + [device_at(y, core, (z + step) % 4, x) for step in (1, 2, 3)]
    barrier = pltpu.get_barrier_semaphore()
    for partner in partners:
        pl.semaphore_signal(barrier, inc=1, device_id=partner, device_id_type=MESH_ID)
    return lambda: pl.semaphore_wait(barrier, len(partners))


def remote(source, target, send_sem, recv_sem, to):
    return pltpu.make_async_remote_copy(
        src_ref=source,
        dst_ref=target,
        send_sem=send_sem,
        recv_sem=recv_sem,
        device_id=to,
        device_id_type=MESH_ID,
    )


class Corner:
    def __init__(self):
        y, core, z, x = place()
        self.y, self.core, self.z, self.x = y, core, z, x
        self.ya, self.xa = jnp.where(core == 0, y, 1 - y), jnp.where(core == 0, 1 - x, x)
        self.yb, self.xb = jnp.where(core == 0, 1 - y, y), jnp.where(core == 0, x, 1 - x)
        self.partner_a = device_at(self.ya, core, z, self.xa)
        self.partner_b = device_at(self.yb, core, z, self.xb)
        self.sibling = device_at(y, 1 - core, z, x)
        self.across = device_at(1 - y, core, z, 1 - x)

    def along_z(self, step):
        return device_at(self.y, self.core, (self.z + step) % 4, self.x)


class Gather:
    def __init__(self, corner, own, whole, send_sem, recv_sem):
        self.at, self.own, self.whole = corner, own, whole
        self.send_sem, self.recv_sem = send_sem, recv_sem

    def to_z(self, step):
        at = self.at
        slot = self.whole.at[at.y, at.core, at.z, at.x]
        return remote(
            self.own, slot, self.send_sem.at[step - 1], self.recv_sem.at[step - 1], at.along_z(step)
        )

    def line(self, y, x, number, to):
        line = self.whole.at[y, self.at.core, :, x]
        return remote(line, line, self.send_sem.at[number], self.recv_sem.at[number], to)

    def to_a(self):
        return self.line(self.at.y, self.at.x, 3, self.at.partner_a)

    def to_b(self, part):
        at = self.at
        y, x = ((at.y, at.x), (at.ya, at.xa))[part]
        return self.line(y, x, 4 + part, at.partner_b)

    def to_sibling(self, part):
        at = self.at
        y, x = ((at.y, at.x), (at.ya, at.xa), (at.yb, at.xb), (1 - at.y, 1 - at.x))[part]
        return self.line(y, x, 6 + part, at.sibling)

    def phase(self, number):
        if number == 0:
            for step in (2, 1, 3):
                self.to_z(step).start()
            at = self.at
            self.whole[at.y, at.core, at.z, at.x] = self.own[...]
        elif number == 1:
            for step in (1, 2, 3):
                self.to_z(step).wait_recv()
            self.to_a().start()
            self.to_b(0).start()
            self.to_sibling(0).start()
        elif number == 2:
            self.to_a().wait_recv()
            self.to_b(1).start()
            self.to_sibling(1).start()
        elif number == 3:
            self.to_b(0).wait_recv()
            self.to_sibling(2).start()
            self.to_b(1).wait_recv()
            self.to_sibling(3).start()
        elif number == 4:
            for part in range(4):
                self.to_sibling(part).wait_recv()

    def finish(self):
        for step in (1, 2, 3):
            self.to_z(step).wait_send()
        self.to_a().wait_send()
        for part in range(2):
            self.to_b(part).wait_send()
        for part in range(4):
            self.to_sibling(part).wait_send()


class GatherPlaneFirst(Gather):
    def slot(self, y, x, number, to):
        slot = self.whole.at[y, self.at.core, self.at.z, x]
        return remote(slot, slot, self.send_sem.at[number], self.recv_sem.at[number], to)

    def to_a(self):
        return self.slot(self.at.y, self.at.x, 3, self.at.partner_a)

    def to_b(self, part):
        at = self.at
        y, x = ((at.y, at.x), (at.ya, at.xa))[part]
        return self.slot(y, x, 4 + part, at.partner_b)

    def plane(self, z, number, to):
        plane = self.whole.at[:, self.at.core, z]
        return remote(plane, plane, self.send_sem.at[number], self.recv_sem.at[number], to)

    def to_z(self, step):
        return self.plane(self.at.z, step - 1, self.at.along_z(step))

    def to_sibling(self, part):
        return self.plane((self.at.z + part) % 4, 6 + part, self.at.sibling)

    def phase(self, number):
        at = self.at
        if number == 0:
            self.whole[at.y, at.core, at.z, at.x] = self.own[...]
            self.to_a().start()
            self.to_b(0).start()
        elif number == 1:
            self.to_a().wait_recv()
            self.to_b(1).start()
        elif number == 2:
            self.to_b(0).wait_recv()
            self.to_b(1).wait_recv()
            for step in (2, 1, 3):
                self.to_z(step).start()
            self.to_sibling(0).start()
        elif number == 3:
            for step in (1, 3, 2):
                self.to_z(step).wait_recv()
                self.to_sibling(4 - step).start()
        elif number == 4:
            for part in range(4):
                self.to_sibling(part).wait_recv()


class Scatter:
    def __init__(self, corner, whole, out, got_core, got_b, got_a, got_z, send_sem, recv_sem):
        self.at, self.whole, self.out = corner, whole, out
        self.got_core, self.got_b, self.got_a, self.got_z = got_core, got_b, got_a, got_z
        self.send_sem, self.recv_sem = send_sem, recv_sem

    def sems(self, number):
        return self.send_sem.at[number], self.recv_sem.at[number]

    def to_sibling(self):
        return remote(
            self.whole.at[:, 1 - self.at.core], self.got_core, *self.sems(0), self.at.sibling
        )

    def to_b(self, part):
        at = self.at
        y, x = ((at.yb, at.xb), (1 - at.y, 1 - at.x))[part]
        return remote(
            self.whole.at[y, at.core, :, x], self.got_b.at[part], *self.sems(1 + part), at.partner_b
        )

    def to_a(self):
        at = self.at
        return remote(
            self.whole.at[at.ya, at.core, :, at.xa], self.got_a, *self.sems(3), at.partner_a
        )

    def to_z(self, step):
        at = self.at
        return remote(
            self.whole.at[at.y, at.core, (at.z + step) % 4, at.x],
            self.got_z.at[step - 1],
            *self.sems(3 + step),
            at.along_z(step),
        )

    def add_line(self, y, x, other):
        core = self.at.core
        for z in range(4):
            total = self.whole[y, core, z, x].astype(jnp.float32) + other(z).astype(jnp.float32)
            self.whole[y, core, z, x] = total.astype(self.whole.dtype)

    def add_core(self, y, x):
        self.add_line(y, x, lambda z: self.got_core[y, z, x])

    def phase(self, number):
        at = self.at
        if number == 0:
            self.to_sibling().start()
        elif number == 1:
            self.to_sibling().wait_recv()
            self.add_core(at.yb, at.xb)
            self.to_b(0).start()
            self.add_core(1 - at.y, 1 - at.x)
            self.to_b(1).start()
            self.add_core(at.ya, at.xa)
            self.add_core(at.y, at.x)
        elif number == 2:
            self.to_b(1).wait_recv()
            self.add_line(at.ya, at.xa, lambda z: self.got_b[1, z])
            self.to_a().start()
            self.to_b(0).wait_recv()
            self.add_line(at.y, at.x, lambda z: self.got_b[0, z])
        elif number == 3:
            self.to_a().wait_recv()
            self.add_line(at.y, at.x, lambda z: self.got_a[z])
            for step in (2, 1, 3):
                self.to_z(step).start()
        elif number == 4:
            total = self.whole[at.y, at.core, at.z, at.x].astype(jnp.float32)
            for step in (1, 2, 3):
                self.to_z(step).wait_recv()
                total = total + self.got_z[step - 1].astype(jnp.float32)
            self.out[...] = total

    def finish(self):
        self.to_sibling().wait_send()
        for part in range(2):
            self.to_b(part).wait_send()
        self.to_a().wait_send()
        for step in (1, 2, 3):
            self.to_z(step).wait_send()


class ScatterDirect(Scatter):
    def phase(self, number):
        at = self.at
        if number == 1:
            self.to_sibling().wait_recv()
            self.add_core(1 - at.y, 1 - at.x)
            self.to_b(1).start()
            self.add_core(at.yb, at.xb)
            self.to_b(0).start()
            self.add_core(at.ya, at.xa)
            self.to_a().start()
            self.add_core(at.y, at.x)
        elif number == 2:
            self.to_a().wait_recv()
            for part in range(2):
                self.to_b(part).wait_recv()
            for z in range(4):
                line = self.whole[at.y, at.core, z, at.x].astype(jnp.float32)
                for got in (self.got_a[z], self.got_b[0, z], self.got_b[1, z]):
                    line = line + got.astype(jnp.float32)
                self.whole[at.y, at.core, z, at.x] = line.astype(self.whole.dtype)
            for step in (2, 1, 3):
                self.to_z(step).start()
        elif number != 3:
            super().phase(number)

    def to_b(self, part):
        at = self.at
        y, x, to = ((at.yb, at.xb, at.partner_b), (1 - at.y, 1 - at.x, at.across))[part]
        return remote(self.whole.at[y, at.core, :, x], self.got_b.at[part], *self.sems(1 + part), to)


class ScatterPlaneLast(Scatter):
    def to_z(self, step):
        at = self.at
        return remote(
            self.whole.at[:, at.core, (at.z + step) % 4],
            self.got_z.at[step - 1],
            *self.sems(3 + step),
            at.along_z(step),
        )

    def to_b(self, part):
        at = self.at
        y, x = ((at.yb, at.xb), (1 - at.y, 1 - at.x))[part]
        source = self.whole.at[y, at.core, at.z, x]
        return remote(source, self.got_b.at[part], *self.sems(1 + part), at.partner_b)

    def to_a(self):
        at = self.at
        source = self.whole.at[at.ya, at.core, at.z, at.xa]
        return remote(source, self.got_a, *self.sems(3), at.partner_a)

    def add(self, y, z, x, *others):
        core = self.at.core
        total = self.whole[y, core, z, x].astype(jnp.float32)
        for other in others:
            total = total + other.astype(jnp.float32)
        self.whole[y, core, z, x] = total.astype(self.whole.dtype)

    def phase(self, number):
        at = self.at
        places = [(y, x) for y in range(2) for x in range(2)]
        if number == 0:
            self.to_sibling().start()
        elif number == 1:
            self.to_sibling().wait_recv()
            for step in (2, 1, 3, 0):
                z = (at.z + step) % 4
                for y, x in places:
                    self.add(y, z, x, self.got_core[y, z, x])
                if step:
                    self.to_z(step).start()
        elif number == 2:
            for step in (1, 2, 3):
                self.to_z(step).wait_recv()
            for y, x in places:
                self.add(y, at.z, x, *[self.got_z[step, y, x] for step in range(3)])
            for part in range(2):
                self.to_b(part).start()
        elif number == 3:
            self.to_b(1).wait_recv()
            self.add(at.ya, at.z, at.xa, self.got_b[1])
            self.to_a().start()
            self.to_b(0).wait_recv()
        elif number == 4:
            self.to_a().wait_recv()
            total = self.whole[at.y, at.core, at.z, at.x].astype(jnp.float32)
            self.out[...] = total + self.got_b[0].astype(jnp.float32) + self.got_a[...].astype(jnp.float32)
LEAD = (2, 2, 4, 2)
TOKENS, WIDTH = 1024, 512
BF, F32 = jnp.bfloat16, jnp.float32
AXES = ("dp", "fsdp")
SHARDS = dict(wqkv=(16, 1664), wo=(16, 512), wi=(16, 2048), wu=(64, 512))


def local_scratch():
    units, tokens = (8, 7, BLOCK, LANES), (TOKENS, WIDTH)
    return dict(
        q=(units, BF),
        k=(units, BF),
        v=(units, BF),
        e=((8, 7, BLOCK, BLOCK), BF),
        marks=((7, BLOCK, LANES), BF),
        share=(tokens, F32),
        combined=(tokens, BF),
        normed=(tokens, F32),
        scale=((TOKENS, LANES), F32),
        hidden=(tokens, BF),
        active=((TOKENS, 2048), BF),
        turn=((TOKENS, 2048), BF),
        grad_outer=(tokens, BF),
        attended=(tokens, BF),
    )


def call(kernel, inputs, spaces, outputs, scratch, sems, **params):
    names = [*inputs, *outputs, *scratch, *sems]

    def body(*refs):
        kernel(types.SimpleNamespace(**dict(zip(names, refs, strict=True))))

    made = pl.pallas_call(
        body,
        out_shape=[jax.ShapeDtypeStruct(*given) for given in outputs.values()],
        in_specs=[pl.BlockSpec(memory_space=spaces.get(name, pltpu.VMEM)) for name in inputs],
        out_specs=[pl.BlockSpec(memory_space=spaces.get(name, pltpu.VMEM)) for name in outputs],
        scratch_shapes=[pltpu.VMEM(*given) for given in scratch.values()]
        + [pltpu.SemaphoreType.DMA(shape) for shape in sems.values()],
        compiler_params=pltpu.CompilerParams(vmem_limit_bytes=63 << 20, **params),
    )(*inputs.values())
    return types.SimpleNamespace(**dict(zip(outputs, made, strict=True)))


def chosen_lanes(count):
    shape = (LANES, 32 * count)
    return low(jnp.where(iota(shape, 0) == lax.rem(iota(shape, 1), count), 1.0, 0.0))


def of_owner(rows, count):
    shape = (rows, 32 * count)
    return lax.rem(iota(shape, 0), 32) == lax.div(iota(shape, 1), count)


def chosen_rows():
    row, column = iota((288, 512), 0), iota((288, 512), 1)
    return low(jnp.where(column == lax.rem(row, 32) * 16 + lax.div(row, 32), 1.0, 0.0))


def unpack_vectors(r):
    packed = r.wqkv[:, :, :, :, :, PACKED : PACKED + LANES].reshape(512, LANES)
    packed = low(nn(chosen_rows(), packed))
    vectors = jnp.where(of_owner(256, 16), nn(packed[:256], chosen_lanes(16)), 0.0)
    for kind in range(8):
        r.vec[kind : kind + 1] = sums(vectors[32 * kind : 32 * (kind + 1)])
    r.ib[...] = sums(jnp.where(of_owner(32, 64), nn(packed[256:], chosen_lanes(64)), 0.0))


def pack_sums(r, early):
    def placed(values, count):
        alone = jnp.where(of_owner(32, count), values, 0.0)
        high = low(alone)
        lanes = chosen_lanes(count)
        return nt(high, lanes) + nt(low(alone - wide(high)), lanes)

    rows = [placed(r.gvec[kind : kind + 1], 16) for kind in (range(2, 8) if early else range(2))]
    rows += [placed(r.gib[...], 64)] if early else []
    chosen = chosen_rows()[64:] if early else chosen_rows()[:64]
    packed = low(tn(chosen, low(jnp.concatenate(rows, axis=0)))).reshape(*LEAD, 16, LANES)
    if not early:
        packed = packed + r.gqkv[:, :, :, :, :, 1536:1664]
    r.gqkv[:, :, :, :, :, 1536:1664] = packed


Q, K, V, O, I0, I1, U0, U1 = range(8)
SU0, SU1, SI0, SI1, SO, SA, SB, SC = range(8, 16)
X_HERE, COT_HERE, OUT_AWAY, GRAD_AWAY0, GRAD_AWAY1 = range(100, 105)
PLAN = [
    (Q, 0), (U1, 0), (K, 0), (V, 0), ZERO, MARK, X_HERE, (U1, 1), (O, 0), (I1, 0), (Q, 1), (K, 1), (V, 1), (I0, 0),
    (U0, 0), (Q, 2), (K, 2), (O, 1), (V, 2), (Q, 3), (I1, 1), (Q, 4), (K, 3), UNPACK, (U1, 2), (V, 3), (I0, 1),
    (K, 4), PROJECT_Q, (O, 2), (U0, 1), (V, 4), PROJECT_K, PROJECT_V,
    [ATTEND, [], [(I0, 2)], [(O, 3), (I1, 2)], [(U0, 2), (O, 4)]], (I0, 3), ATTENDED, (I1, 3), (I0, 4), ACTIVE0,
    (I1, 4), (U0, 3), (U1, 3), ACTIVE1, (U0, 4), FINAL0, (U1, 4), COT_HERE, FINAL, OUT_AWAY, OUTER_GRAD0, OUTER_GRAD1,
    INNER, (SU0, 0), INNER_GRAD0, INNER_GRAD1, (SU1, 0), (SI1, 0), (SU0, 1), HIDDEN, (SI1, 1), OUTPUT_GRAD, (SU1, 1),
    (SO, 0), PACK_EARLY, (SU0, 2), (SI0, 0),
    [BACK, [], [(SO, 1), (SI0, 1)], [QKV_GRAD0, (SU0, 3), (SI1, 2), (SA, 0)], [(SO, 2), (SA, 1), QKV_GRAD1, (SI0, 2), (SI1, 3), (SB, 0)]],
    (SB, 1), QKV_GRAD2, PACK_LATE, (SC, 0), (SU0, 4), (SO, 3), (SA, 2), (SI0, 3), (SC, 1), INPUT, GRAD_AWAY0,
    GRAD_AWAY1, (SB, 2), (SO, 4), (SU1, 2), (SA, 3), (SB, 3), (SC, 2), (SC, 3), (SU1, 3), (SU1, 4), (SI1, 4),
    (SI0, 4), (SB, 4), (SA, 4), (SC, 4),
]


def halves_of(buffer):
    first, second = [buffer.at[i : i + 512].reshape(*LEAD, 16, 2048) for i in (0, 512)]
    return first, second.at[:, :, :, :, :, 0:1664]


def direct_kernel(r):
    r.gi, r.gqkv = halves_of(r.turn)
    r.dq = r.wu.at[0].reshape(TOKENS, 512)
    r.dk = r.wu.at[1].reshape(TOKENS, 512)
    r.dv = r.attended
    r.cot = r.attended
    spare = [
        r.active.at[first : first + 16 * math.prod(lead)].reshape(*lead, 16, 2048)
        for lead, first in (((2, 4, 2), 0), ((2, 4), 256), ((4,), 384), ((3,), 448))
    ]
    local = [
        pltpu.make_async_copy(source, target, r.local.at[i])
        for i, (source, target) in enumerate(
            [(r.x_far, r.x), (r.cot_far, r.cot), (r.out, r.out_far)]
            + [(r.grad.at[BLOCK * i : BLOCK * (i + 1)], r.grad_far.at[BLOCK * i : BLOCK * (i + 1)]) for i in range(4)]
        )
    ]
    own = [
        pltpu.make_async_copy(source, target, r.local.at[7 + i])
        for i, (source, target) in enumerate(
            (
                (r.query_far, r.own_qkv.at[:, 0:512]),
                (r.key_far, r.own_qkv.at[:, 640:1152]),
                (r.value_far, r.own_qkv.at[:, 1152:1664]),
                (r.output_far, r.own_output),
                (r.inner_far, r.own_inner),
                (r.outer_far, r.own_outer),
            )
        )
    ]
    corner = Corner()
    met = greet_partners()
    for copy in (*own, *local[:2]):
        copy.start()
    r.own_small[...] = jnp.zeros_like(r.own_small)
    vectors = [r.own0, r.own1, r.own2, r.own3, r.own4, r.own5, r.own6, r.own7, r.own8]
    for i, vector in enumerate(vectors):
        r.own_small[i : i + 1, 0 : vector.shape[0]] = wide(vector[...]).reshape(1, vector.shape[0])
    r.own_qkv[:, 512:640] = low(r.own_small[...])
    for copy in own:
        copy.wait()
    met()

    def column_part(ref, first, last):
        return ref.at[(slice(None),) * (len(ref.shape) - 1) + (slice(first, last),)]

    pieces = [(column_part, r.own_qkv, r.wqkv, *ends) for ends in ((0, 640), (640, 1152), (1152, 1664))]
    pieces += [(column_part, r.own_output, r.wo, 0, 512)]
    pieces += [(column_part, r.own_inner, r.wi, *ends) for ends in ((0, 1024), (1024, 2048))]
    pieces += [(column_part, r.own_outer, r.wu, *ends) for ends in ((0, 256), (256, 512))]
    gathers = [
        (GatherPlaneFirst if i == U1 else Gather)(corner, cut(own, *ends), cut(whole, *ends), r.gather_send.at[i], r.gather_recv.at[i])
        for i, (cut, own, whole, *ends) in enumerate(pieces)
    ]

    got0 = (r.got0_core, r.got0_b, r.got0_a, r.got0_z)
    got1 = (r.got1_core, r.got1_b, r.got1_a, r.got1_z)
    got2 = (r.got2_core, r.got2_b, r.got2_a, r.got2_z)
    far = (r.far_core, r.far_b, r.far_a, r.far_z)
    pieces = [(column_part, r.gu, r.out_outer, got0, 0, 256), (column_part, r.gu, r.out_outer, far, 256, 512)]
    pieces += [(column_part, r.gi, r.out_inner, got1, *ends) for ends in ((0, 1024), (1024, 2048))]
    pieces += [(column_part, r.go, r.out_output, got2, 0, 512)]
    pieces += [(column_part, r.gqkv, r.out_qkv, spare, *ends) for ends in ((0, 768), (768, 1152), (1152, 1664))]
    kinds = [Scatter, ScatterPlaneLast, *[Scatter] * 5, ScatterDirect]
    scatters = [
        kinds[i](
            corner, cut(whole, *ends), cut(out, *ends), *(got if i < 2 else [cut(ref, *ends) for ref in got]),
            r.scatter_send.at[i], r.scatter_recv.at[i],
        )
        for i, (cut, whole, out, got, *ends) in enumerate(pieces)
    ]
    pieces = gathers + scatters

    def out_away():
        local[2].start()

    def grad_away(side):
        for copy in local[3 + 2 * side : 5 + 2 * side]:
            copy.start()

    def cot_here():
        for piece in gathers:
            piece.finish()
        local[1].wait()

    steps = steps_of(r) | {
        X_HERE: local[0].wait,
        COT_HERE: cot_here,
        OUT_AWAY: out_away,
        GRAD_AWAY0: partial(grad_away, 0),
        GRAD_AWAY1: partial(grad_away, 1),
    }
    def go_all(items):
        for item in items:
            go(item)

    def go(item):
        if isinstance(item, tuple):
            pieces[item[0]].phase(item[1])
        elif isinstance(item, list):
            over_pairs(steps[item[0]], lambda n: go_all(item[1 + n]))
        elif item < X_HERE:
            take(steps[item])
        else:
            steps[item]()

    go_all(PLAN)
    for piece in scatters:
        piece.finish()
    for copy in local[2:]:
        copy.wait()


def received(shard):
    return [(lead + tuple(shard[0]), shard[1]) for lead in ((2, 4, 2), (2, 4), (4,), (3,))]


def direct(inputs, lengths, cotangent, weights, vectors, inner_bias):
    tokens = (TOKENS, WIDTH)
    given = dict(x_far=inputs, cot_far=cotangent, lengths=lengths)
    given |= dict(query_far=weights[0], key_far=weights[1], value_far=weights[2])
    given |= dict(output_far=weights[3], inner_far=weights[4], outer_far=weights[5])
    given |= {"own%d" % i: vector for i, vector in enumerate([*vectors, inner_bias])}
    outputs = dict(
        out_far=(tokens, BF),
        grad_far=(tokens, F32),
        out_qkv=(SHARDS["wqkv"], F32),
        out_output=(SHARDS["wo"], F32),
        out_inner=(SHARDS["wi"], F32),
        out_outer=(SHARDS["wu"], F32),
    )
    whole = {name: (LEAD + shard, BF) for name, shard in SHARDS.items()}
    got0, got1, got2 = [received((shard, BF)) for shard in ((64, 256), (16, 2048), (16, 512))]
    scratch = local_scratch() | whole
    scratch |= dict(
        x=(tokens, BF),
        out=(tokens, BF),
        grad=(tokens, F32),
        gu=whole["wu"],
        go=whole["wo"],
        own_qkv=(SHARDS["wqkv"], BF),
        own_output=(SHARDS["wo"], BF),
        own_inner=(SHARDS["wi"], BF),
        own_outer=(SHARDS["wu"], BF),
        own_small=((16, LANES), F32),
        vec=((8, WIDTH), F32),
        ib=((1, 2048), F32),
        gvec=((8, WIDTH), F32),
        gib=((1, 2048), F32),
        far_core=got0[0],
        far_b=((2, 64, 256), BF),
        far_a=((64, 256), BF),
        far_z=((3, 2, 2, 64, 256), BF),
        got0_core=got0[0], got0_b=got0[1], got0_a=got0[2], got0_z=got0[3],
        got1_core=got1[0], got1_b=got1[1], got1_a=got1[2], got1_z=got1[3],
        got2_core=got2[0], got2_b=got2[1], got2_a=got2[2], got2_z=got2[3],
    )
    sems = dict(gather_send=(8, 10), gather_recv=(8, 10), scatter_send=(8, 7), scatter_recv=(8, 7), local=(13,))
    spaces = {name: pl.ANY for name in (*given, *outputs) if name.endswith("_far")} | dict(lengths=pltpu.SMEM)
    made = call(
        direct_kernel, given, spaces, outputs, scratch, sems, collective_id=0, has_side_effects=True
    )
    return hand_over(made)


def hand_over(made):
    count = 4
    rows = TOKENS // count

    def body(out, grad, qkv, output, inner, outer, *refs):
        to_out, to_grad, to_q, to_k, to_v, to_output, to_inner, to_outer = refs[:8]
        vectors, (held_out, held_grad, held_qkv, sem) = refs[8:17], refs[17:]
        copies = []

        def copy(source, target):
            copies.append(pltpu.make_async_copy(source, target, sem.at[len(copies)]))
            copies[-1].start()
            return copies[-1]

        small = copy(qkv, held_qkv)
        near_ones = [copy(output, to_output), copy(inner, to_inner), copy(outer, to_outer)]
        parts = []
        for i in range(count):
            part = pl.ds(rows * i, rows)
            for source, held, target in ((grad, held_grad, to_grad), (out, held_out, to_out)):
                parts.append((copy(source.at[part], held.at[part]), held.at[part], target.at[part]))
        small.wait()
        for i, target in enumerate((to_q, to_k, to_v)):
            for first, last in PAIRS:
                start = 3 * first + (last - first) * i
                target[:, first:last] = held_qkv[:, start : start + last - first]
        for i, target in enumerate(vectors):
            target[...] = held_qkv[i, 1536 : 1536 + target.shape[0]]
        back = near_ones
        for into, held, target in parts:
            into.wait()
            back.append(copy(held, target))
        for each in back:
            each.wait()

    given = [made.out_far, made.grad_far, made.out_qkv, made.out_output, made.out_inner, made.out_outer]
    square = jax.ShapeDtypeStruct((16, 512), F32)
    shapes = [jax.ShapeDtypeStruct(part.shape, part.dtype) for part in given]
    vectors = [jax.ShapeDtypeStruct((16,), F32)] * 8 + [jax.ShapeDtypeStruct((64,), F32)]
    far, near = pl.BlockSpec(memory_space=pl.ANY), pl.BlockSpec(memory_space=pltpu.VMEM)
    out, grad, q, k, v, output, inner, outer, *vectors = pl.pallas_call(
        body,
        out_shape=[*shapes[:2], square, square, square, *shapes[3:], *vectors],
        in_specs=[far] * 6,
        out_specs=[far, far, *[near] * 15],
        scratch_shapes=[
            pltpu.VMEM((TOKENS, WIDTH), BF),
            pltpu.VMEM((TOKENS, WIDTH), F32),
            pltpu.VMEM(SHARDS["wqkv"], F32),
            pltpu.SemaphoreType.DMA((4 + 4 * count,)),
        ],
    )(*given)
    return out, grad, [q, k, v, output, inner, outer], vectors[:8], vectors[8]


def alone_kernel(r):
    r.gi, r.gqkv = halves_of(r.turn)
    r.cot, r.dv, r.dk = r.attended, r.attended, r.hidden
    here = pltpu.make_async_copy(r.cot_far, r.cot, r.local.at[0])
    here.start()
    here.wait()
    run_local(r)
    away = [
        pltpu.make_async_copy(source, target, r.local.at[1 + i])
        for i, (source, target) in enumerate(((r.gi, r.gi_far), (r.gqkv, r.gqkv_far)))
    ]
    for copy in away:
        copy.start()
    for copy in away:
        copy.wait()


def through_collectives(inputs, lengths, cotangent, weights, vectors, inner_bias):
    weights, vectors, inner_bias = jax.tree.map(
        lambda own: lax.all_gather(own, AXES, axis=0, tiled=True), (weights, vectors, inner_bias)
    )
    empty = jnp.zeros((WIDTH, LANES), BF)
    weights = [jnp.concatenate([weights[0], empty, *weights[1:3]], axis=1), *weights[3:]]
    whole = {name: weight.reshape(LEAD + SHARDS[name]) for name, weight in zip(SHARDS, weights)}
    given = dict(x=inputs, cot_far=cotangent, lengths=lengths, **whole)
    given |= dict(vec=jnp.stack(vectors).astype(F32), ib=inner_bias.astype(F32)[None])
    tokens = (TOKENS, WIDTH)
    outputs = dict(out=(tokens, BF), grad=(tokens, F32), gvec=((8, WIDTH), F32), gib=((1, 2048), F32))
    outputs |= dict(gqkv_far=(LEAD + SHARDS["wqkv"], BF), gi_far=(LEAD + SHARDS["wi"], BF))
    outputs |= dict(go=(LEAD + SHARDS["wo"], BF), gu=(LEAD + SHARDS["wu"], BF))
    spaces = dict(lengths=pltpu.SMEM, cot_far=pl.ANY, gqkv_far=pl.ANY, gi_far=pl.ANY)
    scratch = local_scratch() | dict(dq=(tokens, BF))
    made = call(alone_kernel, given, spaces, outputs, scratch, dict(local=(3,)))
    qkv, output, inner, outer = [
        part.reshape(-1, part.shape[-1]).astype(F32) for part in (made.gqkv_far, made.go, made.gi_far, made.gu)
    ]
    grads = []
    for i in range(3):
        starts = [(3 * first + (last - first) * i, last - first) for first, last in PAIRS]
        grads.append(jnp.concatenate([qkv[:, start : start + count] for start, count in starts], axis=1))
    grads += [output, inner, outer]
    grads, vectors, inner_bias = jax.tree.map(
        lambda part: lax.psum_scatter(part, AXES, scatter_dimension=0, tiled=True),
        (grads, [made.gvec[i] for i in range(8)], made.gib[0]),
    )
    return made.out, made.grad, grads, vectors, inner_bias


def solution(mesh):
    on_chips = (mesh.shape["dp"], mesh.shape["fsdp"]) == (4, 8)
    way = direct if on_chips else through_collectives

    def shards(
        inputs, seq_lengths, query_weight, key_weight, value_weight, output_weight, query_bias, value_bias,
        output_bias, first_gain, first_shift, inner_weight, inner_bias, outer_weight, outer_bias, final_gain,
        final_shift, cotangent,
    ):
        weights = [query_weight, key_weight, value_weight, output_weight, inner_weight, outer_weight]
        vectors = [query_bias, value_bias, output_bias, first_gain, first_shift]
        vectors += [outer_bias, final_gain, final_shift]
        out, grad, grads, vectors, inner_total = way(
            inputs, seq_lengths, cotangent, weights, vectors, inner_bias
        )
        return (out, grad, *grads[:4], *vectors[:5], grads[4], inner_total, grads[5], *vectors[5:])

    flat, rows = P(AXES), P(AXES, None)
    weights = (*[rows] * 4, *[flat] * 5, rows, flat, rows, *[flat] * 3)
    return jax.shard_map(
        shards,
        mesh=mesh,
        in_specs=(rows, rows, *weights, rows),
        out_specs=(rows, rows, *weights),
        check_vma=False,
    )
```

```python
from functools import partial
import math
import types

import jax
import jax.numpy as jnp
from jax import lax
from jax.experimental import pallas as pl
from jax.experimental.pallas import tpu as pltpu
from jax.sharding import PartitionSpec as P

norm_eps = 1e-05
Q_BIAS, V_BIAS, O_BIAS, GAIN_ONE, SHIFT_ONE, U_BIAS, GAIN_TWO, SHIFT_TWO = range(8)
BLOCK = 256
STARTS, PACKED = (0, 640, 1152), 512
PAIRS = ((0, 256), (256, 384), (384, 512))
LANES = 128
far = -1e30


def nn(left, right):
    return jnp.dot(left, right, preferred_element_type=jnp.float32)


def tn(left, right):
    return lax.dot_general(left, right, (((0,), (0,)), ((), ())), preferred_element_type=jnp.float32)


def nt(left, right):
    return lax.dot_general(left, right, (((1,), (1,)), ((), ())), preferred_element_type=jnp.float32)


def low(values):
    return values.astype(jnp.bfloat16)


def wide(values):
    return values.astype(jnp.float32)


def iota(shape, axis):
    return lax.broadcasted_iota(jnp.int32, shape, axis)


def matrix(ref):
    return ref[...].reshape(-1, ref.shape[-1])


def block_of(i):
    return pl.ds(BLOCK * i if isinstance(i, int) else pl.multiple_of(i * BLOCK, BLOCK), BLOCK)


def lanes_of(first):
    return pl.ds(first if isinstance(first, int) else pl.multiple_of(first, LANES), LANES)


def boundaries(lengths):
    starts, ends, at = [], [], 0
    for s in range(lengths.shape[1]):
        starts.append(at)
        at = at + lengths[0, s]
        ends.append(at)
    before, after = [], []
    for edge in (BLOCK, 2 * BLOCK, 3 * BLOCK):
        tail, head = 0, 0
        for start, end in zip(starts, ends):
            across = (start < edge) & (end > edge)
            tail = tail + jnp.where(across, edge - start, 0)
            head = head + jnp.where(across, end - edge, 0)
        before.append(tail)
        after.append(head)
    return starts, ends, before, after


class Attention:
    def __init__(self, lengths):
        self.starts, self.ends, self.before, self.after = boundaries(lengths)
        self.rows = iota((BLOCK, LANES), 0)
        self.lanes = iota((BLOCK, LANES), 1)
        self.left = self.lanes < 64

    def members(self, block):
        rows, lanes = self.rows + block * BLOCK, lax.rem(self.lanes, 64)
        marks = jnp.zeros((BLOCK, LANES), jnp.float32)
        for s, (start, end) in enumerate(zip(self.starts, self.ends)):
            inside = (rows >= start) & (rows < end) & (lanes == s)
            marks = jnp.where(inside, 1.0, marks)
        return marks

    def merged(self, blocks):
        return [*blocks, *[jnp.where(self.in_head(i), blocks[i + 1], blocks[i]) for i in range(3)]]

    def half(self, side):
        return self.left if side == 0 else ~self.left

    def in_head(self, edge):
        return self.rows < self.after[edge]

    def in_tail(self, edge):
        return self.rows >= BLOCK - self.before[edge]

    def pick(self, parts):
        out = []
        for i in range(4):
            block = parts[i]
            if i < 3:
                block = jnp.where(self.in_tail(i), parts[4 + i], block)
            if i > 0:
                block = jnp.where(self.in_head(i - 1), parts[3 + i], block)
            out.append(block)
        return out

    def gather_sums(self, parts):
        out = []
        for i in range(4):
            block = parts[i]
            if i < 3:
                block = block + jnp.where(self.in_head(i), 0.0, parts[4 + i])
            if i > 0:
                block = block + jnp.where(self.in_head(i - 1), parts[3 + i], 0.0)
            out.append(block)
        return out

    def units(self, blocks):
        out = []
        for i in range(4):
            block = blocks[i]
            if i < 3:
                block = jnp.where(self.in_tail(i), 0.0, block)
            if i > 0:
                block = jnp.where(self.in_head(i - 1), 0.0, block)
            out.append(block)
        for i in range(3):
            tail = jnp.where(self.in_tail(i), blocks[i], 0.0)
            out.append(jnp.where(self.in_head(i), blocks[i + 1], tail))
        return out


def square_of(r, part):
    first = STARTS[part]
    return r.wqkv[:, :, :, :, :, first : first + 512].reshape(512, 512)


def mark(r, at):
    for unit, marks in enumerate(at.merged([at.members(i) for i in range(4)])):
        r.marks[unit] = low(marks)


def project(r, at, part):
    dest = (r.q, r.k, r.v)[part]

    def put(unit, product):
        marks = wide(r.marks[unit])
        beside = (marks, jnp.where(lax.rem(at.lanes, 64) < 8, far - far * marks, 0.0), 1.0)[part]
        for pair in range(4):
            both = product[:, LANES * pair : LANES * (pair + 1)]
            for side in range(2):
                dest[2 * pair + side, unit] = low(jnp.where(at.half(side), both, beside))

    head = [iota((BLOCK, 512), 0) < count for count in at.after]
    for i in range(4):
        product = nn(r.x[block_of(i)], square_of(r, part))
        if part == 0:
            product = (product + r.vec[Q_BIAS : Q_BIAS + 1]) * 0.125
        elif part == 2:
            product = product + r.vec[V_BIAS : V_BIAS + 1]
        put(i, product)
        if i > 0:
            put(3 + i, jnp.where(head[i - 1], product, before))
        before = product


def attend(r, at, pair):
    outs = []
    for side in range(2):
        head = 2 * pair + side
        parts = []
        for unit in range(7):
            scores = nt(r.k[head, unit], r.q[head, unit])
            top = jnp.max(scores, axis=0, keepdims=True)
            grown = low(jnp.exp(scores - top))
            r.e[head, unit] = grown
            parts.append(tn(grown, r.v[head, unit]))
        outs.append(at.pick(parts))
    columns = lanes_of(pair * LANES)
    for i in range(4):
        even, odd = outs[0][i], outs[1][i]
        share = 1.0 / pltpu.roll(jnp.where(at.left, odd, even), 64, 1)
        mixed = jnp.where(at.left, even, odd) * share
        r.combined[BLOCK * i : BLOCK * (i + 1), columns] = low(mixed)
        r.share[BLOCK * i : BLOCK * (i + 1), columns] = share


def normal(values):
    center = values - jnp.mean(values, axis=-1, keepdims=True)
    spread = jnp.mean(center * center, axis=-1, keepdims=True)
    scale = lax.rsqrt(spread + norm_eps)
    return center * scale, scale


def normal_back(grad, normed, scale):
    return scale * (
        grad
        - jnp.mean(grad, axis=-1, keepdims=True)
        - normed * jnp.mean(grad * normed, axis=-1, keepdims=True)
    )


def sums(values):
    return jnp.sum(values, axis=0, keepdims=True)


def attended_rows(r, i):
    rows = block_of(i)
    attended = nn(r.combined[rows], matrix(r.wo)) + r.vec[O_BIAS : O_BIAS + 1]
    normed, scale = normal(wide(r.x[rows]) + attended)
    r.normed[rows] = normed
    r.scale[rows] = jnp.broadcast_to(scale, (BLOCK, LANES))
    r.hidden[rows] = low(normed * r.vec[GAIN_ONE : GAIN_ONE + 1] + r.vec[SHIFT_ONE : SHIFT_ONE + 1])


def active_rows(r, side, i):
    rows = block_of(i)
    hidden_low = r.hidden[rows]
    slope = math.sqrt(2 / math.pi)
    for part in (2 * side, 2 * side + 1):
        columns = slice(512 * part, 512 * (part + 1))
        inner = nn(hidden_low, r.wi[:, :, :, :, :, columns].reshape(512, 512)) + r.ib[:, columns]
        square = inner * inner
        half = 0.5 * jnp.tanh(inner * (slope + (slope * 0.044715) * square)) + 0.5
        active = inner * half
        r.active[rows, columns] = low(active)
        turn = half + active * (1.0 - half) * (2 * slope + (6 * slope * 0.044715) * square)
        r.turn[rows, columns] = low(turn)


def outer_half(r, rows, side):
    columns = slice(256 * side, 256 * (side + 1))
    return nn(r.active[rows], r.wu[:, :, :, :, :, columns].reshape(2048, 256))


def first_half_rows(r, i):
    rows = block_of(i)
    r.grad[rows, 0:256] = outer_half(r, rows, 0)


def final_rows(r, i):
    rows = block_of(i)
    hidden = r.normed[rows] * r.vec[GAIN_ONE : GAIN_ONE + 1] + r.vec[SHIFT_ONE : SHIFT_ONE + 1]
    outer = jnp.concatenate([r.grad[rows, 0:256], outer_half(r, rows, 1)], axis=1) + r.vec[U_BIAS : U_BIAS + 1]
    normed, scale = normal(outer + hidden + wide(r.x[rows]))
    gain = r.vec[GAIN_TWO : GAIN_TWO + 1]
    r.out[rows] = low(normed * gain + r.vec[SHIFT_TWO : SHIFT_TWO + 1])
    grad = wide(r.cot[rows])
    r.gvec[GAIN_TWO : GAIN_TWO + 1] += sums(grad * normed)
    r.gvec[SHIFT_TWO : SHIFT_TWO + 1] += sums(grad)
    grad_two = normal_back(grad * gain, normed, scale)
    r.grad[rows] = grad_two
    grad_outer = low(grad_two)
    r.grad_outer[rows] = grad_outer
    r.gvec[U_BIAS : U_BIAS + 1] += sums(wide(grad_outer))


def rows_of(ref, quarter):
    return ref[quarter // 2, quarter % 2].reshape(-1, ref.shape[-1])


def outer_weight_grad(r, side):
    for quarter in range(4):
        rows, columns = slice(512 * quarter, 512 * (quarter + 1)), slice(256 * side, 256 * (side + 1))
        product = low(tn(r.active[:, rows], r.grad_outer[:, columns]))
        r.gu[quarter // 2, quarter % 2, :, :, :, columns] = product.reshape(4, 2, -1, 256)


def inner_rows(r, i):
    rows = block_of(i)
    grad_outer = r.grad_outer[rows]
    for part in range(4):
        columns = slice(512 * part, 512 * (part + 1))
        grad_inner = low(nt(grad_outer, rows_of(r.wu, part)) * wide(r.turn[rows, columns]))
        r.active[rows, columns] = grad_inner
        r.gib[:, columns] += sums(wide(grad_inner))


def inner_weight_grad(r, side):
    for half in range(2):
        for part in (2 * side, 2 * side + 1):
            columns = slice(512 * part, 512 * (part + 1))
            product = low(tn(r.hidden[:, 256 * half : 256 * (half + 1)], r.active[:, columns]))
            r.gi[half, :, :, :, :, columns] = product.reshape(2, 4, 2, -1, 512)


def hidden_rows(r, i):
    rows = block_of(i)
    grad_two = r.grad[rows]
    grad_hidden = nt(r.active[rows], matrix(r.wi)) + grad_two
    normed = r.normed[rows]
    r.gvec[GAIN_ONE : GAIN_ONE + 1] += sums(grad_hidden * normed)
    r.gvec[SHIFT_ONE : SHIFT_ONE + 1] += sums(grad_hidden)
    gain = r.vec[GAIN_ONE : GAIN_ONE + 1]
    grad_one = normal_back(grad_hidden * gain, normed, r.scale[rows, 0:1])
    r.grad[rows] = grad_two + grad_one
    attended = low(grad_one)
    r.attended[rows] = attended
    r.gvec[O_BIAS : O_BIAS + 1] += sums(wide(attended))
    r.grad_outer[rows] = low(nt(attended, matrix(r.wo)))


def output_weight_grad(r):
    for half in range(2):
        product = low(tn(r.combined[:, 256 * half : 256 * (half + 1)], r.attended[...]))
        r.go[half] = product.reshape(r.go.shape[1:])


def attend_back(r, at, pair):
    columns = lanes_of(pair * LANES)
    ones = low(jnp.where((iota((LANES, LANES), 0) < 64) == (iota((LANES, LANES), 1) < 64), 1.0, 0.0))
    sides = [[], []]
    for i in range(4):
        rows = slice(BLOCK * i, BLOCK * (i + 1))
        grad = wide(r.grad_outer[rows, columns])
        share = r.share[rows, columns]
        product = grad * wide(r.combined[rows, columns])
        high = low(product)
        total = nn(high, ones) + nn(low(product - wide(high)), ones)
        total = pltpu.roll(-(total * share), 64, 1)
        rest = total - wide(low(total))
        lanes = lax.rem(at.lanes, 64)
        beside = jnp.where(lanes == 0, total, jnp.where(lanes == 1, rest, 0.0))
        grad = grad * share
        for side in range(2):
            sides[side].append(jnp.where(at.half(side), grad, beside))
    found = [[], [], []]
    for side in range(2):
        head = 2 * pair + side
        parts = [[], [], []]
        for unit, grad in enumerate(at.units(sides[side])):
            grad = low(grad)
            grown = r.e[head, unit]
            scores = low(wide(grown) * nt(r.v[head, unit], grad))
            parts[0].append(tn(scores, r.k[head, unit]))
            parts[1].append(nn(scores, r.q[head, unit]))
            parts[2].append(nn(grown, grad))
        for which in range(3):
            found[which].append(at.gather_sums(parts[which]))
    for which in range(3):
        total = 0.0
        for i in range(4):
            both = jnp.where(at.left, found[which][0][i], found[which][1][i])
            both = low(both * 0.125 if which == 0 else both)
            (r.dq, r.dk, r.dv)[which][BLOCK * i : BLOCK * (i + 1), columns] = both
            total = total + wide(both)
        if which != 1:
            r.gvec[which // 2 : which // 2 + 1, columns] = sums(total)


def qkv_weight_grad(r, piece):
    first, last = PAIRS[piece]
    for part, grads in enumerate((r.dq, r.dk, r.dv)):
        start = 3 * first + (last - first) * part
        for half in range(2):
            product = low(tn(r.x[:, 256 * half : 256 * (half + 1)], grads[:, first:last]))
            columns = slice(start, start + last - first)
            r.gqkv[half, :, :, :, :, columns] = product.reshape(2, 4, 2, -1, last - first)


def input_rows(r, i):
    rows = block_of(i)
    total = r.grad[rows]
    for part, grads in enumerate((r.dq, r.dk, r.dv)):
        total = total + nt(grads[rows], square_of(r, part))
    r.grad[rows] = total


(
    ZERO, MARK, UNPACK, PROJECT_Q, PROJECT_K, PROJECT_V, ATTEND, ATTENDED, ACTIVE0, ACTIVE1, FINAL0, FINAL, OUTER_GRAD0, OUTER_GRAD1, INNER,
    INNER_GRAD0, INNER_GRAD1, HIDDEN, OUTPUT_GRAD, PACK_EARLY, BACK, QKV_GRAD0, QKV_GRAD1, QKV_GRAD2, PACK_LATE, INPUT,
) = range(26)
LOCAL = [step for step in range(26) if step not in (UNPACK, PACK_EARLY, PACK_LATE)]


def all_rows(rows, r, *given):
    for i in range(4):
        rows(r, *given, i)


def rows_by_two(rows, r):
    def two(i, carried):
        rows(r, 2 * i)
        rows(r, 2 * i + 1)
        return carried

    lax.fori_loop(0, 2, two, 0)


def zero(r):
    r.gvec[...] = jnp.zeros_like(r.gvec)
    r.gib[...] = jnp.zeros_like(r.gib)


def steps_of(r):
    at = Attention(r.lengths)
    steps = {
        ZERO: partial(zero, r),
        MARK: partial(mark, r, at),
        UNPACK: partial(unpack_vectors, r),
        ATTEND: partial(attend, r, at),
        ATTENDED: partial(all_rows, attended_rows, r),
        FINAL0: partial(all_rows, first_half_rows, r),
        FINAL: partial(all_rows, final_rows, r),
        INNER: partial(all_rows, inner_rows, r),
        HIDDEN: partial(rows_by_two, hidden_rows, r),
        OUTPUT_GRAD: partial(output_weight_grad, r),
        PACK_EARLY: partial(pack_sums, r, True),
        BACK: partial(attend_back, r, at),
        PACK_LATE: partial(pack_sums, r, False),
        INPUT: partial(rows_by_two, input_rows, r),
    }
    for i in range(3):
        steps[PROJECT_Q + i] = partial(project, r, at, i)
        steps[QKV_GRAD0 + i] = partial(qkv_weight_grad, r, i)
    for i in range(2):
        steps[ACTIVE0 + i] = partial(all_rows, active_rows, r, i)
        steps[OUTER_GRAD0 + i] = partial(outer_weight_grad, r, i)
        steps[INNER_GRAD0 + i] = partial(inner_weight_grad, r, i)
    return steps


def always():
    return lax.axis_index("dp") >= 0


def take(step):
    pl.when(always())(step)


def over_pairs(step, between):
    def body(pair, carried):
        for n in range(4):
            pl.when(pair == n)(partial(between, n))
        step(pair)
        return carried

    lax.fori_loop(0, 4, body, 0)


def run_local(r):
    steps = steps_of(r)
    for step in LOCAL:
        if step in (ATTEND, BACK):
            over_pairs(steps[step], lambda n: None)
        else:
            take(steps[step])
MESH_ID = pl.DeviceIdType.MESH


def place():
    outer, inner = lax.axis_index("dp"), lax.axis_index("fsdp")
    return outer // 2, outer % 2, inner // 2, inner % 2


def device_at(y, core, z, x):
    return (y * 2 + core, z * 2 + x)


def greet_partners():
    y, core, z, x = place()
    partners = [
        device_at(y, 1 - core, z, x),
        device_at(1 - y, core, z, x),
        device_at(y, core, z, 1 - x),
        device_at(1 - y, core, z, 1 - x),
    ] + [device_at(y, core, (z + step) % 4, x) for step in (1, 2, 3)]
    barrier = pltpu.get_barrier_semaphore()
    for partner in partners:
        pl.semaphore_signal(barrier, inc=1, device_id=partner, device_id_type=MESH_ID)
    return lambda: pl.semaphore_wait(barrier, len(partners))


def remote(source, target, send_sem, recv_sem, to):
    return pltpu.make_async_remote_copy(
        src_ref=source,
        dst_ref=target,
        send_sem=send_sem,
        recv_sem=recv_sem,
        device_id=to,
        device_id_type=MESH_ID,
    )


class Corner:
    def __init__(self):
        y, core, z, x = place()
        self.y, self.core, self.z, self.x = y, core, z, x
        self.ya, self.xa = jnp.where(core == 0, y, 1 - y), jnp.where(core == 0, 1 - x, x)
        self.yb, self.xb = jnp.where(core == 0, 1 - y, y), jnp.where(core == 0, x, 1 - x)
        self.partner_a = device_at(self.ya, core, z, self.xa)
        self.partner_b = device_at(self.yb, core, z, self.xb)
        self.sibling = device_at(y, 1 - core, z, x)
        self.across = device_at(1 - y, core, z, 1 - x)

    def along_z(self, step):
        return device_at(self.y, self.core, (self.z + step) % 4, self.x)


class Gather:
    def __init__(self, corner, own, whole, send_sem, recv_sem):
        self.at, self.own, self.whole = corner, own, whole
        self.send_sem, self.recv_sem = send_sem, recv_sem

    def to_z(self, step):
        at = self.at
        slot = self.whole.at[at.y, at.core, at.z, at.x]
        return remote(
            self.own, slot, self.send_sem.at[step - 1], self.recv_sem.at[step - 1], at.along_z(step)
        )

    def line(self, y, x, number, to):
        line = self.whole.at[y, self.at.core, :, x]
        return remote(line, line, self.send_sem.at[number], self.recv_sem.at[number], to)

    def to_a(self):
        return self.line(self.at.y, self.at.x, 3, self.at.partner_a)

    def to_b(self, part):
        at = self.at
        y, x = ((at.y, at.x), (at.ya, at.xa))[part]
        return self.line(y, x, 4 + part, at.partner_b)

    def to_sibling(self, part):
        at = self.at
        y, x = ((at.y, at.x), (at.ya, at.xa), (at.yb, at.xb), (1 - at.y, 1 - at.x))[part]
        return self.line(y, x, 6 + part, at.sibling)

    def phase(self, number):
        if number == 0:
            for step in (2, 1, 3):
                self.to_z(step).start()
            at = self.at
            self.whole[at.y, at.core, at.z, at.x] = self.own[...]
        elif number == 1:
            for step in (1, 2, 3):
                self.to_z(step).wait_recv()
            self.to_a().start()
            self.to_b(0).start()
            self.to_sibling(0).start()
        elif number == 2:
            self.to_a().wait_recv()
            self.to_b(1).start()
            self.to_sibling(1).start()
        elif number == 3:
            self.to_b(0).wait_recv()
            self.to_sibling(2).start()
            self.to_b(1).wait_recv()
            self.to_sibling(3).start()
        elif number == 4:
            for part in range(4):
                self.to_sibling(part).wait_recv()

    def finish(self):
        for step in (1, 2, 3):
            self.to_z(step).wait_send()
        self.to_a().wait_send()
        for part in range(2):
            self.to_b(part).wait_send()
        for part in range(4):
            self.to_sibling(part).wait_send()


class GatherPlaneFirst(Gather):
    def slot(self, y, x, number, to):
        slot = self.whole.at[y, self.at.core, self.at.z, x]
        return remote(slot, slot, self.send_sem.at[number], self.recv_sem.at[number], to)

    def to_a(self):
        return self.slot(self.at.y, self.at.x, 3, self.at.partner_a)

    def to_b(self, part):
        at = self.at
        y, x = ((at.y, at.x), (at.ya, at.xa))[part]
        return self.slot(y, x, 4 + part, at.partner_b)

    def plane(self, z, number, to):
        plane = self.whole.at[:, self.at.core, z]
        return remote(plane, plane, self.send_sem.at[number], self.recv_sem.at[number], to)

    def to_z(self, step):
        return self.plane(self.at.z, step - 1, self.at.along_z(step))

    def to_sibling(self, part):
        return self.plane((self.at.z + part) % 4, 6 + part, self.at.sibling)

    def phase(self, number):
        at = self.at
        if number == 0:
            self.whole[at.y, at.core, at.z, at.x] = self.own[...]
            self.to_a().start()
            self.to_b(0).start()
        elif number == 1:
            self.to_a().wait_recv()
            self.to_b(1).start()
        elif number == 2:
            self.to_b(0).wait_recv()
            self.to_b(1).wait_recv()
            for step in (2, 1, 3):
                self.to_z(step).start()
            self.to_sibling(0).start()
        elif number == 3:
            for step in (1, 3, 2):
                self.to_z(step).wait_recv()
                self.to_sibling(4 - step).start()
        elif number == 4:
            for part in range(4):
                self.to_sibling(part).wait_recv()


class Scatter:
    def __init__(self, corner, whole, out, got_core, got_b, got_a, got_z, send_sem, recv_sem):
        self.at, self.whole, self.out = corner, whole, out
        self.got_core, self.got_b, self.got_a, self.got_z = got_core, got_b, got_a, got_z
        self.send_sem, self.recv_sem = send_sem, recv_sem

    def sems(self, number):
        return self.send_sem.at[number], self.recv_sem.at[number]

    def to_sibling(self):
        return remote(
            self.whole.at[:, 1 - self.at.core], self.got_core, *self.sems(0), self.at.sibling
        )

    def to_b(self, part):
        at = self.at
        y, x = ((at.yb, at.xb), (1 - at.y, 1 - at.x))[part]
        return remote(
            self.whole.at[y, at.core, :, x], self.got_b.at[part], *self.sems(1 + part), at.partner_b
        )

    def to_a(self):
        at = self.at
        return remote(
            self.whole.at[at.ya, at.core, :, at.xa], self.got_a, *self.sems(3), at.partner_a
        )

    def to_z(self, step):
        at = self.at
        return remote(
            self.whole.at[at.y, at.core, (at.z + step) % 4, at.x],
            self.got_z.at[step - 1],
            *self.sems(3 + step),
            at.along_z(step),
        )

    def add_line(self, y, x, other):
        core = self.at.core
        for z in range(4):
            total = self.whole[y, core, z, x].astype(jnp.float32) + other(z).astype(jnp.float32)
            self.whole[y, core, z, x] = total.astype(self.whole.dtype)

    def add_core(self, y, x):
        self.add_line(y, x, lambda z: self.got_core[y, z, x])

    def phase(self, number):
        at = self.at
        if number == 0:
            self.to_sibling().start()
        elif number == 1:
            self.to_sibling().wait_recv()
            self.add_core(at.yb, at.xb)
            self.to_b(0).start()
            self.add_core(1 - at.y, 1 - at.x)
            self.to_b(1).start()
            self.add_core(at.ya, at.xa)
            self.add_core(at.y, at.x)
        elif number == 2:
            self.to_b(1).wait_recv()
            self.add_line(at.ya, at.xa, lambda z: self.got_b[1, z])
            self.to_a().start()
            self.to_b(0).wait_recv()
            self.add_line(at.y, at.x, lambda z: self.got_b[0, z])
        elif number == 3:
            self.to_a().wait_recv()
            self.add_line(at.y, at.x, lambda z: self.got_a[z])
            for step in (2, 1, 3):
                self.to_z(step).start()
        elif number == 4:
            total = self.whole[at.y, at.core, at.z, at.x].astype(jnp.float32)
            for step in (1, 2, 3):
                self.to_z(step).wait_recv()
                total = total + self.got_z[step - 1].astype(jnp.float32)
            self.out[...] = total

    def finish(self):
        self.to_sibling().wait_send()
        for part in range(2):
            self.to_b(part).wait_send()
        self.to_a().wait_send()
        for step in (1, 2, 3):
            self.to_z(step).wait_send()


class ScatterDirect(Scatter):
    def phase(self, number):
        at = self.at
        if number == 1:
            self.to_sibling().wait_recv()
            self.add_core(1 - at.y, 1 - at.x)
            self.to_b(1).start()
            self.add_core(at.yb, at.xb)
            self.to_b(0).start()
            self.add_core(at.ya, at.xa)
            self.to_a().start()
            self.add_core(at.y, at.x)
        elif number == 2:
            self.to_a().wait_recv()
            for part in range(2):
                self.to_b(part).wait_recv()
            for z in range(4):
                line = self.whole[at.y, at.core, z, at.x].astype(jnp.float32)
                for got in (self.got_a[z], self.got_b[0, z], self.got_b[1, z]):
                    line = line + got.astype(jnp.float32)
                self.whole[at.y, at.core, z, at.x] = line.astype(self.whole.dtype)
            for step in (2, 1, 3):
                self.to_z(step).start()
        elif number != 3:
            super().phase(number)

    def to_b(self, part):
        at = self.at
        y, x, to = ((at.yb, at.xb, at.partner_b), (1 - at.y, 1 - at.x, at.across))[part]
        return remote(self.whole.at[y, at.core, :, x], self.got_b.at[part], *self.sems(1 + part), to)


class ScatterPlaneLast(Scatter):
    def to_z(self, step):
        at = self.at
        return remote(
            self.whole.at[:, at.core, (at.z + step) % 4],
            self.got_z.at[step - 1],
            *self.sems(3 + step),
            at.along_z(step),
        )

    def to_b(self, part):
        at = self.at
        y, x = ((at.yb, at.xb), (1 - at.y, 1 - at.x))[part]
        source = self.whole.at[y, at.core, at.z, x]
        return remote(source, self.got_b.at[part], *self.sems(1 + part), at.partner_b)

    def to_a(self):
        at = self.at
        source = self.whole.at[at.ya, at.core, at.z, at.xa]
        return remote(source, self.got_a, *self.sems(3), at.partner_a)

    def add(self, y, z, x, *others):
        core = self.at.core
        total = self.whole[y, core, z, x].astype(jnp.float32)
        for other in others:
            total = total + other.astype(jnp.float32)
        self.whole[y, core, z, x] = total.astype(self.whole.dtype)

    def phase(self, number):
        at = self.at
        places = [(y, x) for y in range(2) for x in range(2)]
        if number == 0:
            self.to_sibling().start()
        elif number == 1:
            self.to_sibling().wait_recv()
            for step in (2, 1, 3, 0):
                z = (at.z + step) % 4
                for y, x in places:
                    self.add(y, z, x, self.got_core[y, z, x])
                if step:
                    self.to_z(step).start()
        elif number == 2:
            for step in (1, 2, 3):
                self.to_z(step).wait_recv()
            for y, x in places:
                self.add(y, at.z, x, *[self.got_z[step, y, x] for step in range(3)])
            for part in range(2):
                self.to_b(part).start()
        elif number == 3:
            self.to_b(1).wait_recv()
            self.add(at.ya, at.z, at.xa, self.got_b[1])
            self.to_a().start()
            self.to_b(0).wait_recv()
        elif number == 4:
            self.to_a().wait_recv()
            total = self.whole[at.y, at.core, at.z, at.x].astype(jnp.float32)
            self.out[...] = total + self.got_b[0].astype(jnp.float32) + self.got_a[...].astype(jnp.float32)
LEAD = (2, 2, 4, 2)
TOKENS, WIDTH = 1024, 512
BF, F32 = jnp.bfloat16, jnp.float32
AXES = ("dp", "fsdp")
SHARDS = dict(wqkv=(16, 1664), wo=(16, 512), wi=(16, 2048), wu=(64, 512))


def local_scratch():
    units, tokens = (8, 7, BLOCK, LANES), (TOKENS, WIDTH)
    return dict(
        q=(units, BF),
        k=(units, BF),
        v=(units, BF),
        e=((8, 7, BLOCK, BLOCK), BF),
        marks=((7, BLOCK, LANES), BF),
        share=(tokens, F32),
        combined=(tokens, BF),
        normed=(tokens, F32),
        scale=((TOKENS, LANES), F32),
        hidden=(tokens, BF),
        active=((TOKENS, 2048), BF),
        turn=((TOKENS, 2048), BF),
        grad_outer=(tokens, BF),
        attended=(tokens, BF),
    )


def call(kernel, inputs, spaces, outputs, scratch, sems, **params):
    names = [*inputs, *outputs, *scratch, *sems]

    def body(*refs):
        kernel(types.SimpleNamespace(**dict(zip(names, refs, strict=True))))

    made = pl.pallas_call(
        body,
        out_shape=[jax.ShapeDtypeStruct(*given) for given in outputs.values()],
        in_specs=[pl.BlockSpec(memory_space=spaces.get(name, pltpu.VMEM)) for name in inputs],
        out_specs=[pl.BlockSpec(memory_space=spaces.get(name, pltpu.VMEM)) for name in outputs],
        scratch_shapes=[pltpu.VMEM(*given) for given in scratch.values()]
        + [pltpu.SemaphoreType.DMA(shape) for shape in sems.values()],
        compiler_params=pltpu.CompilerParams(vmem_limit_bytes=63 << 20, **params),
    )(*inputs.values())
    return types.SimpleNamespace(**dict(zip(outputs, made, strict=True)))


def chosen_lanes(count):
    shape = (LANES, 32 * count)
    return low(jnp.where(iota(shape, 0) == lax.rem(iota(shape, 1), count), 1.0, 0.0))


def of_owner(rows, count):
    shape = (rows, 32 * count)
    return lax.rem(iota(shape, 0), 32) == lax.div(iota(shape, 1), count)


def chosen_rows():
    row, column = iota((288, 512), 0), iota((288, 512), 1)
    return low(jnp.where(column == lax.rem(row, 32) * 16 + lax.div(row, 32), 1.0, 0.0))


def unpack_vectors(r):
    packed = r.wqkv[:, :, :, :, :, PACKED : PACKED + LANES].reshape(512, LANES)
    packed = low(nn(chosen_rows(), packed))
    vectors = jnp.where(of_owner(256, 16), nn(packed[:256], chosen_lanes(16)), 0.0)
    for kind in range(8):
        r.vec[kind : kind + 1] = sums(vectors[32 * kind : 32 * (kind + 1)])
    r.ib[...] = sums(jnp.where(of_owner(32, 64), nn(packed[256:], chosen_lanes(64)), 0.0))


def pack_sums(r, early):
    def placed(values, count):
        alone = jnp.where(of_owner(32, count), values, 0.0)
        high = low(alone)
        lanes = chosen_lanes(count)
        return nt(high, lanes) + nt(low(alone - wide(high)), lanes)

    rows = [placed(r.gvec[kind : kind + 1], 16) for kind in (range(2, 8) if early else range(2))]
    rows += [placed(r.gib[...], 64)] if early else []
    chosen = chosen_rows()[64:] if early else chosen_rows()[:64]
    packed = low(tn(chosen, low(jnp.concatenate(rows, axis=0)))).reshape(*LEAD, 16, LANES)
    if not early:
        packed = packed + r.gqkv[:, :, :, :, :, 1536:1664]
    r.gqkv[:, :, :, :, :, 1536:1664] = packed


Q, K, V, O, I0, I1, U0, U1 = range(8)
SU0, SU1, SI0, SI1, SO, SA, SB, SC = range(8, 16)
X_HERE, COT_HERE, OUT_AWAY, GRAD_AWAY0, GRAD_AWAY1 = range(100, 105)
PLAN = [
    (Q, 0), (U1, 0), (K, 0), (V, 0), ZERO, MARK, X_HERE, (U1, 1), (O, 0), (I1, 0), (Q, 1), (K, 1), (V, 1), (I0, 0),
    (U0, 0), (Q, 2), (K, 2), (O, 1), (V, 2), (Q, 3), (I1, 1), (Q, 4), (K, 3), UNPACK, (U1, 2), (V, 3), (I0, 1),
    (K, 4), PROJECT_Q, (O, 2), (U0, 1), (V, 4), PROJECT_K, PROJECT_V,
    [ATTEND, [], [(I0, 2)], [(O, 3), (I1, 2)], [(U0, 2), (O, 4)]], (I0, 3), ATTENDED, (I1, 3), (I0, 4), ACTIVE0,
    (I1, 4), (U0, 3), (U1, 3), ACTIVE1, (U0, 4), FINAL0, (U1, 4), COT_HERE, FINAL, OUT_AWAY, OUTER_GRAD0, (SU0, 0),
    OUTER_GRAD1, INNER, (SU0, 1), INNER_GRAD0, INNER_GRAD1, (SI0, 0), HIDDEN, (SU1, 0), (SI0, 1), OUTPUT_GRAD,
    PACK_EARLY, (SO, 0), (SU0, 2), (SI1, 0), (SU1, 1),
    [BACK, [], [(SO, 1), (SI1, 1)], [QKV_GRAD0, (SO, 2), (SI0, 2)], [(SI1, 2), (SA, 0), QKV_GRAD1, (SB, 0), (SO, 3), (SI0, 3), (SA, 1), (SU0, 3), (SB, 1)]],
    QKV_GRAD2, PACK_LATE, (SA, 2), (SC, 0), (SB, 2), (SO, 4), (SI1, 3), (SC, 1), (SB, 3), (SI0, 4), (SU1, 2), (SA, 3),
    INPUT, GRAD_AWAY0, GRAD_AWAY1, (SC, 2), (SC, 3), (SB, 4), (SU1, 3), (SI1, 4), (SU1, 4), (SA, 4), (SU0, 4),
    (SC, 4),
]


def halves_of(buffer):
    first, second = [buffer.at[i : i + 512].reshape(*LEAD, 16, 2048) for i in (0, 512)]
    return first, second.at[:, :, :, :, :, 0:1664]


def direct_kernel(r):
    r.gi, r.gqkv = halves_of(r.turn)
    r.dq = r.wu.at[0].reshape(TOKENS, 512)
    r.dk = r.wu.at[1].reshape(TOKENS, 512)
    r.dv = r.attended
    r.cot = r.attended
    spare = [
        r.active.at[first : first + 16 * math.prod(lead)].reshape(*lead, 16, 2048)
        for lead, first in (((2, 4, 2), 0), ((2, 4), 256), ((4,), 384), ((3,), 448))
    ]
    local = [
        pltpu.make_async_copy(source, target, r.local.at[i])
        for i, (source, target) in enumerate(
            [(r.x_far, r.x), (r.cot_far, r.cot), (r.out, r.out_far)]
            + [(r.grad.at[BLOCK * i : BLOCK * (i + 1)], r.grad_far.at[BLOCK * i : BLOCK * (i + 1)]) for i in range(4)]
        )
    ]
    own = [
        pltpu.make_async_copy(source, target, r.local.at[7 + i])
        for i, (source, target) in enumerate(
            (
                (r.query_far, r.own_qkv.at[:, 0:512]),
                (r.key_far, r.own_qkv.at[:, 640:1152]),
                (r.value_far, r.own_qkv.at[:, 1152:1664]),
                (r.output_far, r.own_output),
                (r.inner_far, r.own_inner),
                (r.outer_far, r.own_outer),
            )
        )
    ]
    corner = Corner()
    met = greet_partners()
    for copy in (*own, *local[:2]):
        copy.start()
    r.own_small[...] = jnp.zeros_like(r.own_small)
    vectors = [r.own0, r.own1, r.own2, r.own3, r.own4, r.own5, r.own6, r.own7, r.own8]
    for i, vector in enumerate(vectors):
        r.own_small[i : i + 1, 0 : vector.shape[0]] = wide(vector[...]).reshape(1, vector.shape[0])
    r.own_qkv[:, 512:640] = low(r.own_small[...])
    for copy in own:
        copy.wait()
    met()

    def column_part(ref, first, last):
        return ref.at[(slice(None),) * (len(ref.shape) - 1) + (slice(first, last),)]

    pieces = [(column_part, r.own_qkv, r.wqkv, *ends) for ends in ((0, 640), (640, 1152), (1152, 1664))]
    pieces += [(column_part, r.own_output, r.wo, 0, 512)]
    pieces += [(column_part, r.own_inner, r.wi, *ends) for ends in ((0, 1024), (1024, 2048))]
    pieces += [(column_part, r.own_outer, r.wu, *ends) for ends in ((0, 256), (256, 512))]
    gathers = [
        (GatherPlaneFirst if i == U1 else Gather)(corner, cut(own, *ends), cut(whole, *ends), r.gather_send.at[i], r.gather_recv.at[i])
        for i, (cut, own, whole, *ends) in enumerate(pieces)
    ]

    got0 = (r.got0_core, r.got0_b, r.got0_a, r.got0_z)
    got1 = (r.got1_core, r.got1_b, r.got1_a, r.got1_z)
    got2 = (r.got2_core, r.got2_b, r.got2_a, r.got2_z)
    far = (r.far_core, r.far_b, r.far_a, r.far_z)
    pieces = [(column_part, r.gu, r.out_outer, got0, 0, 256), (column_part, r.gu, r.out_outer, far, 256, 512)]
    pieces += [(column_part, r.gi, r.out_inner, got1, *ends) for ends in ((0, 1024), (1024, 2048))]
    pieces += [(column_part, r.go, r.out_output, got2, 0, 512)]
    pieces += [(column_part, r.gqkv, r.out_qkv, spare, *ends) for ends in ((0, 768), (768, 1152), (1152, 1664))]
    kinds = [Scatter, ScatterPlaneLast, *[Scatter] * 5, ScatterDirect]
    scatters = [
        kinds[i](
            corner, cut(whole, *ends), cut(out, *ends), *(got if i < 2 else [cut(ref, *ends) for ref in got]),
            r.scatter_send.at[i], r.scatter_recv.at[i],
        )
        for i, (cut, whole, out, got, *ends) in enumerate(pieces)
    ]
    pieces = gathers + scatters

    def out_away():
        local[2].start()

    def grad_away(side):
        for copy in local[3 + 2 * side : 5 + 2 * side]:
            copy.start()

    def cot_here():
        for piece in gathers:
            piece.finish()
        local[1].wait()

    steps = steps_of(r) | {
        X_HERE: local[0].wait,
        COT_HERE: cot_here,
        OUT_AWAY: out_away,
        GRAD_AWAY0: partial(grad_away, 0),
        GRAD_AWAY1: partial(grad_away, 1),
    }
    def go_all(items):
        for item in items:
            go(item)

    def go(item):
        if isinstance(item, tuple):
            pieces[item[0]].phase(item[1])
        elif isinstance(item, list):
            over_pairs(steps[item[0]], lambda n: go_all(item[1 + n]))
        elif item < X_HERE:
            take(steps[item])
        else:
            steps[item]()

    go_all(PLAN)
    for piece in scatters:
        piece.finish()
    for copy in local[2:]:
        copy.wait()


def received(shard):
    return [(lead + tuple(shard[0]), shard[1]) for lead in ((2, 4, 2), (2, 4), (4,), (3,))]


def direct(inputs, lengths, cotangent, weights, vectors, inner_bias):
    tokens = (TOKENS, WIDTH)
    given = dict(x_far=inputs, cot_far=cotangent, lengths=lengths)
    given |= dict(query_far=weights[0], key_far=weights[1], value_far=weights[2])
    given |= dict(output_far=weights[3], inner_far=weights[4], outer_far=weights[5])
    given |= {"own%d" % i: vector for i, vector in enumerate([*vectors, inner_bias])}
    outputs = dict(
        out_far=(tokens, BF),
        grad_far=(tokens, F32),
        out_qkv=(SHARDS["wqkv"], F32),
        out_output=(SHARDS["wo"], F32),
        out_inner=(SHARDS["wi"], F32),
        out_outer=(SHARDS["wu"], F32),
    )
    whole = {name: (LEAD + shard, BF) for name, shard in SHARDS.items()}
    got0, got1, got2 = [received((shard, BF)) for shard in ((64, 256), (16, 2048), (16, 512))]
    scratch = local_scratch() | whole
    scratch |= dict(
        x=(tokens, BF),
        out=(tokens, BF),
        grad=(tokens, F32),
        gu=whole["wu"],
        go=whole["wo"],
        own_qkv=(SHARDS["wqkv"], BF),
        own_output=(SHARDS["wo"], BF),
        own_inner=(SHARDS["wi"], BF),
        own_outer=(SHARDS["wu"], BF),
        own_small=((16, LANES), F32),
        vec=((8, WIDTH), F32),
        ib=((1, 2048), F32),
        gvec=((8, WIDTH), F32),
        gib=((1, 2048), F32),
        far_core=got0[0],
        far_b=((2, 64, 256), BF),
        far_a=((64, 256), BF),
        far_z=((3, 2, 2, 64, 256), BF),
        got0_core=got0[0], got0_b=got0[1], got0_a=got0[2], got0_z=got0[3],
        got1_core=got1[0], got1_b=got1[1], got1_a=got1[2], got1_z=got1[3],
        got2_core=got2[0], got2_b=got2[1], got2_a=got2[2], got2_z=got2[3],
    )
    sems = dict(gather_send=(8, 10), gather_recv=(8, 10), scatter_send=(8, 7), scatter_recv=(8, 7), local=(13,))
    spaces = {name: pl.ANY for name in (*given, *outputs) if name.endswith("_far")} | dict(lengths=pltpu.SMEM)
    made = call(
        direct_kernel, given, spaces, outputs, scratch, sems, collective_id=0, has_side_effects=True
    )
    return hand_over(made)


def hand_over(made):
    count = 4
    rows = TOKENS // count

    def body(out, grad, qkv, output, inner, outer, *refs):
        to_out, to_grad, to_q, to_k, to_v, to_output, to_inner, to_outer = refs[:8]
        vectors, (held_out, held_grad, held_qkv, sem) = refs[8:17], refs[17:]
        copies = []

        def copy(source, target):
            copies.append(pltpu.make_async_copy(source, target, sem.at[len(copies)]))
            copies[-1].start()
            return copies[-1]

        small = copy(qkv, held_qkv)
        near_ones = [copy(output, to_output), copy(inner, to_inner), copy(outer, to_outer)]
        parts = []
        for i in range(count):
            part = pl.ds(rows * i, rows)
            for source, held, target in ((grad, held_grad, to_grad), (out, held_out, to_out)):
                parts.append((copy(source.at[part], held.at[part]), held.at[part], target.at[part]))
        small.wait()
        for i, target in enumerate((to_q, to_k, to_v)):
            for first, last in PAIRS:
                start = 3 * first + (last - first) * i
                target[:, first:last] = held_qkv[:, start : start + last - first]
        for i, target in enumerate(vectors):
            target[...] = held_qkv[i, 1536 : 1536 + target.shape[0]]
        back = near_ones
        for into, held, target in parts:
            into.wait()
            back.append(copy(held, target))
        for each in back:
            each.wait()

    given = [made.out_far, made.grad_far, made.out_qkv, made.out_output, made.out_inner, made.out_outer]
    square = jax.ShapeDtypeStruct((16, 512), F32)
    shapes = [jax.ShapeDtypeStruct(part.shape, part.dtype) for part in given]
    vectors = [jax.ShapeDtypeStruct((16,), F32)] * 8 + [jax.ShapeDtypeStruct((64,), F32)]
    far, near = pl.BlockSpec(memory_space=pl.ANY), pl.BlockSpec(memory_space=pltpu.VMEM)
    out, grad, q, k, v, output, inner, outer, *vectors = pl.pallas_call(
        body,
        out_shape=[*shapes[:2], square, square, square, *shapes[3:], *vectors],
        in_specs=[far] * 6,
        out_specs=[far, far, *[near] * 15],
        scratch_shapes=[
            pltpu.VMEM((TOKENS, WIDTH), BF),
            pltpu.VMEM((TOKENS, WIDTH), F32),
            pltpu.VMEM(SHARDS["wqkv"], F32),
            pltpu.SemaphoreType.DMA((4 + 4 * count,)),
        ],
    )(*given)
    return out, grad, [q, k, v, output, inner, outer], vectors[:8], vectors[8]


def alone_kernel(r):
    r.gi, r.gqkv = halves_of(r.turn)
    r.cot, r.dv, r.dk = r.attended, r.attended, r.hidden
    here = pltpu.make_async_copy(r.cot_far, r.cot, r.local.at[0])
    here.start()
    here.wait()
    run_local(r)
    away = [
        pltpu.make_async_copy(source, target, r.local.at[1 + i])
        for i, (source, target) in enumerate(((r.gi, r.gi_far), (r.gqkv, r.gqkv_far)))
    ]
    for copy in away:
        copy.start()
    for copy in away:
        copy.wait()


def through_collectives(inputs, lengths, cotangent, weights, vectors, inner_bias):
    weights, vectors, inner_bias = jax.tree.map(
        lambda own: lax.all_gather(own, AXES, axis=0, tiled=True), (weights, vectors, inner_bias)
    )
    empty = jnp.zeros((WIDTH, LANES), BF)
    weights = [jnp.concatenate([weights[0], empty, *weights[1:3]], axis=1), *weights[3:]]
    whole = {name: weight.reshape(LEAD + SHARDS[name]) for name, weight in zip(SHARDS, weights)}
    given = dict(x=inputs, cot_far=cotangent, lengths=lengths, **whole)
    given |= dict(vec=jnp.stack(vectors).astype(F32), ib=inner_bias.astype(F32)[None])
    tokens = (TOKENS, WIDTH)
    outputs = dict(out=(tokens, BF), grad=(tokens, F32), gvec=((8, WIDTH), F32), gib=((1, 2048), F32))
    outputs |= dict(gqkv_far=(LEAD + SHARDS["wqkv"], BF), gi_far=(LEAD + SHARDS["wi"], BF))
    outputs |= dict(go=(LEAD + SHARDS["wo"], BF), gu=(LEAD + SHARDS["wu"], BF))
    spaces = dict(lengths=pltpu.SMEM, cot_far=pl.ANY, gqkv_far=pl.ANY, gi_far=pl.ANY)
    scratch = local_scratch() | dict(dq=(tokens, BF))
    made = call(alone_kernel, given, spaces, outputs, scratch, dict(local=(3,)))
    qkv, output, inner, outer = [
        part.reshape(-1, part.shape[-1]).astype(F32) for part in (made.gqkv_far, made.go, made.gi_far, made.gu)
    ]
    grads = []
    for i in range(3):
        starts = [(3 * first + (last - first) * i, last - first) for first, last in PAIRS]
        grads.append(jnp.concatenate([qkv[:, start : start + count] for start, count in starts], axis=1))
    grads += [output, inner, outer]
    grads, vectors, inner_bias = jax.tree.map(
        lambda part: lax.psum_scatter(part, AXES, scatter_dimension=0, tiled=True),
        (grads, [made.gvec[i] for i in range(8)], made.gib[0]),
    )
    return made.out, made.grad, grads, vectors, inner_bias


def solution(mesh):
    on_chips = (mesh.shape["dp"], mesh.shape["fsdp"]) == (4, 8)
    way = direct if on_chips else through_collectives

    def shards(
        inputs, seq_lengths, query_weight, key_weight, value_weight, output_weight, query_bias, value_bias,
        output_bias, first_gain, first_shift, inner_weight, inner_bias, outer_weight, outer_bias, final_gain,
        final_shift, cotangent,
    ):
        weights = [query_weight, key_weight, value_weight, output_weight, inner_weight, outer_weight]
        vectors = [query_bias, value_bias, output_bias, first_gain, first_shift]
        vectors += [outer_bias, final_gain, final_shift]
        out, grad, grads, vectors, inner_total = way(
            inputs, seq_lengths, cotangent, weights, vectors, inner_bias
        )
        return (out, grad, *grads[:4], *vectors[:5], grads[4], inner_total, grads[5], *vectors[5:])

    flat, rows = P(AXES), P(AXES, None)
    weights = (*[rows] * 4, *[flat] * 5, rows, flat, rows, *[flat] * 3)
    return jax.shard_map(
        shards,
        mesh=mesh,
        in_specs=(rows, rows, *weights, rows),
        out_specs=(rows, rows, *weights),
        check_vma=False,
    )
```
